32 devices in a mesh: dp: 8 (over y, x, core), fsdp: 4 (over z).
Axes of the slice: x: 2, y: 2, z: 4, core: 2. Of those that a mesh axis runs over, the one named last changes fastest.
Arguments:
- tokens: bfloat16 [16384, 1024], P(('dp', 'fsdp')), may hold values from -6 to 6
- cotangent: bfloat16 [16384, 1024], P(('dp', 'fsdp')), may hold values from -6 to 6
- cont_lengths: int32 [8, 8], P('dp'), may hold values from 1 to 256, 1024 in all within a row
- ln1_gain: bfloat16 [1, 1024], P(None, 'fsdp'), may hold values from 0.099609375 to 1.8984375
- ln1_bias: bfloat16 [1, 1024], P(None, 'fsdp'), may hold values from -3 to 3
- w_qkv: bfloat16 [1, 1024, 3072], P(None, 'fsdp'), may hold values from -0.1875 to 0.1875
- q_bias: bfloat16 [1, 1024], P(None, 'fsdp'), may hold values from -3 to 3
- v_bias: bfloat16 [1, 1024], P(None, 'fsdp'), may hold values from -3 to 3
- w_out: bfloat16 [1, 1024, 1024], P(None, 'fsdp'), may hold values from -1 to 1
- out_bias: bfloat16 [1, 1024], P(None, 'fsdp'), may hold values from -2 to 2
- ln2_gain: bfloat16 [1, 1024], P(None, 'fsdp'), may hold values from 0.099609375 to 1.8984375
- ln2_bias: bfloat16 [1, 1024], P(None, 'fsdp'), may hold values from -3 to 3
- w_up: bfloat16 [1, 1024, 4096], P(None, 'fsdp'), may hold values from -0.1875 to 0.1875
- up_bias: bfloat16 [1, 4096], P(None, 'fsdp'), may hold values from -3 to 3
- w_down: bfloat16 [1, 4096, 1024], P(None, 'fsdp'), may hold values from -0.125 to 0.125
- down_bias: bfloat16 [1, 1024], P(None, 'fsdp'), may hold values from -2 to 2
Outputs:
- output: bfloat16 [16384, 1024], P(('dp', 'fsdp'))
- input_grad: bfloat16 [16384, 1024], P(('dp', 'fsdp'))
- grad_ln1_gain: float32 [1, 1024], P(None, 'fsdp')
- grad_ln1_bias: float32 [1, 1024], P(None, 'fsdp')
- grad_w_qkv: float32 [1, 1024, 3072], P(None, 'fsdp')
- grad_q_bias: float32 [1, 1024], P(None, 'fsdp')
- grad_v_bias: float32 [1, 1024], P(None, 'fsdp')
- grad_w_out: float32 [1, 1024, 1024], P(None, 'fsdp')
- grad_out_bias: float32 [1, 1024], P(None, 'fsdp')
- grad_ln2_gain: float32 [1, 1024], P(None, 'fsdp')
- grad_ln2_bias: float32 [1, 1024], P(None, 'fsdp')
- grad_w_up: float32 [1, 1024, 4096], P(None, 'fsdp')
- grad_up_bias: float32 [1, 4096], P(None, 'fsdp')
- grad_w_down: float32 [1, 4096, 1024], P(None, 'fsdp')
- grad_down_bias: float32 [1, 1024], P(None, 'fsdp')
The draws below stay inside these ranges and needn't reach their ends.
Inputs may be any that keep to these rules, and one draw needn't show every extreme that they name: `cont_lengths`: each group's 8 continuation lengths sum to 1024, and in every group the longest equals 256.
All inputs are finite; a program needn't handle non-finite values.
Results may differ from the reference program's by a relative error of at most 0.025.
Values may be sent and summed in bfloat16 or wider, within the bound.
No kernel may reach another device: no remote copies, remote signals or barrier semaphores. Data moves between devices by JAX's collectives and lax.ppermute only.
A program may use at most 192 MiB of HBM per device.

```python
import math
import jax
import jax.numpy as jnp
import numpy as np
from jax import lax

D = 1024
H = 16
HD = 64
FF = 4096
LAYERS = 1
NCONT = 8
GROUP = 2048
GROUPS = 8
TOKENS = 16384


def level_of(key, shape, cuts, least, largest):
    loudness = 1.0
    for dim, parts in cuts:
        heights = jax.random.uniform(jax.random.fold_in(jax.random.fold_in(key, 6), dim), (parts,), jnp.float32, least / len(cuts), largest / len(cuts))
        loudness = loudness * jnp.repeat(jnp.exp(heights), shape[dim] // parts).reshape((-1,) + (1,) * (len(shape) - 1 - dim))
    return loudness


def profile(number_of, total, limit, lean):
    weights = [(1 << 20) // math.isqrt(grade ** lean) + 1 for grade in range(2, number_of + 1)]
    rest, counts = total - limit - (number_of - 1), [1] * (number_of - 1)
    while rest > 0:
        free = [i for i in range(number_of - 1) if counts[i] < limit]
        pool, remaining = sum([weights[i] for i in free]), rest
        for i in free:
            addition = min(limit - counts[i], max(1, remaining * weights[i] // pool), rest)
            counts[i] = counts[i] + addition
            rest = rest - addition
    return np.array([limit] + counts)


def uneven(key, amount, total, most, skew):
    if amount == 2:
        one = jax.random.randint(key, (), max(1, total - most), min(most, total - 1) + 1)
        return jnp.stack([one, total - one])
    sizes = jnp.asarray(profile(amount, total, most, skew), jnp.int32)
    couples = (amount - 1) // 2
    donor, sink = sizes[1:1 + 2 * couples:2], sizes[2:2 + 2 * couples:2]
    room = jnp.minimum(donor - 1, most - sink)
    passed = jax.random.randint(jax.random.fold_in(key, 1), (couples,), 0, 1 << 20) % (room + 1)
    sizes = sizes.at[1:1 + 2 * couples:2].set(donor - passed).at[2:2 + 2 * couples:2].set(sink + passed)
    return sizes[jax.random.permutation(jax.random.fold_in(key, 2), amount)]


def centred(key, shape, width, most, cuts=(), kind=jnp.bfloat16):
    values = width * jax.random.normal(key, shape, jnp.float32)
    if cuts:
        values = values * level_of(key, shape, cuts, -0.22, 0.18)
    return jnp.clip(values, -most, most).astype(kind)


def setup_inputs(seed: int = 0) -> dict:
    splits = jax.random.split(jax.random.key(seed), 17)
    return {
        "tokens": centred(splits[0], (TOKENS, D), 1.0, 6.0, ((0, 32),)),
        "cotangent": centred(splits[1], (TOKENS, D), 1.0, 6.0, ((0, 32),)),
        "cont_lengths": jax.vmap(lambda own: uneven(own, NCONT, GROUP // 2, GROUP // 8, 1))(jax.random.split(splits[2], GROUPS)).reshape((GROUPS, NCONT)).astype(jnp.int32),
        "ln1_gain": jnp.clip(1.0 + 0.18 * jax.random.normal(splits[3], (LAYERS, D), jnp.float32), 0.099609375, 1.8984375).astype(jnp.bfloat16),
        "ln1_bias": centred(splits[4], (LAYERS, D), 0.5, 3.0, ((1, 4),)),
        "w_qkv": centred(splits[5], (LAYERS, D, 3 * D), D ** -0.5, 0.1875, ((1, 4),)),
        "q_bias": centred(splits[6], (LAYERS, D), 0.5, 3.0, ((1, 4),)),
        "v_bias": centred(splits[7], (LAYERS, D), 0.5, 3.0, ((1, 4),)),
        "w_out": centred(splits[8], (LAYERS, D, D), (D // 32) ** -0.5, 1.0, ((1, 4),)),
        "out_bias": centred(splits[9], (LAYERS, D), 0.3, 2.0, ((1, 4),)),
        "ln2_gain": jnp.clip(1.0 + 0.18 * jax.random.normal(splits[10], (LAYERS, D), jnp.float32), 0.099609375, 1.8984375).astype(jnp.bfloat16),
        "ln2_bias": centred(splits[11], (LAYERS, D), 0.5, 3.0, ((1, 4),)),
        "w_up": centred(splits[12], (LAYERS, D, FF), D ** -0.5, 0.1875, ((1, 4),)),
        "up_bias": centred(splits[13], (LAYERS, FF), 0.5, 3.0, ((1, 4),)),
        "w_down": centred(splits[14], (LAYERS, FF, D), (FF // 2) ** -0.5, 0.125, ((1, 4),)),
        "down_bias": centred(splits[15], (LAYERS, D), 0.3, 2.0, ((1, 4),)),
    }


EPSILON = 1e-05
NEG_LARGE = -1e+30
HIGHEST = lax.Precision.HIGHEST

@jax.custom_vjp
def low(v):
    return lax.optimization_barrier(v.astype(jnp.bfloat16)).astype(jnp.float32)

@jax.custom_vjp
def low_back(v):
    return v

def low_keep(v):
    return (low(v), None)

def low_pass(kept, grad):
    return (grad,)

def back_keep(v):
    return (v, None)

def back_low(kept, grad):
    return (low(grad),)
low.defvjp(low_keep, low_pass)
low_back.defvjp(back_keep, back_low)

def matmul(left, right):
    return jnp.dot(left, right, precision=HIGHEST)

def norm_apply(stream, norm_gain, norm_bias):
    row_mean = lax.optimization_barrier(jnp.mean(stream, -1, keepdims=True))
    centered = stream - row_mean
    variance = lax.optimization_barrier(jnp.mean(centered * centered, -1, keepdims=True))
    return centered * lax.rsqrt(variance + EPSILON) * norm_gain + norm_bias

def segment_ids(lengths):
    prompt_len = GROUP // 2
    cont_ends = jnp.cumsum(lengths.astype(jnp.int32)).astype(jnp.int32)
    positions = jnp.arange(prompt_len, dtype=jnp.int32)
    cont_ids = (1 + lax.optimization_barrier(jnp.sum((positions[:, None] >= cont_ends[None, :]).astype(jnp.int32), 1))).astype(jnp.int32)
    return jnp.concatenate([jnp.zeros((prompt_len,), jnp.int32), cont_ids])

def attend(queries, keys_in, values_in, segment):
    block_rows = min(512, GROUP)
    block_count = GROUP // block_rows
    key_heads = keys_in.reshape(GROUP, H, HD)
    value_heads = values_in.reshape(GROUP, H, HD)
    positions = jnp.arange(GROUP, dtype=jnp.int32)

    def one_block(pieces):
        query_block, query_pos, query_seg = pieces
        scores = jnp.einsum('qhd,khd->hqk', query_block, key_heads, precision=HIGHEST) * HD ** (-0.5)
        allowed = (positions[None, :] <= query_pos[:, None]) & ((segment[None, :] == 0) | (segment[None, :] == query_seg[:, None]))
        scores = low_back(jnp.where(allowed[None], scores, NEG_LARGE))
        probs = jax.nn.softmax(scores, axis=-1)
        mixed = jnp.einsum('hqk,khd->qhd', low(probs), value_heads, precision=HIGHEST)
        return mixed.reshape(block_rows, H * HD)
    result = lax.map(jax.checkpoint(one_block), (queries.reshape(block_count, block_rows, H, HD), positions.reshape(block_count, block_rows), segment.reshape(block_count, block_rows)))
    return result.reshape(GROUP, H * HD)

def layer_apply(stream, weights, segment):
    gain_one, bias_one, weight_qkv, bias_q, bias_v, weight_out, bias_out, gain_two, bias_two, weight_up, bias_up, weight_down, bias_down = weights
    hidden_one = low(norm_apply(stream, gain_one, bias_one))
    combined = matmul(hidden_one, weight_qkv)
    queries = low(low_back(combined[:, :D] + bias_q))
    keys_in = low(low_back(combined[:, D:2 * D]))
    values_in = low(low_back(combined[:, 2 * D:] + bias_v))
    attended = low(low_back(attend(queries, keys_in, values_in, segment)))
    middle = stream + low_back(matmul(attended, weight_out) + bias_out)
    hidden_two = low(norm_apply(middle, gain_two, bias_two))
    before_act = low_back(matmul(hidden_two, weight_up) + bias_up)
    activated = low(jax.nn.gelu(before_act, approximate=True))
    return middle + low_back(matmul(activated, weight_down) + bias_down)

def reference(tokens, cotangent, cont_lengths, ln1_gain, ln1_bias, w_qkv, q_bias, v_bias, w_out, out_bias, ln2_gain, ln2_bias, w_up, up_bias, w_down, down_bias):
    params = tuple((weight_array.astype(jnp.float32) for weight_array in (ln1_gain, ln1_bias, w_qkv, q_bias, v_bias, w_out, out_bias, ln2_gain, ln2_bias, w_up, up_bias, w_down, down_bias)))
    segments = jax.vmap(segment_ids)(cont_lengths)

    def forward(stream_all, weight_set):

        def one_group(pieces):
            stream, segment = pieces
            for layer_index in range(LAYERS):
                stream = layer_apply(stream, tuple((weight_array[layer_index] for weight_array in weight_set)), segment)
            return stream
        result = lax.map(jax.checkpoint(one_group), (stream_all.reshape(GROUPS, GROUP, D), segments))
        return result.reshape(TOKENS, D)
    final, pull = jax.vjp(forward, tokens.astype(jnp.float32), params)
    grad_tokens, grads = pull(cotangent.astype(jnp.float32))
    return (final.astype(jnp.bfloat16), grad_tokens.astype(jnp.bfloat16), grads[0], grads[1], grads[2], grads[3], grads[4], grads[5], grads[6], grads[7], grads[8], grads[9], grads[10], grads[11], grads[12])
```

```python
import jax
import jax.numpy as jnp
from jax import lax
from jax.sharding import PartitionSpec as P

H = 16
LAYERS = 1


EPSILON = 1e-05
NEG_LARGE = -1e30


def norm_apply(stream, norm_gain, norm_bias):
    row_mean = jnp.mean(stream, -1, keepdims=True)
    centered = stream - row_mean
    variance = jnp.mean(centered * centered, -1, keepdims=True)
    return centered * lax.rsqrt(variance + EPSILON) * norm_gain + norm_bias


def gelu_tanh(values_in):
    return jax.nn.gelu(values_in, approximate=True)


def segment_ids(lengths, group_len):
    prompt_len = group_len // 2
    order = jnp.arange(lengths.shape[0], dtype=jnp.int32)
    cont_ends = jnp.sum(jnp.where(order[:, None] <= order[None, :], lengths[:, None], 0), 0)
    positions = jnp.arange(prompt_len, dtype=jnp.int32)
    cont_ids = 1 + jnp.sum((positions[:, None] >= cont_ends[None, :]).astype(jnp.int32), 1)
    return jnp.concatenate([jnp.zeros((prompt_len,), jnp.int32), cont_ids])


def fetch_weights(params, layer_index):
    sliced = [weight_array[layer_index] for weight_array in params]
    return (
        lax.all_gather(sliced[0], "fsdp", axis=0, tiled=True),
        lax.all_gather(sliced[1], "fsdp", axis=0, tiled=True),
        lax.all_gather(sliced[2], "fsdp", axis=0, tiled=True),
        lax.all_gather(sliced[3], "fsdp", axis=0, tiled=True),
        lax.all_gather(sliced[4], "fsdp", axis=0, tiled=True),
        lax.all_gather(sliced[5], "fsdp", axis=0, tiled=True),
        lax.all_gather(sliced[6], "fsdp", axis=0, tiled=True),
        lax.all_gather(sliced[7], "fsdp", axis=0, tiled=True),
        lax.all_gather(sliced[8], "fsdp", axis=0, tiled=True),
        lax.all_gather(sliced[9], "fsdp", axis=0, tiled=True),
        lax.all_gather(sliced[10], "fsdp", axis=0, tiled=True),
        lax.all_gather(sliced[11], "fsdp", axis=0, tiled=True),
        lax.all_gather(sliced[12], "fsdp", axis=0, tiled=True),
    )


def fetch_again(params, layer_index):
    sliced = [weight_array[layer_index] for weight_array in params]
    return (
        lax.all_gather(sliced[0], "fsdp", axis=0, tiled=True),
        lax.all_gather(sliced[1], "fsdp", axis=0, tiled=True),
        lax.all_gather(sliced[2], "fsdp", axis=0, tiled=True),
        lax.all_gather(sliced[3], "fsdp", axis=0, tiled=True),
        lax.all_gather(sliced[4], "fsdp", axis=0, tiled=True),
        lax.all_gather(sliced[5], "fsdp", axis=0, tiled=True),
        lax.all_gather(sliced[6], "fsdp", axis=0, tiled=True),
        lax.all_gather(sliced[7], "fsdp", axis=0, tiled=True),
        lax.all_gather(sliced[8], "fsdp", axis=0, tiled=True),
        lax.all_gather(sliced[9], "fsdp", axis=0, tiled=True),
        lax.all_gather(sliced[10], "fsdp", axis=0, tiled=True),
        lax.all_gather(sliced[11], "fsdp", axis=0, tiled=True),
        lax.all_gather(sliced[12], "fsdp", axis=0, tiled=True),
    )


def reduce_sectioned(grads):
    shards = (
        lax.psum_scatter(
            grads[0].astype(jnp.bfloat16), "fsdp", scatter_dimension=0, tiled=True
        ).astype(jnp.float32),
        lax.psum_scatter(
            grads[1].astype(jnp.bfloat16), "fsdp", scatter_dimension=0, tiled=True
        ).astype(jnp.float32),
        lax.psum_scatter(
            grads[2].astype(jnp.bfloat16), "fsdp", scatter_dimension=0, tiled=True
        ).astype(jnp.float32),
        lax.psum_scatter(
            grads[3].astype(jnp.bfloat16), "fsdp", scatter_dimension=0, tiled=True
        ).astype(jnp.float32),
        lax.psum_scatter(
            grads[4].astype(jnp.bfloat16), "fsdp", scatter_dimension=0, tiled=True
        ).astype(jnp.float32),
        lax.psum_scatter(
            grads[5].astype(jnp.bfloat16), "fsdp", scatter_dimension=0, tiled=True
        ).astype(jnp.float32),
        lax.psum_scatter(
            grads[6].astype(jnp.bfloat16), "fsdp", scatter_dimension=0, tiled=True
        ).astype(jnp.float32),
        lax.psum_scatter(
            grads[7].astype(jnp.bfloat16), "fsdp", scatter_dimension=0, tiled=True
        ).astype(jnp.float32),
        lax.psum_scatter(
            grads[8].astype(jnp.bfloat16), "fsdp", scatter_dimension=0, tiled=True
        ).astype(jnp.float32),
        lax.psum_scatter(
            grads[9].astype(jnp.bfloat16), "fsdp", scatter_dimension=0, tiled=True
        ).astype(jnp.float32),
        lax.psum_scatter(
            grads[10].astype(jnp.bfloat16), "fsdp", scatter_dimension=0, tiled=True
        ).astype(jnp.float32),
        lax.psum_scatter(
            grads[11].astype(jnp.bfloat16), "fsdp", scatter_dimension=0, tiled=True
        ).astype(jnp.float32),
        lax.psum_scatter(
            grads[12].astype(jnp.bfloat16), "fsdp", scatter_dimension=0, tiled=True
        ).astype(jnp.float32),
    )
    return (
        lax.psum(shards[0].astype(jnp.bfloat16), "dp").astype(jnp.float32),
        lax.psum(shards[1].astype(jnp.bfloat16), "dp").astype(jnp.float32),
        lax.psum(shards[2].astype(jnp.bfloat16), "dp").astype(jnp.float32),
        lax.psum(shards[3].astype(jnp.bfloat16), "dp").astype(jnp.float32),
        lax.psum(shards[4].astype(jnp.bfloat16), "dp").astype(jnp.float32),
        lax.psum(shards[5].astype(jnp.bfloat16), "dp").astype(jnp.float32),
        lax.psum(shards[6].astype(jnp.bfloat16), "dp").astype(jnp.float32),
        lax.psum(shards[7].astype(jnp.bfloat16), "dp").astype(jnp.float32),
        lax.psum(shards[8].astype(jnp.bfloat16), "dp").astype(jnp.float32),
        lax.psum(shards[9].astype(jnp.bfloat16), "dp").astype(jnp.float32),
        lax.psum(shards[10].astype(jnp.bfloat16), "dp").astype(jnp.float32),
        lax.psum(shards[11].astype(jnp.bfloat16), "dp").astype(jnp.float32),
        lax.psum(shards[12].astype(jnp.bfloat16), "dp").astype(jnp.float32),
    )


def body(
    tokens,
    cotangent,
    cont_lengths,
    ln1_gain,
    ln1_bias,
    w_qkv,
    q_bias,
    v_bias,
    w_out,
    out_bias,
    ln2_gain,
    ln2_bias,
    w_up,
    up_bias,
    w_down,
    down_bias,
):
    params = (
        ln1_gain,
        ln1_bias,
        w_qkv,
        q_bias,
        v_bias,
        w_out,
        out_bias,
        ln2_gain,
        ln2_bias,
        w_up,
        up_bias,
        w_down,
        down_bias,
    )
    row_count = tokens.shape[0]
    model_width = tokens.shape[1]
    fsdp_size = lax.axis_size("fsdp")
    group_len = row_count * fsdp_size
    head_count = H
    head_dim = model_width // head_count
    score_scale = head_dim ** (-0.5)
    block_size = min(512, group_len // 2)
    block_total = group_len // block_size
    seg_all = segment_ids(cont_lengths[0], group_len)
    first_pos = lax.axis_index("fsdp") * row_count
    query_pos = first_pos + jnp.arange(row_count, dtype=jnp.int32)
    query_seg = lax.dynamic_slice_in_dim(seg_all, first_pos, row_count)
    key_range = jnp.arange(block_size, dtype=jnp.int32)

    def block_keys(block_index):
        block_start = block_index * block_size
        key_seg = lax.dynamic_slice_in_dim(seg_all, block_start, block_size)
        key_pos = block_start + key_range
        allowed = (key_pos[None, :] <= query_pos[:, None]) & (
            (key_seg[None, :] == 0) | (key_seg[None, :] == query_seg[:, None])
        )
        needed_flag = (block_start <= first_pos + row_count - 1) & (
            (key_seg[0] == 0) | (key_seg[block_size - 1] >= query_seg[0])
        )
        return (block_start, allowed, needed_flag)

    def key_value_block(keys_all, values_all, block_start):
        key_block = lax.dynamic_slice_in_dim(keys_all, block_start, block_size, 0).reshape(
            block_size, head_count, head_dim
        )
        value_block = lax.dynamic_slice_in_dim(values_all, block_start, block_size, 0).reshape(
            block_size, head_count, head_dim
        )
        return (key_block, value_block)

    stream = tokens.astype(jnp.float32)
    layer_index = 0
    weights = fetch_weights(params, layer_index)
    (
        gain_one,
        bias_one,
        weight_qkv,
        bias_q,
        bias_v,
        weight_out,
        bias_out,
        gain_two,
        bias_two,
        weight_up,
        bias_up,
        weight_down,
        bias_down,
    ) = weights
    hidden_one = norm_apply(
        stream, gain_one.astype(jnp.float32), bias_one.astype(jnp.float32)
    ).astype(jnp.bfloat16)
    combined = jnp.dot(hidden_one, weight_qkv, preferred_element_type=jnp.float32)
    queries = (combined[:, :model_width] + bias_q.astype(jnp.float32)).astype(jnp.bfloat16)
    keys_local = combined[:, model_width : 2 * model_width].astype(jnp.bfloat16)
    values_local = (combined[:, 2 * model_width :] + bias_v.astype(jnp.float32)).astype(
        jnp.bfloat16
    )
    keys_all = lax.all_gather(keys_local, "fsdp", axis=0, tiled=True)
    values_all = lax.all_gather(values_local, "fsdp", axis=0, tiled=True)
    query_heads = queries.reshape(row_count, head_count, head_dim)
    start_state = (
        jnp.full((head_count, row_count), NEG_LARGE, jnp.float32),
        jnp.zeros((head_count, row_count), jnp.float32),
        jnp.zeros((row_count, head_count, head_dim), jnp.float32),
    )

    def visit(block_index, carry):
        block_start, allowed, needed_flag = block_keys(block_index)

        def visit_work(state):
            row_max, row_total, weighted = state
            key_block, value_block = key_value_block(keys_all, values_all, block_start)
            scores = (
                jnp.einsum(
                    "qhd,khd->hqk", query_heads, key_block, preferred_element_type=jnp.float32
                )
                * score_scale
            )
            scores = jnp.where(allowed[None], scores, NEG_LARGE)
            new_max = jnp.maximum(row_max, jnp.max(scores, -1))
            probs = jnp.where(allowed[None], jnp.exp(scores - new_max[:, :, None]), 0.0)
            fade = jnp.exp(row_max - new_max)
            row_total = row_total * fade + jnp.sum(probs, -1)
            weighted = weighted * fade.T[:, :, None] + jnp.einsum(
                "hqk,khd->qhd",
                probs.astype(jnp.bfloat16),
                value_block,
                preferred_element_type=jnp.float32,
            )
            return (new_max, row_total, weighted)

        return lax.cond(needed_flag, visit_work, lambda state: state, carry)

    row_max, row_total, weighted = lax.fori_loop(0, block_total, visit, start_state)
    attended = (weighted / row_total.T[:, :, None]).reshape(row_count, model_width)
    attended, log_total = (attended, row_max + jnp.log(row_total))
    attn_low = attended.astype(jnp.bfloat16)
    middle = stream + (
        jnp.dot(attn_low, weight_out, preferred_element_type=jnp.float32)
        + bias_out.astype(jnp.float32)
    )
    hidden_two = norm_apply(
        middle, gain_two.astype(jnp.float32), bias_two.astype(jnp.float32)
    ).astype(jnp.bfloat16)
    before_act = jnp.dot(
        hidden_two, weight_up, preferred_element_type=jnp.float32
    ) + bias_up.astype(jnp.float32)
    activated = gelu_tanh(before_act).astype(jnp.bfloat16)
    result = middle + (
        jnp.dot(activated, weight_down, preferred_element_type=jnp.float32)
        + bias_down.astype(jnp.float32)
    )
    stream, saved = (
        result,
        (
            stream,
            hidden_one,
            queries,
            keys_all,
            values_all,
            attended,
            log_total,
            attn_low,
            middle,
            hidden_two,
            before_act,
            activated,
        ),
    )
    saved_layers = [saved]
    output = stream.astype(jnp.bfloat16)
    grad_stream = cotangent.astype(jnp.float32)
    reduced = [None] * LAYERS
    for layer_index in reversed(range(LAYERS)):
        weights = fetch_again(params, layer_index)
        (
            layer_gain_one,
            layer_bias_one,
            layer_weight_qkv,
            layer_bias_q,
            layer_bias_v,
            layer_weight_out,
            layer_bias_out,
            layer_gain_two,
            layer_bias_two,
            layer_weight_up,
            layer_bias_up,
            layer_weight_down,
            layer_bias_down,
        ) = weights
        (
            layer_stream,
            layer_hidden_one,
            layer_queries,
            layer_keys_all,
            layer_values_all,
            layer_attended,
            layer_log_total,
            layer_attn_low,
            layer_middle,
            layer_hidden_two,
            layer_before_act,
            layer_activated,
        ) = saved_layers[layer_index]
        grad_branch = grad_stream.astype(jnp.bfloat16)
        grad_bias_down = jnp.sum(grad_branch.astype(jnp.float32), 0)
        grad_weight_down = jnp.einsum(
            "tf,td->fd", layer_activated, grad_branch, preferred_element_type=jnp.float32
        )
        grad_activated = jnp.einsum(
            "td,fd->tf", grad_branch, layer_weight_down, preferred_element_type=jnp.float32
        )
        grad_before = jax.vjp(gelu_tanh, layer_before_act)[1](grad_activated)[0].astype(
            jnp.bfloat16
        )
        grad_bias_up = jnp.sum(grad_before.astype(jnp.float32), 0)
        grad_weight_up = jnp.einsum(
            "td,tf->df", layer_hidden_two, grad_before, preferred_element_type=jnp.float32
        )
        grad_hidden_two = jnp.einsum(
            "tf,df->td", grad_before, layer_weight_up, preferred_element_type=jnp.float32
        )
        norm_pull = jax.vjp(
            norm_apply,
            layer_middle,
            layer_gain_two.astype(jnp.float32),
            layer_bias_two.astype(jnp.float32),
        )[1]
        grad_middle_norm, grad_gain_two, grad_bias_two = norm_pull(grad_hidden_two)
        grad_middle = grad_stream + grad_middle_norm
        grad_attn_branch = grad_middle.astype(jnp.bfloat16)
        grad_bias_out = jnp.sum(grad_attn_branch.astype(jnp.float32), 0)
        grad_weight_out = jnp.einsum(
            "td,te->de", layer_attn_low, grad_attn_branch, preferred_element_type=jnp.float32
        )
        grad_attended = jnp.einsum(
            "te,de->td", grad_attn_branch, layer_weight_out, preferred_element_type=jnp.float32
        ).astype(jnp.bfloat16)
        layer_row_delta = jnp.sum(
            (grad_attended.astype(jnp.float32) * layer_attended).reshape(
                row_count, head_count, head_dim
            ),
            -1,
        ).T
        attend_keys_all = layer_keys_all
        attend_values_all = layer_values_all
        row_delta = layer_row_delta
        attend_log_total = layer_log_total
        attend_query_heads = layer_queries.reshape(row_count, head_count, head_dim)
        grad_heads = grad_attended.reshape(row_count, head_count, head_dim)
        empty_keys = jnp.zeros((group_len, head_count, head_dim), jnp.float32)
        empty_query = jnp.zeros((row_count, head_count, head_dim), jnp.float32)
        attend_start_state = (empty_query, empty_keys, empty_keys)

        def attend_visit(block_index, carry):
            block_start, allowed, needed_flag = block_keys(block_index)

            def attend_work(state):
                key_block, value_block = key_value_block(
                    attend_keys_all, attend_values_all, block_start
                )
                scores = (
                    jnp.einsum(
                        "qhd,khd->hqk",
                        attend_query_heads,
                        key_block,
                        preferred_element_type=jnp.float32,
                    )
                    * score_scale
                )
                probs = jnp.where(
                    allowed[None], jnp.exp(scores - attend_log_total[:, :, None]), 0.0
                )
                grad_probs = jnp.einsum(
                    "qhd,khd->hqk", grad_heads, value_block, preferred_element_type=jnp.float32
                )
                grad_scores = (probs * (grad_probs - row_delta[:, :, None])).astype(jnp.bfloat16)
                grad_query = (
                    state[0]
                    + jnp.einsum(
                        "hqk,khd->qhd", grad_scores, key_block, preferred_element_type=jnp.float32
                    )
                    * score_scale
                )
                key_part = (
                    jnp.einsum(
                        "hqk,qhd->khd",
                        grad_scores,
                        attend_query_heads,
                        preferred_element_type=jnp.float32,
                    )
                    * score_scale
                )
                value_part = jnp.einsum(
                    "hqk,qhd->khd",
                    probs.astype(jnp.bfloat16),
                    grad_heads,
                    preferred_element_type=jnp.float32,
                )
                grad_key = lax.dynamic_update_slice_in_dim(state[1], key_part, block_start, 0)
                grad_value = lax.dynamic_update_slice_in_dim(state[2], value_part, block_start, 0)
                return (grad_query, grad_key, grad_value)

            return lax.cond(needed_flag, attend_work, lambda state: state, carry)

        final_state = lax.fori_loop(0, block_total, attend_visit, attend_start_state)
        layer_grad_query = final_state[0].reshape(row_count, model_width)
        grad_key_all = final_state[1].reshape(group_len, model_width)
        grad_value_all = final_state[2].reshape(group_len, model_width)
        grad_keys = lax.psum_scatter(
            grad_key_all.astype(jnp.bfloat16), "fsdp", scatter_dimension=0, tiled=True
        )
        grad_values = lax.psum_scatter(
            grad_value_all.astype(jnp.bfloat16), "fsdp", scatter_dimension=0, tiled=True
        )
        grad_query_low = layer_grad_query.astype(jnp.bfloat16)
        grad_combined = jnp.concatenate([grad_query_low, grad_keys, grad_values], 1)
        grad_bias_q = jnp.sum(grad_query_low.astype(jnp.float32), 0)
        grad_bias_v = jnp.sum(grad_values.astype(jnp.float32), 0)
        grad_weight_qkv = jnp.einsum(
            "td,te->de", layer_hidden_one, grad_combined, preferred_element_type=jnp.float32
        )
        grad_hidden_one = jnp.einsum(
            "te,de->td", grad_combined, layer_weight_qkv, preferred_element_type=jnp.float32
        )
        norm_pull_one = jax.vjp(
            norm_apply,
            layer_stream,
            layer_gain_one.astype(jnp.float32),
            layer_bias_one.astype(jnp.float32),
        )[1]
        grad_stream_norm, grad_gain_one, grad_bias_one = norm_pull_one(grad_hidden_one)
        grads = (
            grad_gain_one,
            grad_bias_one,
            grad_weight_qkv,
            grad_bias_q,
            grad_bias_v,
            grad_weight_out,
            grad_bias_out,
            grad_gain_two,
            grad_bias_two,
            grad_weight_up,
            grad_bias_up,
            grad_weight_down,
            grad_bias_down,
        )
        grad_stream, grads = (grad_middle + grad_stream_norm, grads)
        reduced[layer_index] = reduce_sectioned(grads)
    stacked = [jnp.stack([reduced[0][slot]]) for slot in range(13)]
    return (
        output,
        grad_stream.astype(jnp.bfloat16),
        stacked[0],
        stacked[1],
        stacked[2],
        stacked[3],
        stacked[4],
        stacked[5],
        stacked[6],
        stacked[7],
        stacked[8],
        stacked[9],
        stacked[10],
        stacked[11],
        stacked[12],
    )


def solution(mesh):
    in_specs = (
        P(("dp", "fsdp"), None),
        P(("dp", "fsdp"), None),
        P("dp", None),
        P(None, "fsdp"),
        P(None, "fsdp"),
        P(None, "fsdp", None),
        P(None, "fsdp"),
        P(None, "fsdp"),
        P(None, "fsdp", None),
        P(None, "fsdp"),
        P(None, "fsdp"),
        P(None, "fsdp"),
        P(None, "fsdp", None),
        P(None, "fsdp"),
        P(None, "fsdp", None),
        P(None, "fsdp"),
    )
    out_specs = (
        P(("dp", "fsdp"), None),
        P(("dp", "fsdp"), None),
        P(None, "fsdp"),
        P(None, "fsdp"),
        P(None, "fsdp", None),
        P(None, "fsdp"),
        P(None, "fsdp"),
        P(None, "fsdp", None),
        P(None, "fsdp"),
        P(None, "fsdp"),
        P(None, "fsdp"),
        P(None, "fsdp", None),
        P(None, "fsdp"),
        P(None, "fsdp", None),
        P(None, "fsdp"),
    )
    return jax.shard_map(body, mesh=mesh, in_specs=in_specs, out_specs=out_specs, check_vma=False)
```

```python
import functools

import jax
import jax.numpy as jnp
from jax import lax
from jax.experimental import pallas as pl
from jax.experimental.pallas import tpu as pltpu
from jax.sharding import PartitionSpec as P

H = 16
EPSILON = 1e-05
NEG_LARGE = -1e30
F32 = jnp.float32
BF = jnp.bfloat16
MIB = 2**20


def rnd(v):
    return v.astype(BF)


def dot_last(left, right):
    return lax.dot_general(left, right, (((1,), (1,)), ((), ())), preferred_element_type=F32)


def dot_mm(left, right):
    return jnp.dot(left, right, preferred_element_type=F32)


def key_ranges(start, group_len):
    prompt = group_len // 2
    if start < prompt:
        return start, start
    return prompt, max(prompt, start - group_len // 8)


def allowed_mask(shape, key_start, query_start, low_row):
    key_pos = lax.broadcasted_iota(jnp.int32, shape, 0) + key_start
    query_pos = lax.broadcasted_iota(jnp.int32, shape, 1) + query_start
    return (key_pos <= query_pos) & (key_pos >= low_row)


def attend_kernel(group_len, head_dim, q_ref, k_ref, v_ref, low_ref, o_ref, lse_ref):
    size = min(512, group_len // 4)
    scale = jnp.asarray(head_dim**-0.5, BF)
    values_t = v_ref[...].astype(F32).T.astype(BF)
    for start in range(0, group_len, size):
        stop = start + size
        full, near = key_ranges(start, group_len)
        results = []
        for head in range(128 // head_dim):
            lanes = slice(head * head_dim, (head + 1) * head_dim)
            queries = q_ref[start:stop, lanes] * scale
            part = dot_last(k_ref[near:stop, lanes], queries)
            ok = allowed_mask(part.shape, near, start, low_ref[0:1, start:stop])
            part = jnp.where(ok, part, NEG_LARGE)
            top = jnp.max(part, 0, keepdims=True)
            if full:
                rest = dot_last(k_ref[0:full, lanes], queries)
                top = jnp.maximum(top, jnp.max(rest, 0, keepdims=True))
            part = jnp.exp(part - top)
            total = jnp.sum(part, 0, keepdims=True)
            mixed = dot_mm(values_t[lanes, near:stop], part.astype(BF))
            if full:
                rest = jnp.exp(rest - top)
                total += jnp.sum(rest, 0, keepdims=True)
                mixed += dot_mm(values_t[lanes, 0:full], rest.astype(BF))
            results.append(mixed * (1.0 / total))
            lse_ref[0, head : head + 1, start:stop] = top + jnp.log(total)
        o_ref[start:stop, :] = jnp.concatenate(results, 0).T.astype(BF)


def attend_grad_kernel(
    group_len, head_dim, q_ref, k_ref, v_ref, low_ref, o_ref, lse_ref, do_ref, dq_ref, dk_ref, dv_ref, dk_sum, dv_sum
):
    size = min(256, group_len // 8)
    scale = jnp.asarray(head_dim**-0.5, BF)
    keys_t = k_ref[...].astype(F32).T.astype(BF)
    dk_sum[...] = jnp.zeros_like(dk_sum)
    dv_sum[...] = jnp.zeros_like(dv_sum)
    for start in range(0, group_len, size):
        stop = start + size
        full, near = key_ranges(start, group_len)
        product_t = (do_ref[start:stop, :].astype(F32) * o_ref[start:stop, :].astype(F32)).T
        results = []
        for head in range(128 // head_dim):
            lanes = slice(head * head_dim, (head + 1) * head_dim)
            queries = q_ref[start:stop, lanes] * scale
            grads = do_ref[start:stop, lanes]
            delta = jnp.sum(product_t[lanes, :], 0, keepdims=True)
            lse = lse_ref[0, head : head + 1, start:stop]
            dq_t = jnp.zeros((head_dim, size), F32)
            for first, last, masked in ((near, stop, True), (0, full, False)):
                if first == last:
                    continue
                probs = jnp.exp(dot_last(k_ref[first:last, lanes], queries) - lse)
                if masked:
                    ok = allowed_mask(probs.shape, first, start, low_ref[0:1, start:stop])
                    probs = jnp.where(ok, probs, 0.0)
                grad_probs = dot_last(v_ref[first:last, lanes], grads)
                ds = (probs * (grad_probs - delta)).astype(BF)
                dv_sum[head, first:last, :] += dot_mm(probs.astype(BF), grads)
                dk_sum[head, first:last, :] += dot_mm(ds, queries)
                dq_t += dot_mm(keys_t[lanes, first:last], ds)
            results.append(dq_t * head_dim**-0.5)
        dq_ref[start:stop, :] = jnp.concatenate(results, 0).T.astype(BF)
    heads = range(128 // head_dim)
    dk_ref[...] = jnp.concatenate([dk_sum[head] for head in heads], 1).astype(BF)
    dv_ref[...] = jnp.concatenate([dv_sum[head] for head in heads], 1).astype(BF)


def attend(combined, low, head_dim):
    group_len, width = combined.shape[0], combined.shape[1] // 3
    steps = width // 128
    heads = 128 // head_dim
    block = lambda offset: pl.BlockSpec((group_len, 128), lambda i: (0, offset + i))
    return pl.pallas_call(
        functools.partial(attend_kernel, group_len, head_dim),
        grid=(steps,),
        in_specs=[block(0), block(steps), block(2 * steps), pl.BlockSpec((1, group_len), lambda i: (0, 0))],
        out_specs=[block(0), pl.BlockSpec((1, heads, group_len), lambda i: (i, 0, 0))],
        out_shape=[
            jax.ShapeDtypeStruct((group_len, width), BF),
            jax.ShapeDtypeStruct((steps, heads, group_len), F32),
        ],
        compiler_params=pltpu.CompilerParams(vmem_limit_bytes=56 * MIB),
        cost_estimate=pl.CostEstimate(flops=15 * 10**9, bytes_accessed=4 * MIB, transcendentals=0),
    )(combined, combined, combined, low)


def attend_grad(combined, low, mixed, lse, grad_mixed, head_dim):
    group_len, width = mixed.shape
    steps = width // 128
    heads = 128 // head_dim
    block = lambda offset: pl.BlockSpec((group_len, 128), lambda i: (0, offset + i))
    return pl.pallas_call(
        functools.partial(attend_grad_kernel, group_len, head_dim),
        grid=(steps,),
        in_specs=[
            block(0),
            block(steps),
            block(2 * steps),
            pl.BlockSpec((1, group_len), lambda i: (0, 0)),
            block(0),
            pl.BlockSpec((1, heads, group_len), lambda i: (i, 0, 0)),
            block(0),
        ],
        out_specs=[block(0)] * 3,
        out_shape=[jax.ShapeDtypeStruct((group_len, width), BF)] * 3,
        scratch_shapes=[pltpu.VMEM((heads, group_len, head_dim), F32)] * 2,
        compiler_params=pltpu.CompilerParams(vmem_limit_bytes=56 * MIB),
        cost_estimate=pl.CostEstimate(flops=25 * 10**9, bytes_accessed=8 * MIB, transcendentals=0),
    )(combined, combined, combined, low, mixed, lse, grad_mixed)


class Cut:
    def __init__(self, rows, columns, column_parts, replicas, shards):
        self.rows, self.columns, self.shards, self.replicas = rows, columns, shards, replicas
        self.nc, self.nr = column_parts, replicas // column_parts
        self.r, self.c = rows // self.nr, columns // self.nc

    def place(self, piece):
        row = lax.rem(piece, self.nr) * self.r
        column = lax.div(piece, self.nr) * self.c
        return pl.multiple_of(row, 8 if self.r % 16 else 16), pl.multiple_of(column, 128)

    def spot(self, piece, base=0):
        row, column = self.place(piece)
        return pl.ds(base + row, self.r), pl.ds(column, self.c)

    def of(self, shard, piece):
        return lax.dynamic_slice(shard, self.place(piece), (self.r, self.c))

    @property
    def copies(self):
        return 1 + (self.shards - 1) * self.replicas


def fetch(cut, me, z, slots, shard, whole, sems):
    base = pl.multiple_of(z * cut.rows, 16)
    copies = [pltpu.make_async_copy(shard, whole.at[pl.ds(base, cut.rows), :], sems.at[0])]
    for d in range(1, cut.shards):
        base = pl.multiple_of(lax.rem(z + cut.shards - d, cut.shards) * cut.rows, 16)
        for j in range(cut.replicas):
            copies.append(
                pltpu.make_async_copy(
                    slots[j].at[d - 1],
                    whole.at[cut.spot(jnp.bitwise_xor(me, j), base)],
                    sems.at[len(copies)],
                )
            )
    return copies


def start(copies):
    for copy in copies:
        copy.start()


def finish(copies):
    for copy in copies:
        copy.wait()


SMEM_SPEC = pl.BlockSpec(memory_space=pltpu.SMEM)
ANY_SPEC = pl.BlockSpec(memory_space=pl.ANY)
VMEM_SPEC = pl.BlockSpec(memory_space=pltpu.VMEM)


def cost(flops, size):
    return pl.CostEstimate(flops=int(flops), bytes_accessed=int(size), transcendentals=0)


def moments(stream):
    mean = jnp.mean(stream, -1, keepdims=True)
    centered = stream - mean
    scale = lax.rsqrt(jnp.mean(centered * centered, -1, keepdims=True) + EPSILON)
    return centered * scale, scale


def norm_grad(grad_hidden, gain, normal, scale):
    t = grad_hidden * gain
    return scale * (
        t - jnp.mean(t, -1, keepdims=True) - normal * jnp.mean(t * normal, -1, keepdims=True)
    )


def project_kernel(place, block, gain, bias, weight, bias_qkv, h_in, c_in, h_out, c_out):
    normal, _ = moments(block[...].astype(F32))
    hidden = rnd(normal * gain[...] + bias[...])
    h_out[...] = hidden
    c_out[...] = rnd(dot_mm(hidden, weight[...]) + bias_qkv[...])


def project(place, block, gain, bias, weight, bias_qkv, h_all, c_all, distance, shards):
    rows, width = block.shape
    whole = lambda a: pl.BlockSpec(a.shape, lambda i, s: (0,) * a.ndim)
    at = lambda i, s: (lax.rem(s[1] + shards - distance, shards), 0)
    return pl.pallas_call(
        project_kernel,
        grid_spec=pltpu.PrefetchScalarGridSpec(
            num_scalar_prefetch=1,
            grid=(1,),
            in_specs=[whole(a) for a in (block, gain, bias, weight, bias_qkv)] + [ANY_SPEC] * 2,
            out_specs=[pl.BlockSpec((rows, width), at), pl.BlockSpec((rows, c_all.shape[1]), at)],
        ),
        out_shape=[jax.ShapeDtypeStruct(a.shape, BF) for a in (h_all, c_all)],
        input_output_aliases={6: 0, 7: 1},
        compiler_params=pltpu.CompilerParams(vmem_limit_bytes=40 * MIB),
        cost_estimate=cost(2 * rows * width * c_all.shape[1], 6 * MIB),
    )(place, block, gain, bias, weight, bias_qkv, h_all, c_all)


GELU_A = 0.7978845608028654
GELU_B = 0.044715


def gelu_both(u):
    square = u * u
    t = jnp.tanh(GELU_A * u * (1.0 + GELU_B * square))
    value = 0.5 * u * (1.0 + t)
    slope = 0.5 * (1.0 + t) + 0.5 * u * (1.0 - t * t) * (GELU_A * (1.0 + 3.0 * GELU_B * square))
    return value, slope


def forward_kernel(cuts, step, place, mixed, tokens, vectors, bias_up, *refs):
    count = cuts[0].replicas
    lists, refs = refs[: 3 * (count + 1)], refs[3 * (count + 1) :]
    out, hidden, middle, acted, slope, w_out, w_up, w_down, *sems = refs
    me, z = place[0], place[1]
    loads = []
    for n, (cut, whole) in enumerate(zip(cuts, (w_out, w_up, w_down))):
        own = lists[n * (count + 1) : (n + 1) * (count + 1)]
        loads.append(fetch(cut, me, z, own[:count], own[count], whole, sems[n]))
        start(loads[-1])
    finish(loads[0])
    stream = tokens[...].astype(F32) + (dot_mm(mixed[...], w_out[...]) + vectors[0:1, :])
    middle[...] = stream
    normal, _ = moments(stream)
    hidden[...] = rnd(normal * vectors[1:2, :] + vectors[2:3, :])
    finish(loads[1])
    finish(loads[2])
    total = vectors[3:4, :] + stream
    for block in range(0, w_up.shape[1], step):
        columns = slice(block, block + step)
        u = dot_mm(hidden[...], w_up[:, columns]) + bias_up[:, columns]
        value, grad = gelu_both(u)
        value = rnd(value)
        acted[:, columns] = value
        slope[:, columns] = rnd(grad)
        total += dot_mm(value, w_down[columns, :])
    out[...] = rnd(total)


def feed_forward(place, mixed, tokens, vectors, bias_up, cuts, lists):
    rows, width = tokens.shape
    hidden = bias_up.shape[1]
    flat = [a for own in lists for a in own]
    return pl.pallas_call(
        functools.partial(forward_kernel, cuts, min(1024, hidden)),
        in_specs=[SMEM_SPEC] + [VMEM_SPEC] * 4 + [ANY_SPEC] * len(flat),
        out_specs=[VMEM_SPEC] * 5,
        out_shape=[
            jax.ShapeDtypeStruct((rows, width), BF),
            jax.ShapeDtypeStruct((rows, width), BF),
            jax.ShapeDtypeStruct((rows, width), F32),
            jax.ShapeDtypeStruct((rows, hidden), BF),
            jax.ShapeDtypeStruct((rows, hidden), BF),
        ],
        scratch_shapes=[
            pltpu.VMEM((width, width), BF),
            pltpu.VMEM((width, hidden), BF),
            pltpu.VMEM((hidden, width), BF),
        ]
        + [pltpu.SemaphoreType.DMA((cut.copies,)) for cut in cuts],
        compiler_params=pltpu.CompilerParams(vmem_limit_bytes=60 * MIB),
        cost_estimate=cost(2 * rows * width * (width + 2 * hidden), 34 * MIB),
    )(place, mixed, tokens, vectors, bias_up, *flat)


def backward_kernel(cuts, step, place, dm, slope, middle, vectors, *refs):
    count = cuts[0].replicas
    lists, refs = refs[: 3 * (count + 1)], refs[3 * (count + 1) :]
    du, dx2, da, do, grad_up, sums, w_out, w_up, w_down, *sems = refs
    me, z = place[0], place[1]
    loads = []
    for n, whole in ((2, w_down), (1, w_up), (0, w_out)):
        own = lists[n * (count + 1) : (n + 1) * (count + 1)]
        loads.append(fetch(cuts[n], me, z, own[:count], own[count], whole, sems[n]))
        start(loads[-1])
    finish(loads[0])
    finish(loads[1])
    dh2 = jnp.zeros(middle.shape, F32)
    for block in range(0, w_up.shape[1], step):
        columns = slice(block, block + step)
        part = rnd(dot_last(dm[...], w_down[columns, :]) * slope[:, columns].astype(F32))
        du[:, columns] = part
        grad_up[:, columns] = jnp.sum(part.astype(F32), 0, keepdims=True)
        dh2 += dot_last(part, w_up[:, columns])
    normal, scale = moments(middle[...])
    incoming = dm[...].astype(F32)
    stream = incoming + norm_grad(dh2, vectors[1:2, :], normal, scale)
    dx2[...] = stream
    low = rnd(stream)
    da[...] = low
    finish(loads[2])
    do[...] = rnd(dot_last(low, w_out[...]))
    sums[0:1, :] = jnp.sum(incoming, 0, keepdims=True)
    sums[1:2, :] = jnp.sum(dh2 * normal, 0, keepdims=True)
    sums[2:3, :] = jnp.sum(dh2, 0, keepdims=True)
    sums[3:4, :] = jnp.sum(low.astype(F32), 0, keepdims=True)
    sums[4:8, :] = jnp.zeros((4, sums.shape[1]), F32)


def feed_backward(place, dm, slope, middle, vectors, cuts, lists):
    rows, width = dm.shape
    hidden = slope.shape[1]
    flat = [a for own in lists for a in own]
    return pl.pallas_call(
        functools.partial(backward_kernel, cuts, min(1024, hidden)),
        in_specs=[SMEM_SPEC] + [VMEM_SPEC] * 4 + [ANY_SPEC] * len(flat),
        out_specs=[VMEM_SPEC] * 6,
        out_shape=[
            jax.ShapeDtypeStruct((rows, hidden), BF),
            jax.ShapeDtypeStruct((rows, width), F32),
            jax.ShapeDtypeStruct((rows, width), BF),
            jax.ShapeDtypeStruct((rows, width), BF),
            jax.ShapeDtypeStruct((1, hidden), F32),
            jax.ShapeDtypeStruct((8, width), F32),
        ],
        scratch_shapes=[
            pltpu.VMEM((width, width), BF),
            pltpu.VMEM((width, hidden), BF),
            pltpu.VMEM((hidden, width), BF),
        ]
        + [pltpu.SemaphoreType.DMA((cut.copies,)) for cut in cuts],
        compiler_params=pltpu.CompilerParams(vmem_limit_bytes=60 * MIB),
        cost_estimate=cost(2 * rows * width * (width + 2 * hidden), 34 * MIB),
    )(place, dm, slope, middle, vectors, *flat)


def weight_grad_kernel(cut, place, left, right, keep, send, whole):
    whole[...] = lax.dot_general(
        left[...], right[...], (((0,), (0,)), ((), ())), preferred_element_type=F32
    )
    for j in range(cut.replicas):
        value = whole[cut.spot(jnp.bitwise_xor(place[0], j))]
        (keep, send)[j & 1][j >> 1, 0] = rnd(value)


def weight_grad(cut, place, left, right):
    tokens, shards = left.shape[0], cut.shards
    shape = (cut.replicas // 2, shards, cut.r, cut.c)
    piece = pl.BlockSpec((cut.replicas // 2, 1, cut.r, cut.c), lambda d, s: (0, d, 0, 0))
    return pl.pallas_call(
        functools.partial(weight_grad_kernel, cut),
        grid_spec=pltpu.PrefetchScalarGridSpec(
            num_scalar_prefetch=1,
            grid=(shards,),
            in_specs=[
                pl.BlockSpec((tokens, cut.rows), lambda d, s: (0, lax.rem(s[1] + shards - d, shards))),
                pl.BlockSpec(right.shape, lambda d, s: (0, 0)),
            ],
            out_specs=[piece] * 2,
            scratch_shapes=[pltpu.VMEM((cut.rows, cut.columns), F32)],
        ),
        out_shape=[jax.ShapeDtypeStruct(shape, BF)] * 2,
        compiler_params=pltpu.CompilerParams(vmem_limit_bytes=56 * MIB),
        cost_estimate=cost(
            2 * tokens * shards * cut.rows * cut.columns, 2 * shards * cut.rows * cut.columns
        ),
    )(place, left, right)


def widen_kernel(cut, place, *refs):
    out = refs[-1]
    for j in range(cut.replicas):
        out[cut.spot(jnp.bitwise_xor(place[0], j))] = refs[j][...].astype(F32)


def widen(cut, place, slots):
    return pl.pallas_call(
        functools.partial(widen_kernel, cut),
        in_specs=[SMEM_SPEC] + [VMEM_SPEC] * cut.replicas,
        out_specs=VMEM_SPEC,
        out_shape=jax.ShapeDtypeStruct((cut.rows, cut.columns), F32),
        compiler_params=pltpu.CompilerParams(vmem_limit_bytes=48 * MIB),
        cost_estimate=cost(0, 6 * cut.rows * cut.columns),
    )(place, *slots)


def hidden_grad_kernel(place, block, dq, dk, dv, weight, out, sums):
    local = dq.shape[1]
    grad = dot_last(dq[...], weight[:, 0:local])
    grad += dot_last(dk[...], weight[:, local : 2 * local])
    grad += dot_last(dv[...], weight[:, 2 * local :])
    out[...] = rnd(grad)
    normal, _ = moments(block[...].astype(F32))
    sums[0:1, :] = jnp.sum(grad * normal, 0, keepdims=True)
    sums[1:2, :] = jnp.sum(grad, 0, keepdims=True)
    sums[2:8, :] = jnp.zeros((6, sums.shape[1]), F32)


def hidden_grad(place, block, dq, dk, dv, weight, distance, shards):
    rows, width = block.shape
    local = dq.shape[1]
    at = lambda i, s: (lax.rem(s[1] + shards - distance, shards), 0)
    here = lambda i, s: (0, 0)
    return pl.pallas_call(
        hidden_grad_kernel,
        grid_spec=pltpu.PrefetchScalarGridSpec(
            num_scalar_prefetch=1,
            grid=(1,),
            in_specs=[pl.BlockSpec((rows, width), here)]
            + [pl.BlockSpec((rows, local), at)] * 3
            + [pl.BlockSpec(weight.shape, here)],
            out_specs=[pl.BlockSpec((rows, width), here), pl.BlockSpec((8, width), here)],
        ),
        out_shape=[jax.ShapeDtypeStruct((rows, width), BF), jax.ShapeDtypeStruct((8, width), F32)],
        compiler_params=pltpu.CompilerParams(vmem_limit_bytes=40 * MIB),
        cost_estimate=cost(6 * rows * width * local, 5 * MIB),
    )(place, block, dq, dk, dv, weight)


def last_kernel(tokens, travel, own, dx2, gain, out):
    normal, scale = moments(tokens[...].astype(F32))
    grad = travel[...].astype(F32) + own[...].astype(F32)
    out[...] = rnd(dx2[...] + norm_grad(grad, gain[...], normal, scale))


def last(tokens, travel, own, dx2, gain):
    return pl.pallas_call(
        last_kernel,
        in_specs=[VMEM_SPEC] * 5,
        out_specs=VMEM_SPEC,
        out_shape=jax.ShapeDtypeStruct(tokens.shape, BF),
        compiler_params=pltpu.CompilerParams(vmem_limit_bytes=40 * MIB),
        cost_estimate=cost(0, 6 * MIB),
    )(tokens, travel, own, dx2, gain)


def swap(value, bit, replicas):
    return lax.ppermute(value, "dp", [(i, i ^ bit) for i in range(replicas)])


def turn(value, shards, step=1):
    return lax.ppermute(value, "fsdp", [(i, (i + step) % shards) for i in range(shards)])


def chip_bits(replicas, reverse):
    bits = [1 << n for n in range(1, replicas.bit_length() - 1)]
    return bits[::-1] if reverse else bits


def share(piece, replicas, reverse=False):
    parts = {0: piece}
    for bit in chip_bits(replicas, reverse):
        parts |= {m | bit: swap(part, bit, replicas) for m, part in list(parts.items())}
    parts |= {m | 1: swap(part, 1, replicas) for m, part in list(parts.items())}
    return [parts[j] for j in range(replicas)]


def add_low(left, right):
    return rnd(left.astype(F32) + right.astype(F32))


def plane_scatter(keep, send, replicas, reverse=False):
    got = swap(send, 1, replicas)
    parts = {2 * m: add_low(keep[m], got[m]) for m in range(replicas // 2)}
    for bit in chip_bits(replicas, reverse):
        there = [m for m in parts if m & bit]
        moved = swap(jnp.stack([parts[m] for m in there]), bit, replicas)
        parts = {m ^ bit: add_low(parts[m ^ bit], moved[n]) for n, m in enumerate(there)}
    return parts[0]


def ring_sum(parts, shards):
    total = parts[1]
    for d in range(2, shards + 1):
        total = add_low(turn(total, shards), parts[d % shards])
    return total


def gather_weight(cut, place, shard, reverse=False):
    piece = cut.of(shard, place[0])
    slots = jnp.stack([turn(piece, cut.shards, d) for d in range(1, cut.shards)])
    return share(slots, cut.replicas, reverse) + [shard]


def reduce_weight(cut, place, keep, send, reverse=False):
    total = ring_sum(plane_scatter(keep, send, cut.replicas, reverse), cut.shards)
    return widen(cut, place, share(total, cut.replicas, reverse))


def flip_by(value, axis, me, replicas):
    shape = value.shape
    bits = replicas.bit_length() - 1
    value = value.reshape(shape[:axis] + (2,) * bits + shape[axis + 1 :])
    for n in range(bits):
        where = axis + bits - 1 - n
        value = jnp.where((me >> n) & 1 == 1, jnp.flip(value, where), value)
    return value.reshape(shape)


def window_low(lengths, group_len):
    prompt = group_len // 2
    order = jnp.arange(lengths.shape[0], dtype=jnp.int32)
    ends = jnp.sum(jnp.where(order[:, None] <= order[None, :], lengths[:, None], 0), 0)
    pos = jnp.arange(prompt, dtype=jnp.int32)
    starts = jnp.max(jnp.where(ends[:, None] <= pos[None, :], ends[:, None], 0), 0)
    return jnp.concatenate([jnp.zeros((prompt,), jnp.int32), prompt + starts])[None]


def body(
    tokens,
    cotangent,
    cont_lengths,
    ln1_gain,
    ln1_bias,
    w_qkv,
    q_bias,
    v_bias,
    w_out,
    out_bias,
    ln2_gain,
    ln2_bias,
    w_up,
    up_bias,
    w_down,
    down_bias,
):
    rows, width = tokens.shape
    shards, replicas = lax.axis_size("fsdp"), lax.axis_size("dp")
    z, me = lax.axis_index("fsdp"), lax.axis_index("dp")
    place = jnp.stack([me, z]).astype(jnp.int32)
    group_len = rows * shards
    head_dim = width // H
    local = width // shards
    hidden = w_up.shape[2]
    w_qkv, w_out, w_up, w_down = w_qkv[0], w_out[0], w_up[0], w_down[0]
    out_parts = 1
    while w_out.shape[0] * out_parts // replicas < 16:
        out_parts *= 2
    cut_out = Cut(w_out.shape[0], width, out_parts, replicas, shards)
    cut_up = Cut(w_up.shape[0], hidden, hidden // width, replicas, shards)
    cut_down = Cut(w_down.shape[0], width, 1, replicas, shards)
    cuts = (cut_out, cut_up, cut_down)

    blocks = {0: tokens}
    for d in range(1, shards // 2 + 1):
        blocks[d] = turn(blocks[d - 1], shards)
        if shards - d not in blocks:
            blocks[shards - d] = turn(blocks[(shards - d + 1) % shards], shards, shards - 1)

    vectors = (ln1_gain, ln1_bias, q_bias, v_bias, out_bias, ln2_gain, ln2_bias, down_bias, up_bias)
    packed = jnp.concatenate(vectors, 1)
    turned = [packed] + [turn(packed, shards, step) for step in range(shards - 1, 0, -1)]
    turned = jnp.concatenate(turned + turned, 0)
    packed_all = lax.dynamic_slice_in_dim(turned, lax.rem(shards - z, shards), shards)
    full = []
    offset = 0
    for vector in vectors:
        size = vector.shape[1]
        full.append(packed_all[:, offset : offset + size].reshape(1, shards * size).astype(F32))
        offset += size
    gain_one, bias_one, _, _, bias_out, gain_two, bias_two, bias_down, bias_up = full
    middle_vectors = jnp.concatenate([bias_out, gain_two, bias_two, bias_down] * 2, 0)
    start_at = z * local
    bias_q = lax.dynamic_slice_in_dim(full[2], start_at, local, 1)
    bias_v = lax.dynamic_slice_in_dim(full[3], start_at, local, 1)
    bias_qkv = jnp.concatenate([bias_q, jnp.zeros_like(bias_q), bias_v], 1)

    slim = w_qkv.shape[0] // replicas
    mine = lax.dynamic_slice_in_dim(w_qkv, me * slim, slim, 0)
    mine = mine.reshape(slim, 3, shards, local).transpose(2, 0, 1, 3).reshape(shards, slim, 3 * local)
    mine = lax.all_to_all(mine, "fsdp", 0, 0, tiled=True)
    weight_qkv = flip_by(jnp.stack(share(mine, replicas)), 0, me, replicas)
    weight_qkv = weight_qkv.transpose(1, 0, 2, 3).reshape(width, 3 * local)

    h_all = jnp.zeros((group_len, width), BF)
    combined = jnp.zeros((group_len, 3 * local), BF)
    for d in [0] + sorted(range(1, shards), key=lambda d: min(d, shards - d)):
        h_all, combined = project(
            place, blocks[d], gain_one, bias_one, weight_qkv, bias_qkv, h_all, combined, d, shards
        )

    lists = [
        gather_weight(cut_out, place, w_out),
        gather_weight(cut_up, place, w_up),
        gather_weight(cut_down, place, w_down, True),
    ]

    low = window_low(cont_lengths[0], group_len)
    mixed, lse = attend(combined, low, head_dim)
    attended = lax.all_to_all(mixed, "fsdp", 0, 1, tiled=True)
    output, hidden_two, middle, acted, slope = feed_forward(
        place, attended, tokens, middle_vectors, bias_up, cuts, lists
    )

    dm = cotangent
    du, dx2, da, do, grad_bias_up, sums = feed_backward(
        place, dm, slope, middle, middle_vectors, cuts, lists
    )
    grad_mixed = lax.all_to_all(do, "fsdp", 1, 0, tiled=True)
    out_w_down = reduce_weight(cut_down, place, *weight_grad(cut_down, place, acted, dm))
    out_w_up = reduce_weight(cut_up, place, *weight_grad(cut_up, place, hidden_two, du), True)
    out_w_out = reduce_weight(cut_out, place, *weight_grad(cut_out, place, attended, da))

    dq, dk, dv = attend_grad(combined, low, mixed, lse, grad_mixed, head_dim)
    first_sums = jnp.zeros((8, width), F32)
    parts = {}
    for d in [*range(1, shards), 0]:
        parts[d], part_sums = hidden_grad(place, blocks[d], dq, dk, dv, weight_qkv, d, shards)
        first_sums += part_sums
    travel = parts[1]
    for d in range(2, shards):
        travel = add_low(turn(travel, shards), parts[d])
    input_grad = last(tokens, turn(travel, shards), parts[0], dx2, gain_one)

    dc = jnp.concatenate([dq, dk, dv], 1)
    grad_bias_qkv = jnp.sum(dc.astype(F32), 0)
    grad_w_qkv = rnd(jnp.einsum("td,te->de", h_all, dc, preferred_element_type=F32))
    rel = grad_w_qkv.reshape(shards, replicas, slim, 3 * local).transpose(1, 0, 2, 3)
    rel = flip_by(rel, 0, me, replicas)
    rel = rel.reshape(replicas // 2, 2, shards, slim, 3 * local)
    piece = plane_scatter(rel[:, 0], rel[:, 1], replicas)
    piece = lax.all_to_all(piece, "fsdp", 0, 0, tiled=True)
    piece = piece.reshape(shards, slim, 3, local).transpose(1, 2, 0, 3).reshape(slim, 3 * width)
    out_w_qkv = flip_by(jnp.stack(share(piece, replicas)), 0, me, replicas)
    out_w_qkv = out_w_qkv.reshape(w_qkv.shape).astype(F32)

    spread = jnp.zeros((width,), F32)
    grad_bias_q = lax.dynamic_update_slice(spread, grad_bias_qkv[:local], (start_at,))
    grad_bias_v = lax.dynamic_update_slice(spread, grad_bias_qkv[2 * local :], (start_at,))
    small = (
        first_sums[0],
        first_sums[1],
        grad_bias_q,
        grad_bias_v,
        sums[3],
        sums[1],
        sums[2],
        sums[0],
        grad_bias_up,
    )
    total = jnp.concatenate([g.reshape(shards, -1) for g in small], 1)
    bit = 1
    while bit < replicas:
        total = total + swap(total, bit, replicas)
        bit *= 2
    bit = 1
    while bit < shards:
        total = total + lax.ppermute(total, "fsdp", [(i, i ^ bit) for i in range(shards)])
        bit *= 2
    total = lax.dynamic_slice_in_dim(total, z, 1)
    outs = []
    offset = 0
    for vector in vectors:
        outs.append(total[:, offset : offset + vector.shape[1]])
        offset += vector.shape[1]
    return (
        output,
        input_grad,
        outs[0],
        outs[1],
        out_w_qkv[None],
        outs[2],
        outs[3],
        out_w_out[None],
        outs[4],
        outs[5],
        outs[6],
        out_w_up[None],
        outs[8],
        out_w_down[None],
        outs[7],
    )


def solution(mesh):
    vec = P(None, "fsdp")
    mat = P(None, "fsdp", None)
    tok = P(("dp", "fsdp"), None)
    in_specs = (tok, tok, P("dp", None), vec, vec, mat, vec, vec, mat, vec, vec, vec, mat, vec, mat, vec)
    out_specs = (tok, tok, vec, vec, mat, vec, vec, mat, vec, vec, vec, mat, vec, mat, vec)
    return jax.shard_map(body, mesh=mesh, in_specs=in_specs, out_specs=out_specs, check_vma=False)
```

```python
import functools

import jax
import jax.numpy as jnp
from jax import lax
from jax.experimental import pallas as pl
from jax.experimental.pallas import tpu as pltpu
from jax.sharding import PartitionSpec as P

H = 16
EPSILON = 1e-05
NEG_LARGE = -1e30
F32 = jnp.float32
BF = jnp.bfloat16
MIB = 2**20
COST_UNIT = 10**8


def rnd(v):
    return v.astype(BF)


def cost(time):
    return pl.CostEstimate(flops=int(time * COST_UNIT), bytes_accessed=1, transcendentals=0)


def dot_last(left, right):
    return lax.dot_general(left, right, (((1,), (1,)), ((), ())), preferred_element_type=F32)


def dot_mm(left, right):
    return jnp.dot(left, right, preferred_element_type=F32)


def key_ranges(start, group_len):
    prompt = group_len // 2
    if start < prompt:
        return start, start
    return prompt, max(prompt, start - group_len // 8)


def allowed_mask(shape, key_start, query_start, low_row):
    key_pos = lax.broadcasted_iota(jnp.int32, shape, 0) + key_start
    query_pos = lax.broadcasted_iota(jnp.int32, shape, 1) + query_start
    return (key_pos <= query_pos) & (key_pos >= low_row)


def attend_kernel(group_len, head_dim, q_ref, k_ref, v_ref, low_ref, o_ref, lse_ref):
    size = min(512, group_len // 4)
    scale = jnp.asarray(head_dim**-0.5, BF)
    values_t = v_ref[...].astype(F32).T.astype(BF)
    for start in range(0, group_len, size):
        stop = start + size
        full, near = key_ranges(start, group_len)
        results = []
        for head in range(128 // head_dim):
            lanes = slice(head * head_dim, (head + 1) * head_dim)
            queries = q_ref[start:stop, lanes] * scale
            part = dot_last(k_ref[near:stop, lanes], queries)
            ok = allowed_mask(part.shape, near, start, low_ref[0:1, start:stop])
            part = jnp.where(ok, part, NEG_LARGE)
            top = jnp.max(part, 0, keepdims=True)
            if full:
                rest = dot_last(k_ref[0:full, lanes], queries)
                top = jnp.maximum(top, jnp.max(rest, 0, keepdims=True))
            part = jnp.exp(part - top)
            total = jnp.sum(part, 0, keepdims=True)
            mixed = dot_mm(values_t[lanes, near:stop], part.astype(BF))
            if full:
                rest = jnp.exp(rest - top)
                total += jnp.sum(rest, 0, keepdims=True)
                mixed += dot_mm(values_t[lanes, 0:full], rest.astype(BF))
            results.append(mixed * (1.0 / total))
            lse_ref[0, head : head + 1, start:stop] = top + jnp.log(total)
        o_ref[start:stop, :] = jnp.concatenate(results, 0).T.astype(BF)


def attend_grad_kernel(
    group_len, head_dim, q_ref, k_ref, v_ref, low_ref, o_ref, lse_ref, do_ref, *refs
):
    dq_ref, dk_ref, dv_ref, bias_ref, dk_sum, dv_sum = refs[-6:]
    bias = jnp.zeros((1, 128), F32)
    size = min(256, group_len // 8)
    scale = jnp.asarray(head_dim**-0.5, BF)
    keys_t = k_ref[...].astype(F32).T.astype(BF)
    dk_sum[...] = jnp.zeros_like(dk_sum)
    dv_sum[...] = jnp.zeros_like(dv_sum)
    for start in range(0, group_len, size):
        stop = start + size
        full, near = key_ranges(start, group_len)
        product_t = (do_ref[start:stop, :].astype(F32) * o_ref[start:stop, :].astype(F32)).T
        results = []
        for head in range(128 // head_dim):
            lanes = slice(head * head_dim, (head + 1) * head_dim)
            queries = q_ref[start:stop, lanes] * scale
            grads = do_ref[start:stop, lanes]
            delta = jnp.sum(product_t[lanes, :], 0, keepdims=True)
            lse = lse_ref[0, head : head + 1, start:stop]
            dq_t = jnp.zeros((head_dim, size), F32)
            for first, last, masked in ((near, stop, True), (0, full, False)):
                if first == last:
                    continue
                probs = jnp.exp(dot_last(k_ref[first:last, lanes], queries) - lse)
                if masked:
                    ok = allowed_mask(probs.shape, first, start, low_ref[0:1, start:stop])
                    probs = jnp.where(ok, probs, 0.0)
                grad_probs = dot_last(v_ref[first:last, lanes], grads)
                ds = (probs * (grad_probs - delta)).astype(BF)
                dv_sum[head, first:last, :] += dot_mm(probs.astype(BF), grads)
                dk_sum[head, first:last, :] += dot_mm(ds, queries)
                dq_t += dot_mm(keys_t[lanes, first:last], ds)
            results.append(dq_t * head_dim**-0.5)
        dq = jnp.concatenate(results, 0).T.astype(BF)
        dq_ref[start:stop, :] = dq
        bias += jnp.sum(dq.astype(F32), 0, keepdims=True)
    heads = range(128 // head_dim)
    dk_ref[...] = jnp.concatenate([dk_sum[head] for head in heads], 1).astype(BF)
    dv = jnp.concatenate([dv_sum[head] for head in heads], 1).astype(BF)
    dv_ref[...] = dv
    bias_ref[0, 0:1, :] = bias
    bias_ref[0, 1:2, :] = jnp.sum(dv.astype(F32), 0, keepdims=True)


def attend(combined, low, head_dim):
    group_len, width = combined.shape[0], combined.shape[1] // 3
    steps = width // 128
    heads = 128 // head_dim
    block = lambda offset: pl.BlockSpec((group_len, 128), lambda i: (0, offset + i))
    return pl.pallas_call(
        functools.partial(attend_kernel, group_len, head_dim),
        grid=(steps,),
        in_specs=[block(0), block(steps), block(2 * steps), pl.BlockSpec((1, group_len), lambda i: (0, 0))],
        out_specs=[block(0), pl.BlockSpec((1, heads, group_len), lambda i: (i, 0, 0))],
        out_shape=[
            jax.ShapeDtypeStruct((group_len, width), BF),
            jax.ShapeDtypeStruct((steps, heads, group_len), F32),
        ],
        compiler_params=pltpu.CompilerParams(vmem_limit_bytes=56 * MIB),
        cost_estimate=cost(18),
    )(combined, combined, combined, low)


def attend_grad(combined, low, mixed, lse, grad_mixed, head_dim, after=()):
    group_len, width = mixed.shape
    steps = width // 128
    heads = 128 // head_dim
    block = lambda offset: pl.BlockSpec((group_len, 128), lambda i: (0, offset + i))
    return pl.pallas_call(
        functools.partial(attend_grad_kernel, group_len, head_dim),
        grid=(steps,),
        in_specs=[
            block(0),
            block(steps),
            block(2 * steps),
            pl.BlockSpec((1, group_len), lambda i: (0, 0)),
            block(0),
            pl.BlockSpec((1, heads, group_len), lambda i: (i, 0, 0)),
            block(0),
        ]
        + [pl.BlockSpec(memory_space=pl.ANY)] * len(after),
        out_specs=[block(0)] * 3 + [pl.BlockSpec((1, 2, 128), lambda i: (i, 0, 0))],
        out_shape=[jax.ShapeDtypeStruct((group_len, width), BF)] * 3
        + [jax.ShapeDtypeStruct((steps, 2, 128), F32)],
        scratch_shapes=[pltpu.VMEM((heads, group_len, head_dim), F32)] * 2,
        compiler_params=pltpu.CompilerParams(vmem_limit_bytes=56 * MIB),
        cost_estimate=cost(28),
    )(combined, combined, combined, low, mixed, lse, grad_mixed, *after)


class Cut:
    def __init__(self, rows, columns, column_parts, replicas, shards):
        self.rows, self.columns, self.shards, self.replicas = rows, columns, shards, replicas
        self.nc, self.nr = column_parts, replicas // column_parts
        self.r, self.c = rows // self.nr, columns // self.nc

    def place(self, piece):
        half = self.nr // 2
        row = (lax.rem(piece, 2) * half + lax.rem(lax.div(piece, 2), half)) * self.r
        column = lax.div(piece, self.nr) * self.c
        return pl.multiple_of(row, 8 if self.r % 16 else 16), pl.multiple_of(column, 128)

    def spot(self, piece, base=0):
        row, column = self.place(piece)
        return pl.ds(base + row, self.r), pl.ds(column, self.c)

    def of(self, shard, piece):
        return lax.dynamic_slice(shard, self.place(piece), (self.r, self.c))

    @property
    def copies(self):
        return 1 + (self.shards - 1) * self.replicas


def fetch(cut, me, z, slots, first_row, shard, whole, sems):
    base = pl.multiple_of(z * cut.rows, 16)
    copies = [pltpu.make_async_copy(shard, whole.at[pl.ds(base, cut.rows), :], sems.at[0])]
    for d in range(1, cut.shards):
        base = pl.multiple_of(lax.rem(z + cut.shards - d, cut.shards) * cut.rows, 16)
        for j in range(cut.replicas):
            copies.append(
                pltpu.make_async_copy(
                    slots[j].at[d - 1, pl.ds(first_row, cut.r), :],
                    whole.at[cut.spot(jnp.bitwise_xor(me, j), base)],
                    sems.at[len(copies)],
                )
            )
    return copies


def loads_of(cuts, place, lists, wholes, sems):
    count = cuts[0].replicas
    both, down, shards = lists[:count], lists[count : 2 * count], lists[2 * count :]
    sources = ((both, 0), (both, cuts[0].r), (down, 0))
    return [
        fetch(cut, place[0], place[1], slots, row, shard, whole, sem)
        for cut, (slots, row), shard, whole, sem in zip(cuts, sources, shards, wholes, sems)
    ]


def start(copies):
    for copy in copies:
        copy.start()


def finish(copies):
    for copy in copies:
        copy.wait()


MARK = jax.ShapeDtypeStruct((8, 128), F32)
SMEM_SPEC = pl.BlockSpec(memory_space=pltpu.SMEM)
ANY_SPEC = pl.BlockSpec(memory_space=pl.ANY)
VMEM_SPEC = pl.BlockSpec(memory_space=pltpu.VMEM)


def moments(stream):
    mean = jnp.mean(stream, -1, keepdims=True)
    centered = stream - mean
    scale = lax.rsqrt(jnp.mean(centered * centered, -1, keepdims=True) + EPSILON)
    return centered * scale, scale


def norm_grad(grad_hidden, gain, normal, scale):
    t = grad_hidden * gain
    return scale * (
        t - jnp.mean(t, -1, keepdims=True) - normal * jnp.mean(t * normal, -1, keepdims=True)
    )


def project_kernel(place, block, gain, bias, weight, bias_qkv, c_in, h_out, c_out, mark):
    mark[...] = jnp.zeros_like(mark)
    normal, _ = moments(block[...].astype(F32))
    hidden = rnd(normal * gain[...] + bias[...])
    h_out[...] = hidden
    c_out[...] = rnd(dot_mm(hidden, weight[...]) + bias_qkv[...])


def project(place, block, gain, bias, weight, bias_qkv, c_all, distance, shards):
    rows, width = block.shape
    whole = lambda a: pl.BlockSpec(a.shape, lambda i, s: (0,) * a.ndim)
    at = lambda i, s: (lax.rem(s[1] + shards - distance, shards), 0)
    return pl.pallas_call(
        project_kernel,
        grid_spec=pltpu.PrefetchScalarGridSpec(
            num_scalar_prefetch=1,
            grid=(1,),
            in_specs=[whole(a) for a in (block, gain, bias, weight, bias_qkv)] + [ANY_SPEC],
            out_specs=[
                pl.BlockSpec((rows, width), lambda i, s: (0, 0)),
                pl.BlockSpec((rows, c_all.shape[1]), at),
                pl.BlockSpec((8, 128), lambda i, s: (0, 0)),
            ],
        ),
        out_shape=[jax.ShapeDtypeStruct(a.shape, BF) for a in (block, c_all)] + [MARK],
        input_output_aliases={6: 1},
        compiler_params=pltpu.CompilerParams(vmem_limit_bytes=40 * MIB),
        cost_estimate=cost(2.5),
    )(place, block, gain, bias, weight, bias_qkv, c_all)


GELU_A = 0.7978845608028654
GELU_B = 0.044715


def gelu_both(u):
    square = u * u
    t = jnp.tanh(GELU_A * u * (1.0 + GELU_B * square))
    value = 0.5 * u * (1.0 + t)
    slope = 0.5 * (1.0 + t) + 0.5 * u * (1.0 - t * t) * (GELU_A * (1.0 + 3.0 * GELU_B * square))
    return value, slope


def forward_kernel(cuts, step, place, tokens, vectors, bias_up, *refs):
    shards = cuts[0].shards
    mixed, refs = refs[:shards], refs[shards:]
    count = 2 * cuts[0].replicas + 3
    lists, refs = refs[:count], refs[count:]
    out, hidden, middle, acted, slope, w_out, w_up, w_down, *sems = refs
    loads = loads_of(cuts, place, lists, (w_out, w_up, w_down), sems)
    for copies in loads:
        start(copies)
    finish(loads[0])
    stream = tokens[...].astype(F32) + vectors[0:1, :]
    local = mixed[0].shape[1]
    for d in range(shards):
        at = pl.multiple_of(lax.rem(place[1] + shards - d, shards) * local, 16)
        stream += dot_mm(mixed[d][...], w_out[pl.ds(at, local), :])
    middle[...] = stream
    normal, _ = moments(stream)
    hidden[...] = rnd(normal * vectors[1:2, :] + vectors[2:3, :])
    finish(loads[1])
    finish(loads[2])
    total = vectors[3:4, :] + stream
    for block in range(0, w_up.shape[1], step):
        columns = slice(block, block + step)
        u = dot_mm(hidden[...], w_up[:, columns]) + bias_up[:, columns]
        value, grad = gelu_both(u)
        value = rnd(value)
        acted[:, columns] = value
        slope[:, columns] = rnd(grad)
        total += dot_mm(value, w_down[columns, :])
    out[...] = rnd(total)


def feed_forward(place, mixed, tokens, vectors, bias_up, cuts, lists):
    rows, width = tokens.shape
    hidden = bias_up.shape[1]
    return pl.pallas_call(
        functools.partial(forward_kernel, cuts, min(1024, hidden)),
        in_specs=[SMEM_SPEC] + [VMEM_SPEC] * (3 + len(mixed)) + [ANY_SPEC] * len(lists),
        out_specs=[VMEM_SPEC] * 5,
        out_shape=[
            jax.ShapeDtypeStruct((rows, width), BF),
            jax.ShapeDtypeStruct((rows, width), BF),
            jax.ShapeDtypeStruct((rows, width), F32),
            jax.ShapeDtypeStruct((rows, hidden), BF),
            jax.ShapeDtypeStruct((rows, hidden), BF),
        ],
        scratch_shapes=[
            pltpu.VMEM((width, width), BF),
            pltpu.VMEM((width, hidden), BF),
            pltpu.VMEM((hidden, width), BF),
        ]
        + [pltpu.SemaphoreType.DMA((cut.copies,)) for cut in cuts],
        compiler_params=pltpu.CompilerParams(vmem_limit_bytes=60 * MIB),
        cost_estimate=cost(24),
    )(place, tokens, vectors, bias_up, *mixed, *lists)


def backward_kernel(cuts, step, place, dm, slope, middle, vectors, *refs):
    count = 2 * cuts[0].replicas + 3
    lists, refs = refs[:count], refs[count:]
    du, dx2, da, do, grad_up, sums, w_out, w_up, w_down, *sems = refs
    loads = loads_of(cuts, place, lists, (w_out, w_up, w_down), sems)[::-1]
    for copies in loads:
        start(copies)
    finish(loads[0])
    finish(loads[1])
    dh2 = jnp.zeros(middle.shape, F32)
    for block in range(0, w_up.shape[1], step):
        columns = slice(block, block + step)
        part = rnd(dot_last(dm[...], w_down[columns, :]) * slope[:, columns].astype(F32))
        du[:, columns] = part
        grad_up[:, columns] = jnp.sum(part.astype(F32), 0, keepdims=True)
        dh2 += dot_last(part, w_up[:, columns])
    normal, scale = moments(middle[...])
    incoming = dm[...].astype(F32)
    stream = incoming + norm_grad(dh2, vectors[1:2, :], normal, scale)
    dx2[...] = stream
    low = rnd(stream)
    da[...] = low
    finish(loads[2])
    do[...] = rnd(dot_last(low, w_out[...]))
    sums[0:1, :] = jnp.sum(incoming, 0, keepdims=True)
    sums[1:2, :] = jnp.sum(dh2 * normal, 0, keepdims=True)
    sums[2:3, :] = jnp.sum(dh2, 0, keepdims=True)
    sums[3:4, :] = jnp.sum(low.astype(F32), 0, keepdims=True)
    sums[4:8, :] = jnp.zeros((4, sums.shape[1]), F32)


def feed_backward(place, dm, slope, middle, vectors, cuts, lists):
    rows, width = dm.shape
    hidden = slope.shape[1]
    return pl.pallas_call(
        functools.partial(backward_kernel, cuts, min(1024, hidden)),
        in_specs=[SMEM_SPEC] + [VMEM_SPEC] * 4 + [ANY_SPEC] * len(lists),
        out_specs=[VMEM_SPEC] * 6,
        out_shape=[
            jax.ShapeDtypeStruct((rows, hidden), BF),
            jax.ShapeDtypeStruct((rows, width), F32),
            jax.ShapeDtypeStruct((rows, width), BF),
            jax.ShapeDtypeStruct((rows, width), BF),
            jax.ShapeDtypeStruct((1, hidden), F32),
            jax.ShapeDtypeStruct((8, width), F32),
        ],
        scratch_shapes=[
            pltpu.VMEM((width, width), BF),
            pltpu.VMEM((width, hidden), BF),
            pltpu.VMEM((hidden, width), BF),
        ]
        + [pltpu.SemaphoreType.DMA((cut.copies,)) for cut in cuts],
        compiler_params=pltpu.CompilerParams(vmem_limit_bytes=60 * MIB),
        cost_estimate=cost(24),
    )(place, dm, slope, middle, vectors, *lists)


def weight_grad_kernel(cut, place, left, right, *refs):
    keep, send, mark, whole = refs[-4:]
    mark[...] = jnp.zeros_like(mark)
    whole[...] = lax.dot_general(
        left[...], right[...], (((0,), (0,)), ((), ())), preferred_element_type=F32
    )
    for j in range(cut.replicas):
        value = whole[cut.spot(jnp.bitwise_xor(place[0], j))]
        (keep, send)[j & 1][j >> 1, 0] = rnd(value)


def weight_grad(cut, place, left, right, after=()):
    tokens, shards = left.shape[0], cut.shards
    shape = (cut.replicas // 2, shards, cut.r, cut.c)
    piece = pl.BlockSpec((cut.replicas // 2, 1, cut.r, cut.c), lambda d, s: (0, d, 0, 0))
    return pl.pallas_call(
        functools.partial(weight_grad_kernel, cut),
        grid_spec=pltpu.PrefetchScalarGridSpec(
            num_scalar_prefetch=1,
            grid=(shards,),
            in_specs=[
                pl.BlockSpec((tokens, cut.rows), lambda d, s: (0, lax.rem(s[1] + shards - d, shards))),
                pl.BlockSpec(right.shape, lambda d, s: (0, 0)),
            ]
            + [ANY_SPEC] * len(after),
            out_specs=[piece] * 2 + [pl.BlockSpec((8, 128), lambda d, s: (0, 0))],
            scratch_shapes=[pltpu.VMEM((cut.rows, cut.columns), F32)],
        ),
        out_shape=[jax.ShapeDtypeStruct(shape, BF)] * 2 + [MARK],
        compiler_params=pltpu.CompilerParams(vmem_limit_bytes=56 * MIB),
        cost_estimate=cost(10),
    )(place, left, right, *after)


def gather_rows(cut, place, other, lefts, rows):
    size = cut.rows // 2
    half = lax.rem(place[0] + other, 2) * size
    for d in range(cut.shards):
        if len(lefts) > 1:
            part = lefts[d][:, pl.ds(pl.multiple_of(half, 128), size)]
        else:
            column = lax.rem(place[1] + cut.shards - d, cut.shards) * cut.rows + half
            part = lefts[0][:, pl.ds(pl.multiple_of(column, 128), size)]
        rows[:, d * size : (d + 1) * size] = part


def wide_kernel(cut, other, reverse, count, place, right, *refs):
    lefts, refs = refs[:count], refs[count:]
    rows, turned, whole = refs[-3:]
    refs = refs[:-1]
    refs[-3][...] = jnp.zeros_like(refs[-3])
    step = pl.program_id(0)

    @pl.when(step == 0)
    def _():
        gather_rows(cut, place, other, lefts, rows)
        turned[...] = rows[...].astype(F32).T.astype(BF)

    whole[...] = dot_mm(turned[...], right[...])
    half, size = cut.nr // 2, cut.rows // 2
    chip = lax.rem(lax.div(place[0], 2), half)

    def part(n, d):
        row = jnp.bitwise_xor(chip, n) * cut.r + d * size
        return whole[pl.ds(pl.multiple_of(row, 16), cut.r), :]

    for d in range(cut.shards):
        for n in range(half):
            if other:
                refs[-4][n, d] = rnd(part(n, d))
                continue
            got, (stay, go) = refs[0], refs[-5:-3]
            value = rnd(part(n, d) + got[n, d].astype(F32))
            if cut.nc == 1:
                leaves, m = (n >= half // 2, n % (half // 2)) if reverse else (n % 2 == 1, n // 2)
                (go if leaves else stay)[m, d] = value
            else:

                @pl.when(step < cut.nc // 2)
                def _():
                    stay[n, d] = value

                @pl.when(step >= cut.nc // 2)
                def _():
                    go[n, d] = value


def wide_grad(cut, place, left, right, other, got, reverse, after):
    lefts = left if isinstance(left, list) else [left]
    tokens, half, count = right.shape[0], cut.nr // 2, cut.nc // 2
    block = (half, cut.shards, cut.r, cut.c)
    here = lambda i, s: (i, 0, 0, 0)
    if other:
        specs, sizes = [pl.BlockSpec(block, here)], [cut.replicas // 2]
    elif cut.nc == 1:
        specs, sizes = [pl.BlockSpec((half // 2,) + block[1:], here)] * 2, [cut.replicas // 4] * 2
    else:
        specs = [
            pl.BlockSpec(block, lambda i, s: (jnp.minimum(i, count - 1), 0, 0, 0)),
            pl.BlockSpec(block, lambda i, s: (jnp.maximum(i - count, 0), 0, 0, 0)),
        ]
        sizes = [cut.replicas // 4] * 2
    return pl.pallas_call(
        functools.partial(wide_kernel, cut, other, reverse, len(lefts)),
        grid_spec=pltpu.PrefetchScalarGridSpec(
            num_scalar_prefetch=1,
            grid=(cut.nc,),
            in_specs=[
                pl.BlockSpec(
                    (tokens, cut.c), lambda i, s: (0, jnp.bitwise_xor(lax.div(s[0], 2 * half), i))
                ),
            ]
            + [pl.BlockSpec(a.shape, lambda i, s: (0, 0)) for a in lefts]
            + [pl.BlockSpec(block, here)] * len(got)
            + [ANY_SPEC] * len(after),
            out_specs=specs + [pl.BlockSpec((8, 128), lambda i, s: (0, 0))],
            scratch_shapes=[
                pltpu.VMEM((tokens, cut.shards * cut.rows // 2), BF),
                pltpu.VMEM((cut.shards * cut.rows // 2, tokens), BF),
                pltpu.VMEM((cut.shards * cut.rows // 2, cut.c), F32),
            ],
        ),
        out_shape=[jax.ShapeDtypeStruct((n, cut.shards, cut.r, cut.c), BF) for n in sizes] + [MARK],
        compiler_params=pltpu.CompilerParams(vmem_limit_bytes=56 * MIB),
        cost_estimate=cost(6),
    )(place, right, *lefts, *got, *after)


def half_spots(cut, me):
    half = cut.nr // 2
    for m in range(cut.replicas // 2):
        chip = jnp.bitwise_xor(lax.div(me, 2), m)
        row = pl.multiple_of(lax.rem(chip, half) * cut.r, 8 if cut.r % 16 else 16)
        column = pl.multiple_of(lax.div(chip, half) * cut.c, 128)
        yield m, (pl.ds(row, cut.r), pl.ds(column, cut.c))


def send_grad_kernel(cut, place, left, right, *refs):
    send, mark, whole = refs[-3:]
    mark[...] = jnp.zeros_like(mark)
    whole[...] = lax.dot_general(
        left[...], right[...], (((0,), (0,)), ((), ())), preferred_element_type=F32
    )
    for m, spot in half_spots(cut, place[0]):
        send[m, 0] = rnd(whole[spot])


def keep_grad_kernel(cut, reverse, place, left, right, got, *refs):
    stay, go, mark, whole = refs[-4:]
    mark[...] = jnp.zeros_like(mark)
    whole[...] = lax.dot_general(
        left[...], right[...], (((0,), (0,)), ((), ())), preferred_element_type=F32
    )
    count = cut.replicas // 4
    for m, spot in half_spots(cut, place[0]):
        leaves, n = (m >= count, m % count) if reverse else (m % 2 == 1, m // 2)
        (go if leaves else stay)[n, 0] = rnd(whole[spot] + got[m, 0].astype(F32))


def half_grad(kernel, cut, place, left, right, other, slots, results, after):
    tokens, shards = left.shape[0], cut.shards
    pick = lambda d, s: (
        0,
        lax.rem(s[1] + shards - d, shards) * 2 + lax.rem(s[0] + other, 2),
    )
    piece = lambda count: pl.BlockSpec((count, 1, cut.r, cut.c), lambda d, s: (0, d, 0, 0))
    return pl.pallas_call(
        kernel,
        grid_spec=pltpu.PrefetchScalarGridSpec(
            num_scalar_prefetch=1,
            grid=(shards,),
            in_specs=[
                pl.BlockSpec((tokens, cut.rows // 2), pick),
                pl.BlockSpec(right.shape, lambda d, s: (0, 0)),
            ]
            + [piece(a.shape[0]) for a in slots]
            + [ANY_SPEC] * len(after),
            out_specs=[piece(n) for n in results] + [pl.BlockSpec((8, 128), lambda d, s: (0, 0))],
            scratch_shapes=[pltpu.VMEM((cut.rows // 2, cut.columns), F32)],
        ),
        out_shape=[jax.ShapeDtypeStruct((n, shards, cut.r, cut.c), BF) for n in results] + [MARK],
        compiler_params=pltpu.CompilerParams(vmem_limit_bytes=56 * MIB),
        cost_estimate=cost(7.5),
    )(place, left, right, *slots, *after)


def send_grad(cut, place, left, right, after=()):
    if cut.rows <= 256:
        return wide_grad(cut, place, left, right, 1, (), False, after)
    kernel = functools.partial(send_grad_kernel, cut)
    return half_grad(kernel, cut, place, left, right, 1, (), (cut.replicas // 2,), after)


def keep_grad(cut, place, left, right, got, reverse, after=()):
    if cut.rows <= 256:
        return wide_grad(cut, place, left, right, 0, (got,), reverse, after)
    kernel = functools.partial(keep_grad_kernel, cut, reverse)
    return half_grad(kernel, cut, place, left, right, 0, (got,), (cut.replicas // 4,) * 2, after)


def qkv_grad_kernel(slim, replicas, shards, place, dq, dk, dv, small, *refs):
    keep, send, mark, whole = refs[-4:]
    blocks = refs[:shards]
    rows = blocks[0].shape[0]
    mark[...] = jnp.zeros_like(mark)
    local = dq.shape[1]
    for n, right in enumerate((dq, dk, dv)):
        total = jnp.zeros((whole.shape[0], local), F32)
        for d in range(shards):
            at = pl.ds(pl.multiple_of(lax.rem(place[1] + shards - d, shards) * rows, 16), rows)
            total += lax.dot_general(
                blocks[d][...], right[at, :], (((0,), (0,)), ((), ())), preferred_element_type=F32
            )
        whole[:, n * local : (n + 1) * local] = total
    first = lax.broadcasted_iota(jnp.int32, (16, 3 * local), 0) == 0
    for j in range(replicas):
        piece = jnp.bitwise_xor(place[0], j)
        out = (keep, send)[j & 1]
        out[j >> 1, 0, 0:slim] = rnd(whole[pl.ds(pl.multiple_of(piece * slim, 8), slim), :])
        out[j >> 1, 0, slim:] = rnd(jnp.where(first, small[0, pl.ds(piece, 1), :], 0.0))


def qkv_grad(place, hiddens, dq, dk, dv, small, slim, shards, after):
    replicas, (tokens, local) = small.shape[1], dq.shape
    rows, width = slim * replicas, 3 * local
    here = pl.BlockSpec((tokens, local), lambda f, s: (0, 0))
    piece = pl.BlockSpec((replicas // 2, 1, slim + 16, width), lambda f, s: (0, f, 0, 0))
    return pl.pallas_call(
        functools.partial(qkv_grad_kernel, slim, replicas, shards),
        grid_spec=pltpu.PrefetchScalarGridSpec(
            num_scalar_prefetch=1,
            grid=(shards,),
            in_specs=[here, here, here]
            + [pl.BlockSpec((1, replicas, width), lambda f, s: (f, 0, 0))]
            + [pl.BlockSpec((tokens // shards, rows), lambda f, s: (0, f))] * shards
            + [ANY_SPEC] * len(after),
            out_specs=[piece] * 2 + [pl.BlockSpec((8, 128), lambda f, s: (0, 0))],
            scratch_shapes=[pltpu.VMEM((rows, width), F32)],
        ),
        out_shape=[jax.ShapeDtypeStruct((replicas // 2, shards, slim + 16, width), BF)] * 2 + [MARK],
        compiler_params=pltpu.CompilerParams(vmem_limit_bytes=48 * MIB),
        cost_estimate=cost(6.5),
    )(place, dq, dk, dv, small, *hiddens, *after)


def widen_kernel(cuts, qkv_rows, place, own_a, other_a, own_b, other_b, w_out, w_up, w_down, w_qkv, small):
    cut_out, cut_up, cut_down = cuts
    width = own_a.shape[2]
    for j in range(cut_out.replicas):
        piece = jnp.bitwise_xor(place[0], j)
        left, right, m = (own_a, own_b, j >> 1) if j % 2 == 0 else (other_a, other_b, j >> 1)
        row = cut_out.r
        w_out[cut_out.spot(piece)] = left[m, 0:row].astype(F32)
        w_up[cut_up.spot(piece)] = left[m, row : row + cut_up.r].astype(F32)
        row += cut_up.r
        spot = pl.ds(pl.multiple_of(piece * 8, 8), 8)
        small[spot, :] = left[m, row : row + 8].astype(F32)
        row = cut_down.r
        w_down[cut_down.spot(piece)] = right[m, 0:row].astype(F32)
        spot = pl.ds(pl.multiple_of(piece * qkv_rows, 8), qkv_rows)
        shards, local = cut_out.shards, width // cut_out.shards
        for k in range(3):
            for d in range(shards):
                column = k * width + lax.rem(place[1] + shards - d, shards) * local
                part = right[m, row : row + qkv_rows, d * local : (d + 1) * local].astype(F32)
                w_qkv[spot, pl.ds(pl.multiple_of(column, 128), local)] = part
            row += qkv_rows


def widen(cuts, qkv_rows, place, own_a, other_a, own_b, other_b):
    width = own_a.shape[2]
    shapes = [(cut.rows, cut.columns) for cut in cuts]
    shapes += [(qkv_rows * cuts[0].replicas, 3 * width), (8 * cuts[0].replicas, width)]
    return pl.pallas_call(
        functools.partial(widen_kernel, cuts, qkv_rows),
        in_specs=[SMEM_SPEC] + [VMEM_SPEC] * 4,
        out_specs=[VMEM_SPEC] * 5,
        out_shape=[jax.ShapeDtypeStruct(shape, F32) for shape in shapes],
        compiler_params=pltpu.CompilerParams(vmem_limit_bytes=48 * MIB),
        cost_estimate=cost(7),
    )(place, own_a, other_a, own_b, other_b)


def hidden_grad_kernel(place, block, dq, dk, dv, weight, *refs):
    out, sums = refs[-2:]
    local = dq.shape[1]
    grad = dot_last(dq[...], weight[:, 0:local])
    grad += dot_last(dk[...], weight[:, local : 2 * local])
    grad += dot_last(dv[...], weight[:, 2 * local :])
    out[...] = rnd(grad)
    normal, _ = moments(block[...].astype(F32))
    sums[0:1, :] = jnp.sum(grad * normal, 0, keepdims=True)
    sums[1:2, :] = jnp.sum(grad, 0, keepdims=True)
    sums[2:8, :] = jnp.zeros((6, sums.shape[1]), F32)


def hidden_grad(place, block, dq, dk, dv, weight, distance, shards, after=()):
    rows, width = block.shape
    local = dq.shape[1]
    at = lambda i, s: (lax.rem(s[1] + shards - distance, shards), 0)
    here = lambda i, s: (0, 0)
    return pl.pallas_call(
        hidden_grad_kernel,
        grid_spec=pltpu.PrefetchScalarGridSpec(
            num_scalar_prefetch=1,
            grid=(1,),
            in_specs=[pl.BlockSpec((rows, width), here)]
            + [pl.BlockSpec((rows, local), at)] * 3
            + [pl.BlockSpec(weight.shape, here)]
            + [ANY_SPEC] * len(after),
            out_specs=[pl.BlockSpec((rows, width), here), pl.BlockSpec((8, width), here)],
        ),
        out_shape=[jax.ShapeDtypeStruct((rows, width), BF), jax.ShapeDtypeStruct((8, width), F32)],
        compiler_params=pltpu.CompilerParams(vmem_limit_bytes=40 * MIB),
        cost_estimate=cost(3),
    )(place, block, dq, dk, dv, weight, *after)


def last_kernel(tokens, travel, own, dx2, gain, out, mark):
    mark[...] = jnp.zeros_like(mark)
    normal, scale = moments(tokens[...].astype(F32))
    grad = travel[...].astype(F32) + own[...].astype(F32)
    out[...] = rnd(dx2[...] + norm_grad(grad, gain[...], normal, scale))


def last(tokens, travel, own, dx2, gain):
    return pl.pallas_call(
        last_kernel,
        in_specs=[VMEM_SPEC] * 5,
        out_specs=[VMEM_SPEC] * 2,
        out_shape=[jax.ShapeDtypeStruct(tokens.shape, BF), MARK],
        compiler_params=pltpu.CompilerParams(vmem_limit_bytes=40 * MIB),
        cost_estimate=cost(2.5),
    )(tokens, travel, own, dx2, gain)


def swap(value, bit, replicas):
    return lax.ppermute(value, "dp", [(i, i ^ bit) for i in range(replicas)])


def around(value, shards):
    blocks = {0: value}
    for d in range(1, shards // 2 + 1):
        blocks[d] = turn(blocks[d - 1], shards)
        if shards - d not in blocks:
            blocks[shards - d] = turn(blocks[(shards - d + 1) % shards], shards, shards - 1)
    return blocks


def turn(value, shards, step=1):
    return lax.ppermute(value, "fsdp", [(i, (i + step) % shards) for i in range(shards)])


def chip_bits(replicas, reverse):
    bits = [1 << n for n in range(1, replicas.bit_length() - 1)]
    return bits[::-1] if reverse else bits


def share_chips(piece, replicas, reverse=False, pause=lambda part: part):
    parts = {0: piece}
    for n, bit in enumerate(chip_bits(replicas, reverse)):
        more = {m | bit: swap(part, bit, replicas) for m, part in parts.items()}
        parts |= {m: part if n else pause(part) for m, part in more.items()}
    return [parts[2 * m] for m in range(replicas // 2)]


def share(piece, replicas, reverse=False, pause=lambda part: part):
    slots = []
    for part in share_chips(piece, replicas, reverse, pause):
        slots += [part, swap(part, 1, replicas)]
    return slots


def idle_kernel(*refs):
    pass


def gate(value, *after):
    return pl.pallas_call(
        idle_kernel,
        in_specs=[ANY_SPEC] * (1 + len(after)),
        out_specs=ANY_SPEC,
        out_shape=jax.ShapeDtypeStruct(value.shape, value.dtype),
        input_output_aliases={0: 0},
        cost_estimate=cost(0),
    )(value, *after)


def add_low(left, right):
    return rnd(left.astype(F32) + right.astype(F32))


def fold_kernel(left_stay, right_stay, left_go, right_go, *refs):
    stay, go, mark = refs[-3:]
    stay[...] = add_low(left_stay[...], right_stay[...])
    go[...] = add_low(left_go[...], right_go[...])
    mark[...] = jnp.zeros_like(mark)


def fold(left, right, reverse, after=()):
    n, shards, r, c = left.shape
    deep = shards if r * c < 2**16 else 1
    stay = lambda i, d: (i if reverse else 2 * i, d, 0, 0)
    go = lambda i, d: (i + n // 2 if reverse else 2 * i + 1, d, 0, 0)
    block = (1, deep, r, c)
    return pl.pallas_call(
        fold_kernel,
        grid=(n // 2, shards // deep),
        in_specs=[pl.BlockSpec(block, stay)] * 2 + [pl.BlockSpec(block, go)] * 2 + [ANY_SPEC] * len(after),
        out_specs=[pl.BlockSpec(block, lambda i, d: (i, d, 0, 0))] * 2
        + [pl.BlockSpec((8, 128), lambda i, d: (0, 0))],
        out_shape=[jax.ShapeDtypeStruct((n // 2, shards, r, c), BF)] * 2 + [MARK],
        compiler_params=pltpu.CompilerParams(vmem_limit_bytes=32 * MIB),
        cost_estimate=cost(3),
    )(left, right, left, right, *after)


def close_kernel(counts, *refs):
    total, first, mark = refs[-3:]
    mark[...] = jnp.zeros_like(mark)
    row = n = 0
    for count in counts:
        value = refs[n][0, 0].astype(F32)
        for m in range(1, count):
            value += refs[n + m][0, 0].astype(F32)
        value = rnd(value)
        n += count
        rows = pl.ds(row, value.shape[0])
        total[0, rows, :] = value

        @pl.when(pl.program_id(0) == min(1, pl.num_programs(0) - 1))
        def _():
            first[rows, :] = value

        row += value.shape[0]


def close(groups, after=()):
    _, shards, _, c = groups[0][0].shape
    height = sum(group[0].shape[2] for group in groups)
    flat = [a for group in groups for a in group]
    return pl.pallas_call(
        functools.partial(close_kernel, [len(group) for group in groups]),
        grid=(shards,),
        in_specs=[pl.BlockSpec((1, 1) + a.shape[2:], lambda d: (0, d, 0, 0)) for a in flat]
        + [ANY_SPEC] * len(after),
        out_specs=[
            pl.BlockSpec((1, height, c), lambda d: (d, 0, 0)),
            pl.BlockSpec((height, c), lambda d: (0, 0)),
            pl.BlockSpec((8, 128), lambda d: (0, 0)),
        ],
        out_shape=[
            jax.ShapeDtypeStruct((shards, height, c), BF),
            jax.ShapeDtypeStruct((height, c), BF),
            MARK,
        ],
        compiler_params=pltpu.CompilerParams(vmem_limit_bytes=32 * MIB),
        cost_estimate=cost(3),
    )(*flat, *after)


def close_parts_kernel(count, *refs):
    value = refs[0][...].astype(F32)
    for m in range(1, count):
        value += refs[m][...].astype(F32)
    refs[-2][...] = rnd(value)
    refs[-1][...] = jnp.zeros_like(refs[-1])


def close_parts(parts, after=()):
    return pl.pallas_call(
        functools.partial(close_parts_kernel, len(parts)),
        in_specs=[VMEM_SPEC] * len(parts) + [ANY_SPEC] * len(after),
        out_specs=[VMEM_SPEC] * 2,
        out_shape=[jax.ShapeDtypeStruct(parts[0].shape, BF), MARK],
        compiler_params=pltpu.CompilerParams(vmem_limit_bytes=32 * MIB),
        cost_estimate=cost(1),
    )(*parts, *after)


def join_kernel(travel, part, *refs):
    total, mark = refs[-2:]
    total[...] = add_low(travel[...], part[0])
    mark[...] = jnp.zeros_like(mark)


def join(travel, parts, d, after=()):
    r, c = travel.shape
    return pl.pallas_call(
        join_kernel,
        grid=(1,),
        in_specs=[
            pl.BlockSpec((r, c), lambda i: (0, 0)),
            pl.BlockSpec((1, r, c), lambda i: (d, 0, 0)),
        ]
        + [ANY_SPEC] * len(after),
        out_specs=[pl.BlockSpec((r, c), lambda i: (0, 0)), pl.BlockSpec((8, 128), lambda i: (0, 0))],
        out_shape=[jax.ShapeDtypeStruct((r, c), BF), MARK],
        compiler_params=pltpu.CompilerParams(vmem_limit_bytes=32 * MIB),
        cost_estimate=cost(1),
    )(travel, parts, *after)


def direct(parts, replicas):
    return [part if m == 0 else swap(part, 2 * m, replicas) for m, part in enumerate(parts)]


def spread_kernel(left, right, *refs):
    count = left.shape[0]
    for m in range(count):
        refs[-1 - count + m][...] = add_low(left[m], right[m])
    refs[-1][...] = jnp.zeros_like(refs[-1])


def spread(left, right, after=()):
    n, shards, r, c = left.shape
    block = pl.BlockSpec((n, 1, r, c), lambda d: (0, d, 0, 0))
    part = pl.BlockSpec((1, r, c), lambda d: (d, 0, 0))
    return pl.pallas_call(
        spread_kernel,
        grid=(shards,),
        in_specs=[block] * 2 + [ANY_SPEC] * len(after),
        out_specs=[part] * n + [pl.BlockSpec((8, 128), lambda d: (0, 0))],
        out_shape=[jax.ShapeDtypeStruct((shards, r, c), BF)] * n + [MARK],
        compiler_params=pltpu.CompilerParams(vmem_limit_bytes=32 * MIB),
        cost_estimate=cost(3),
    )(left, right, *after)


def gather_sum_kernel(count, place, *refs):
    value = refs[0][...].astype(F32)
    for m in range(1, count):
        value += refs[m][...].astype(F32)
    refs[-2][...] = rnd(value)
    refs[-1][...] = jnp.zeros_like(refs[-1])


def gather_sum(place, parts, after=()):
    shards, r, c = parts[0].shape
    return pl.pallas_call(
        functools.partial(gather_sum_kernel, len(parts)),
        grid_spec=pltpu.PrefetchScalarGridSpec(
            num_scalar_prefetch=1,
            grid=(shards,),
            in_specs=[pl.BlockSpec((1, r, c), lambda d, s: (lax.rem(s[1] + d, shards), 0, 0))] * len(parts)
            + [ANY_SPEC] * len(after),
            out_specs=[
                pl.BlockSpec((1, r, c), lambda d, s: (d, 0, 0)),
                pl.BlockSpec((8, 128), lambda d, s: (0, 0)),
            ],
        ),
        out_shape=[jax.ShapeDtypeStruct((shards, r, c), BF), MARK],
        compiler_params=pltpu.CompilerParams(vmem_limit_bytes=32 * MIB),
        cost_estimate=cost(2),
    )(place, *parts, *after)


class Scatter:
    def __init__(self, keep, send, replicas, reverse, first=0):
        self.replicas, self.reverse = replicas, reverse
        self.bits = chip_bits(replicas, reverse)
        bit = self.bits.pop(0) if first else 1
        self.pair = (keep, swap(send, bit, replicas))

    def step(self, mark):
        keep, go, mark = fold(*self.pair, self.reverse, (mark,))
        self.pair = (keep, swap(go, self.bits.pop(0), self.replicas))
        return mark


def flip_by(value, axis, me, replicas):
    shape = value.shape
    bits = replicas.bit_length() - 1
    value = value.reshape(shape[:axis] + (2,) * bits + shape[axis + 1 :])
    for n in range(bits):
        where = axis + bits - 1 - n
        value = jnp.where((me >> n) & 1 == 1, jnp.flip(value, where), value)
    return value.reshape(shape)


def window_low(lengths, group_len):
    prompt = group_len // 2
    order = jnp.arange(lengths.shape[0], dtype=jnp.int32)
    ends = jnp.sum(jnp.where(order[:, None] <= order[None, :], lengths[:, None], 0), 0)
    pos = jnp.arange(prompt, dtype=jnp.int32)
    starts = jnp.max(jnp.where(ends[:, None] <= pos[None, :], ends[:, None], 0), 0)
    return jnp.concatenate([jnp.zeros((prompt,), jnp.int32), prompt + starts])[None]


def body(
    tokens,
    cotangent,
    cont_lengths,
    ln1_gain,
    ln1_bias,
    w_qkv,
    q_bias,
    v_bias,
    w_out,
    out_bias,
    ln2_gain,
    ln2_bias,
    w_up,
    up_bias,
    w_down,
    down_bias,
):
    rows, width = tokens.shape
    shards, replicas = lax.axis_size("fsdp"), lax.axis_size("dp")
    z, me = lax.axis_index("fsdp"), lax.axis_index("dp")
    place = jnp.stack([me, z]).astype(jnp.int32)
    group_len = rows * shards
    head_dim = width // H
    local = width // shards
    hidden = w_up.shape[2]
    w_qkv, w_out, w_up, w_down = w_qkv[0], w_out[0], w_up[0], w_down[0]
    cut_out = Cut(w_out.shape[0], width, 1, replicas, shards)
    cut_up = Cut(w_up.shape[0], hidden, hidden // width, replicas, shards)
    cut_down = Cut(w_down.shape[0], width, 1, replicas, shards)
    cuts = (cut_out, cut_up, cut_down)

    vectors = (ln1_gain, ln1_bias, q_bias, v_bias, out_bias, ln2_gain, ln2_bias, down_bias, up_bias)
    packed = jnp.concatenate(vectors, 1)
    slim = w_qkv.shape[0] // replicas
    mine = lax.dynamic_slice_in_dim(w_qkv, me * slim, slim, 0)
    mine = mine.reshape(slim, 3, shards, local).transpose(2, 0, 1, 3).reshape(shards, slim, 3 * local)
    turned = [packed] + [turn(packed, shards, step) for step in range(shards - 1, 0, -1)]
    turned = jnp.concatenate(turned + turned, 0)
    packed_all = lax.dynamic_slice_in_dim(turned, lax.rem(shards - z, shards), shards)
    full = []
    offset = 0
    for vector in vectors:
        size = vector.shape[1]
        full.append(packed_all[:, offset : offset + size].reshape(1, shards * size).astype(F32))
        offset += size
    gain_one, bias_one, _, _, bias_out, gain_two, bias_two, bias_down, bias_up = full
    middle_vectors = jnp.concatenate([bias_out, gain_two, bias_two, bias_down] * 2, 0)
    start_at = z * local
    bias_q = lax.dynamic_slice_in_dim(full[2], start_at, local, 1)
    bias_v = lax.dynamic_slice_in_dim(full[3], start_at, local, 1)
    bias_qkv = jnp.concatenate([bias_q, jnp.zeros_like(bias_q), bias_v], 1)

    piece = jnp.concatenate(
        [cut.of(shard, me) for cut, shard in ((cut_out, w_out), (cut_up, w_up), (cut_down, w_down))], 0
    )
    piece = gate(piece, mine)
    slots = around(piece, shards)
    near = (slots[1], slots[shards - 1])
    blocks = around(gate(tokens, packed, *near), shards)
    mine = gate(lax.all_to_all(mine, "fsdp", 0, 0, tiled=True), *near)
    weight_qkv = flip_by(jnp.stack(share(mine, replicas)), 0, me, replicas)
    weight_qkv = weight_qkv.transpose(1, 0, 2, 3).reshape(width, 3 * local)

    hiddens = [None] * shards
    combined = jnp.zeros((group_len, 3 * local), BF)
    for d in [0] + sorted(range(1, shards), key=lambda d: min(d, shards - d)):
        if d == shards // 2:
            early = mark
        hiddens[d], combined, mark = project(
            place, blocks[d], gain_one, bias_one, weight_qkv, bias_qkv, combined, d, shards
        )

    edge = cut_out.r + cut_up.r
    slots = [gate(slots[d], early) for d in range(1, shards)]
    upper = jnp.stack([slot[:edge] for slot in slots])
    lower = jnp.stack([slot[edge:] for slot in slots])

    low = window_low(cont_lengths[0], group_len)
    mixed, lse = attend(combined, low, head_dim)
    attended = [
        lax.dynamic_slice_in_dim(mixed, lax.rem(z + d, shards) * rows, rows) for d in range(shards)
    ]
    attended = [turn(block, shards, d) if d else block for d, block in enumerate(attended)]
    pause = lambda part: gate(part, mark)
    lists = share(upper, replicas, False, pause) + share(lower, replicas, True, pause)
    lists += [w_out, w_up, w_down]
    output, hidden_two, middle, acted, slope = feed_forward(
        place, attended, tokens, middle_vectors, bias_up, cuts, lists
    )

    dm = cotangent
    du, dx2, da, do, grad_bias_up, sums = feed_backward(
        place, dm, slope, middle, middle_vectors, cuts, lists
    )
    grad_mixed = lax.all_to_all(do, "fsdp", 1, 0, tiled=True)
    terms = ((cut_down, acted, dm, False), (cut_up, hidden_two, du, True), (cut_out, attended, da, False))
    mark = grad_bias_up
    scatters = []
    if all(cut.rows % 256 == 0 for cut in cuts):
        gots = []
        for cut, left, right, _ in terms:
            send, mark = send_grad(cut, place, left, right, (mark,) if gots else ())
            gots.append(swap(send, 1, replicas))
        for (cut, left, right, reverse), got in zip(terms, gots):
            stay, go, mark = keep_grad(cut, place, left, right, got, reverse, (mark,))
            if cut is cut_out:
                halves = (stay, go)
                out = [halves[m % 2][m // 2 : m // 2 + 1] for m in range(replicas // 2)]
            else:
                scatters.append(Scatter(stay, go, replicas, reverse, True))
    else:
        turned = [attended[-d % shards] for d in range(shards)] * 2
        joined = lax.dynamic_slice_in_dim(
            jnp.concatenate(turned, 1), lax.rem(shards - z, shards) * local, width, 1
        )
        for cut, left, right, reverse in terms:
            left = joined if left is attended else left
            keep, send, mark = weight_grad(cut, place, left, right, (mark,))
            if cut is cut_out:
                *out, mark = spread(keep, swap(send, 1, replicas), (mark,))
                out = [part[None] for part in out]
            else:
                scatters.append(Scatter(keep, send, replicas, reverse))
        for scatter in scatters:
            mark = scatter.step(mark)
    down, up = scatters
    out = direct(out, replicas)

    dq, dk, dv, bias_sums = attend_grad(combined, low, mixed, lse, grad_mixed, head_dim, (mark,))
    parts = {}
    parts[1 % shards], first_sums = hidden_grad(place, blocks[1 % shards], dq, dk, dv, weight_qkv, 1, shards)
    travel = turn(parts[1 % shards], shards)
    mark = first_sums
    while down.bits:
        mark = down.step(mark)
        mark = up.step(mark)
    out, mark = close_parts(out, (mark,))
    for d in [*range(2, shards), 0]:
        parts[d], mark = hidden_grad(
            place, blocks[d], dq, dk, dv, weight_qkv, d, shards, (mark,)
        )
        first_sums += mark

    blank = jnp.zeros((width,), F32)
    grad_bias_q = lax.dynamic_update_slice(blank, bias_sums[:, 0].reshape(-1), (start_at,))
    grad_bias_v = lax.dynamic_update_slice(blank, bias_sums[:, 1].reshape(-1), (start_at,))
    small = (
        first_sums[0],
        first_sums[1],
        grad_bias_q,
        grad_bias_v,
        sums[3],
        sums[1],
        sums[2],
        sums[0],
        grad_bias_up,
    )
    small = jnp.concatenate([g.reshape(shards, -1) for g in small], 1)
    count = small.shape[1] // replicas
    small = small.reshape(shards, replicas, count)
    small = jnp.pad(small, ((0, 0), (0, 0), (0, 3 * local - count)))
    others = list(range(2, shards))
    if others:
        step, mark = join(travel, parts[others[0]][None], 0, (mark,))
        travel = turn(step, shards)
    keep, send, mark = qkv_grad(place, hiddens, dq, dk, dv, small, slim, shards, (mark,))
    got = swap(send, 1, replicas)

    sums_all, first, mark = close(([out], up.pair, down.pair), (mark,))
    ring = turn(first, shards)
    *qkv, mark = spread(keep, got, (mark,))
    qkv = direct(qkv, replicas)
    come = None
    for d in range(2, shards + 1):
        total, mark = join(ring, sums_all, d % shards, (mark,))
        if d < shards:
            ring = turn(total, shards)
        if come is None:
            piece, mark = gather_sum(place, qkv, (mark,))
            come = [piece[0]] + [turn(piece[e], shards, e) for e in range(1, shards)]
    for d in others[1:]:
        step, mark = join(travel, parts[d][None], 0, (mark,))
        travel = turn(step, shards)
    input_grad, last_mark = last(tokens, travel, parts[0], dx2, gain_one)
    rows_qkv = jnp.concatenate(
        [
            jnp.concatenate([block[:slim, k * local : (k + 1) * local] for block in come], 1)
            for k in range(3)
        ],
        0,
    )
    row_small = rnd(sum(block[slim, :count].astype(F32) for block in come))
    row_small = jnp.pad(row_small[None], ((0, 15), (0, width - count)))
    upper = jnp.concatenate([total[:edge], row_small], 0)
    lower = jnp.concatenate([total[edge:], rows_qkv], 0)
    own_a = gate(jnp.stack(share_chips(upper, replicas, False)), last_mark)
    own_b = gate(jnp.stack(share_chips(lower, replicas, True)), last_mark)
    out_w_out, out_w_up, out_w_down, out_w_qkv, total = widen(
        cuts, slim, place, own_a, swap(own_a, 1, replicas), own_b, swap(own_b, 1, replicas)
    )
    total = total.reshape(replicas, 8, width)[:, 0, :count].reshape(1, -1)
    outs = []
    offset = 0
    for vector in vectors:
        outs.append(total[:, offset : offset + vector.shape[1]])
        offset += vector.shape[1]
    return (
        output,
        input_grad,
        outs[0],
        outs[1],
        out_w_qkv[None],
        outs[2],
        outs[3],
        out_w_out[None],
        outs[4],
        outs[5],
        outs[6],
        out_w_up[None],
        outs[8],
        out_w_down[None],
        outs[7],
    )


def solution(mesh):
    vec = P(None, "fsdp")
    mat = P(None, "fsdp", None)
    tok = P(("dp", "fsdp"), None)
    in_specs = (tok, tok, P("dp", None), vec, vec, mat, vec, vec, mat, vec, vec, vec, mat, vec, mat, vec)
    out_specs = (tok, tok, vec, vec, mat, vec, vec, mat, vec, vec, vec, mat, vec, mat, vec)
    return jax.shard_map(body, mesh=mesh, in_specs=in_specs, out_specs=out_specs, check_vma=False)
```

```python
import functools

import jax
import jax.numpy as jnp
from jax import lax
from jax.experimental import pallas as pl
from jax.experimental.pallas import tpu as pltpu
from jax.sharding import PartitionSpec as P

H = 16
EPSILON = 1e-05
NEG_LARGE = -1e30
F32 = jnp.float32
BF = jnp.bfloat16
MIB = 2**20
COST_UNIT = 10**8


def rnd(v):
    return v.astype(BF)


def cost(time):
    return pl.CostEstimate(flops=int(time * COST_UNIT), bytes_accessed=1, transcendentals=0)


def dot_last(left, right):
    return lax.dot_general(left, right, (((1,), (1,)), ((), ())), preferred_element_type=F32)


def dot_mm(left, right):
    return jnp.dot(left, right, preferred_element_type=F32)


def key_ranges(start, group_len):
    prompt = group_len // 2
    if start < prompt:
        return start, start
    return prompt, max(prompt, start - group_len // 8)


def allowed_mask(shape, key_start, query_start, low_row):
    key_pos = lax.broadcasted_iota(jnp.int32, shape, 0) + key_start
    query_pos = lax.broadcasted_iota(jnp.int32, shape, 1) + query_start
    return (key_pos <= query_pos) & (key_pos >= low_row)


def attend_kernel(group_len, head_dim, q_ref, k_ref, v_ref, low_ref, o_ref, lse_ref):
    size = min(512, group_len // 4)
    scale = jnp.asarray(head_dim**-0.5, BF)
    values_t = v_ref[...].astype(F32).T.astype(BF)
    for start in range(0, group_len, size):
        stop = start + size
        full, near = key_ranges(start, group_len)
        results = []
        for head in range(128 // head_dim):
            lanes = slice(head * head_dim, (head + 1) * head_dim)
            queries = q_ref[start:stop, lanes] * scale
            part = dot_last(k_ref[near:stop, lanes], queries)
            ok = allowed_mask(part.shape, near, start, low_ref[0:1, start:stop])
            part = jnp.where(ok, part, NEG_LARGE)
            top = jnp.max(part, 0, keepdims=True)
            if full:
                rest = dot_last(k_ref[0:full, lanes], queries)
                top = jnp.maximum(top, jnp.max(rest, 0, keepdims=True))
            part = jnp.exp(part - top)
            total = jnp.sum(part, 0, keepdims=True)
            mixed = dot_mm(values_t[lanes, near:stop], part.astype(BF))
            if full:
                rest = jnp.exp(rest - top)
                total += jnp.sum(rest, 0, keepdims=True)
                mixed += dot_mm(values_t[lanes, 0:full], rest.astype(BF))
            results.append(mixed * (1.0 / total))
            lse_ref[0, head : head + 1, start:stop] = top + jnp.log(total)
        o_ref[start:stop, :] = jnp.concatenate(results, 0).T.astype(BF)


def attend_grad_kernel(
    group_len, head_dim, q_ref, k_ref, v_ref, low_ref, o_ref, lse_ref, do_ref, *refs
):
    dq_ref, dk_ref, dv_ref, bias_ref, dk_sum, dv_sum = refs[-6:]
    bias = jnp.zeros((1, 128), F32)
    size = min(256, group_len // 8)
    scale = jnp.asarray(head_dim**-0.5, BF)
    keys_t = k_ref[...].astype(F32).T.astype(BF)
    dk_sum[...] = jnp.zeros_like(dk_sum)
    dv_sum[...] = jnp.zeros_like(dv_sum)
    for start in range(0, group_len, size):
        stop = start + size
        full, near = key_ranges(start, group_len)
        product_t = (do_ref[start:stop, :].astype(F32) * o_ref[start:stop, :].astype(F32)).T
        results = []
        for head in range(128 // head_dim):
            lanes = slice(head * head_dim, (head + 1) * head_dim)
            queries = q_ref[start:stop, lanes] * scale
            grads = do_ref[start:stop, lanes]
            delta = jnp.sum(product_t[lanes, :], 0, keepdims=True)
            lse = lse_ref[0, head : head + 1, start:stop]
            dq_t = jnp.zeros((head_dim, size), F32)
            for first, last, masked in ((near, stop, True), (0, full, False)):
                if first == last:
                    continue
                probs = jnp.exp(dot_last(k_ref[first:last, lanes], queries) - lse)
                if masked:
                    ok = allowed_mask(probs.shape, first, start, low_ref[0:1, start:stop])
                    probs = jnp.where(ok, probs, 0.0)
                grad_probs = dot_last(v_ref[first:last, lanes], grads)
                ds = (probs * (grad_probs - delta)).astype(BF)
                dv_sum[head, first:last, :] += dot_mm(probs.astype(BF), grads)
                dk_sum[head, first:last, :] += dot_mm(ds, queries)
                dq_t += dot_mm(keys_t[lanes, first:last], ds)
            results.append(dq_t * head_dim**-0.5)
        dq = jnp.concatenate(results, 0).T.astype(BF)
        dq_ref[start:stop, :] = dq
        bias += jnp.sum(dq.astype(F32), 0, keepdims=True)
    heads = range(128 // head_dim)
    dk_ref[...] = jnp.concatenate([dk_sum[head] for head in heads], 1).astype(BF)
    dv = jnp.concatenate([dv_sum[head] for head in heads], 1).astype(BF)
    dv_ref[...] = dv
    bias_ref[0, 0:1, :] = bias
    bias_ref[0, 1:2, :] = jnp.sum(dv.astype(F32), 0, keepdims=True)


def attend(combined, low, head_dim):
    group_len, width = combined.shape[0], combined.shape[1] // 3
    steps = width // 128
    heads = 128 // head_dim
    block = lambda offset: pl.BlockSpec((group_len, 128), lambda i: (0, offset + i))
    return pl.pallas_call(
        functools.partial(attend_kernel, group_len, head_dim),
        grid=(steps,),
        in_specs=[block(0), block(steps), block(2 * steps), pl.BlockSpec((1, group_len), lambda i: (0, 0))],
        out_specs=[block(0), pl.BlockSpec((1, heads, group_len), lambda i: (i, 0, 0))],
        out_shape=[
            jax.ShapeDtypeStruct((group_len, width), BF),
            jax.ShapeDtypeStruct((steps, heads, group_len), F32),
        ],
        compiler_params=pltpu.CompilerParams(vmem_limit_bytes=56 * MIB),
        cost_estimate=cost(18),
    )(combined, combined, combined, low)


def attend_grad(combined, low, mixed, lse, grad_mixed, head_dim, after=()):
    group_len, width = mixed.shape
    steps = width // 128
    heads = 128 // head_dim
    block = lambda offset: pl.BlockSpec((group_len, 128), lambda i: (0, offset + i))
    return pl.pallas_call(
        functools.partial(attend_grad_kernel, group_len, head_dim),
        grid=(steps,),
        in_specs=[
            block(0),
            block(steps),
            block(2 * steps),
            pl.BlockSpec((1, group_len), lambda i: (0, 0)),
            block(0),
            pl.BlockSpec((1, heads, group_len), lambda i: (i, 0, 0)),
            block(0),
        ]
        + [pl.BlockSpec(memory_space=pl.ANY)] * len(after),
        out_specs=[block(0)] * 3 + [pl.BlockSpec((1, 2, 128), lambda i: (i, 0, 0))],
        out_shape=[jax.ShapeDtypeStruct((group_len, width), BF)] * 3
        + [jax.ShapeDtypeStruct((steps, 2, 128), F32)],
        scratch_shapes=[pltpu.VMEM((heads, group_len, head_dim), F32)] * 2,
        compiler_params=pltpu.CompilerParams(vmem_limit_bytes=56 * MIB),
        cost_estimate=cost(28),
    )(combined, combined, combined, low, mixed, lse, grad_mixed, *after)


class Cut:
    def __init__(self, rows, columns, column_parts, replicas, shards):
        self.rows, self.columns, self.shards, self.replicas = rows, columns, shards, replicas
        self.nc, self.nr = column_parts, replicas // column_parts
        self.r, self.c = rows // self.nr, columns // self.nc

    def place(self, piece):
        half = self.nr // 2
        row = (lax.rem(piece, 2) * half + lax.rem(lax.div(piece, 2), half)) * self.r
        column = lax.div(piece, self.nr) * self.c
        return pl.multiple_of(row, 8 if self.r % 16 else 16), pl.multiple_of(column, 128)

    def spot(self, piece, base=0):
        row, column = self.place(piece)
        return pl.ds(base + row, self.r), pl.ds(column, self.c)

    def of(self, shard, piece):
        return lax.dynamic_slice(shard, self.place(piece), (self.r, self.c))

    @property
    def copies(self):
        return 1 + (self.shards - 1) * self.replicas


def fetch(cut, me, z, slots, first_row, shard, whole, sems):
    base = pl.multiple_of(z * cut.rows, 16)
    copies = [pltpu.make_async_copy(shard, whole.at[pl.ds(base, cut.rows), :], sems.at[0])]
    for d in range(1, cut.shards):
        base = pl.multiple_of(lax.rem(z + cut.shards - d, cut.shards) * cut.rows, 16)
        for j in range(cut.replicas):
            copies.append(
                pltpu.make_async_copy(
                    slots[j].at[d - 1, pl.ds(first_row, cut.r), :],
                    whole.at[cut.spot(jnp.bitwise_xor(me, j), base)],
                    sems.at[len(copies)],
                )
            )
    return copies


def loads_of(cuts, place, lists, wholes, sems):
    count = cuts[0].replicas
    both, down, shards = lists[:count], lists[count : 2 * count], lists[2 * count :]
    sources = ((both, 0), (both, cuts[0].r), (down, 0))
    return [
        fetch(cut, place[0], place[1], slots, row, shard, whole, sem)
        for cut, (slots, row), shard, whole, sem in zip(cuts, sources, shards, wholes, sems)
    ]


def start(copies):
    for copy in copies:
        copy.start()


def finish(copies):
    for copy in copies:
        copy.wait()


MARK = jax.ShapeDtypeStruct((8, 128), F32)
SMEM_SPEC = pl.BlockSpec(memory_space=pltpu.SMEM)
ANY_SPEC = pl.BlockSpec(memory_space=pl.ANY)
VMEM_SPEC = pl.BlockSpec(memory_space=pltpu.VMEM)


def moments(stream):
    mean = jnp.mean(stream, -1, keepdims=True)
    centered = stream - mean
    scale = lax.rsqrt(jnp.mean(centered * centered, -1, keepdims=True) + EPSILON)
    return centered * scale, scale


def norm_grad(grad_hidden, gain, normal, scale):
    t = grad_hidden * gain
    return scale * (
        t - jnp.mean(t, -1, keepdims=True) - normal * jnp.mean(t * normal, -1, keepdims=True)
    )


def project_kernel(place, block, gain, bias, weight, bias_qkv, c_in, h_out, c_out, mark):
    mark[...] = jnp.zeros_like(mark)
    normal, _ = moments(block[...].astype(F32))
    hidden = rnd(normal * gain[...] + bias[...])
    h_out[...] = hidden
    c_out[...] = rnd(dot_mm(hidden, weight[...]) + bias_qkv[...])


def project(place, block, gain, bias, weight, bias_qkv, c_all, distance, shards):
    rows, width = block.shape
    whole = lambda a: pl.BlockSpec(a.shape, lambda i, s: (0,) * a.ndim)
    at = lambda i, s: (lax.rem(s[1] + shards - distance, shards), 0)
    return pl.pallas_call(
        project_kernel,
        grid_spec=pltpu.PrefetchScalarGridSpec(
            num_scalar_prefetch=1,
            grid=(1,),
            in_specs=[whole(a) for a in (block, gain, bias, weight, bias_qkv)] + [ANY_SPEC],
            out_specs=[
                pl.BlockSpec((rows, width), lambda i, s: (0, 0)),
                pl.BlockSpec((rows, c_all.shape[1]), at),
                pl.BlockSpec((8, 128), lambda i, s: (0, 0)),
            ],
        ),
        out_shape=[jax.ShapeDtypeStruct(a.shape, BF) for a in (block, c_all)] + [MARK],
        input_output_aliases={6: 1},
        compiler_params=pltpu.CompilerParams(vmem_limit_bytes=40 * MIB),
        cost_estimate=cost(2.5),
    )(place, block, gain, bias, weight, bias_qkv, c_all)


GELU_A = 0.7978845608028654
GELU_B = 0.044715


def gelu_both(u):
    square = u * u
    t = jnp.tanh(GELU_A * u * (1.0 + GELU_B * square))
    value = 0.5 * u * (1.0 + t)
    slope = 0.5 * (1.0 + t) + 0.5 * u * (1.0 - t * t) * (GELU_A * (1.0 + 3.0 * GELU_B * square))
    return value, slope


def forward_kernel(cuts, step, place, tokens, vectors, bias_up, *refs):
    shards = cuts[0].shards
    mixed, refs = refs[:shards], refs[shards:]
    count = 2 * cuts[0].replicas + 3
    lists, refs = refs[:count], refs[count:]
    out, hidden, middle, acted, slope, w_out, w_up, w_down, *sems = refs
    loads = loads_of(cuts, place, lists, (w_out, w_up, w_down), sems)
    for copies in loads:
        start(copies)
    finish(loads[0])
    stream = tokens[...].astype(F32) + vectors[0:1, :]
    local = mixed[0].shape[1]
    for d in range(shards):
        at = pl.multiple_of(lax.rem(place[1] + shards - d, shards) * local, 16)
        stream += dot_mm(mixed[d][...], w_out[pl.ds(at, local), :])
    middle[...] = stream
    normal, _ = moments(stream)
    hidden[...] = rnd(normal * vectors[1:2, :] + vectors[2:3, :])
    finish(loads[1])
    finish(loads[2])
    total = vectors[3:4, :] + stream
    for block in range(0, w_up.shape[1], step):
        columns = slice(block, block + step)
        u = dot_mm(hidden[...], w_up[:, columns]) + bias_up[:, columns]
        value, grad = gelu_both(u)
        value = rnd(value)
        acted[:, columns] = value
        slope[:, columns] = rnd(grad)
        total += dot_mm(value, w_down[columns, :])
    out[...] = rnd(total)


def feed_forward(place, mixed, tokens, vectors, bias_up, cuts, lists):
    rows, width = tokens.shape
    hidden = bias_up.shape[1]
    return pl.pallas_call(
        functools.partial(forward_kernel, cuts, min(1024, hidden)),
        in_specs=[SMEM_SPEC] + [VMEM_SPEC] * (3 + len(mixed)) + [ANY_SPEC] * len(lists),
        out_specs=[VMEM_SPEC] * 5,
        out_shape=[
            jax.ShapeDtypeStruct((rows, width), BF),
            jax.ShapeDtypeStruct((rows, width), BF),
            jax.ShapeDtypeStruct((rows, width), F32),
            jax.ShapeDtypeStruct((rows, hidden), BF),
            jax.ShapeDtypeStruct((rows, hidden), BF),
        ],
        scratch_shapes=[
            pltpu.VMEM((width, width), BF),
            pltpu.VMEM((width, hidden), BF),
            pltpu.VMEM((hidden, width), BF),
        ]
        + [pltpu.SemaphoreType.DMA((cut.copies,)) for cut in cuts],
        compiler_params=pltpu.CompilerParams(vmem_limit_bytes=60 * MIB),
        cost_estimate=cost(24),
    )(place, tokens, vectors, bias_up, *mixed, *lists)


def backward_kernel(cuts, step, place, dm, slope, middle, vectors, *refs):
    count = 2 * cuts[0].replicas + 3
    lists, refs = refs[:count], refs[count:]
    du, dx2, da, do, grad_up, sums, w_out, w_up, w_down, *sems = refs
    loads = loads_of(cuts, place, lists, (w_out, w_up, w_down), sems)[::-1]
    for copies in loads:
        start(copies)
    finish(loads[0])
    finish(loads[1])
    dh2 = jnp.zeros(middle.shape, F32)
    for block in range(0, w_up.shape[1], step):
        columns = slice(block, block + step)
        part = rnd(dot_last(dm[...], w_down[columns, :]) * slope[:, columns].astype(F32))
        du[:, columns] = part
        grad_up[:, columns] = jnp.sum(part.astype(F32), 0, keepdims=True)
        dh2 += dot_last(part, w_up[:, columns])
    normal, scale = moments(middle[...])
    incoming = dm[...].astype(F32)
    stream = incoming + norm_grad(dh2, vectors[1:2, :], normal, scale)
    dx2[...] = stream
    low = rnd(stream)
    da[...] = low
    finish(loads[2])
    do[...] = rnd(dot_last(low, w_out[...]))
    sums[0:1, :] = jnp.sum(incoming, 0, keepdims=True)
    sums[1:2, :] = jnp.sum(dh2 * normal, 0, keepdims=True)
    sums[2:3, :] = jnp.sum(dh2, 0, keepdims=True)
    sums[3:4, :] = jnp.sum(low.astype(F32), 0, keepdims=True)
    sums[4:8, :] = jnp.zeros((4, sums.shape[1]), F32)


def feed_backward(place, dm, slope, middle, vectors, cuts, lists):
    rows, width = dm.shape
    hidden = slope.shape[1]
    return pl.pallas_call(
        functools.partial(backward_kernel, cuts, min(1024, hidden)),
        in_specs=[SMEM_SPEC] + [VMEM_SPEC] * 4 + [ANY_SPEC] * len(lists),
        out_specs=[VMEM_SPEC] * 6,
        out_shape=[
            jax.ShapeDtypeStruct((rows, hidden), BF),
            jax.ShapeDtypeStruct((rows, width), F32),
            jax.ShapeDtypeStruct((rows, width), BF),
            jax.ShapeDtypeStruct((rows, width), BF),
            jax.ShapeDtypeStruct((1, hidden), F32),
            jax.ShapeDtypeStruct((8, width), F32),
        ],
        scratch_shapes=[
            pltpu.VMEM((width, width), BF),
            pltpu.VMEM((width, hidden), BF),
            pltpu.VMEM((hidden, width), BF),
        ]
        + [pltpu.SemaphoreType.DMA((cut.copies,)) for cut in cuts],
        compiler_params=pltpu.CompilerParams(vmem_limit_bytes=60 * MIB),
        cost_estimate=cost(24),
    )(place, dm, slope, middle, vectors, *lists)


def weight_grad_kernel(cut, place, left, right, *refs):
    keep, send, mark, whole = refs[-4:]
    mark[...] = jnp.zeros_like(mark)
    whole[...] = lax.dot_general(
        left[...], right[...], (((0,), (0,)), ((), ())), preferred_element_type=F32
    )
    for j in range(cut.replicas):
        value = whole[cut.spot(jnp.bitwise_xor(place[0], j))]
        (keep, send)[j & 1][j >> 1, 0] = rnd(value)


def weight_grad(cut, place, left, right, after=()):
    tokens, shards = left.shape[0], cut.shards
    shape = (cut.replicas // 2, shards, cut.r, cut.c)
    piece = pl.BlockSpec((cut.replicas // 2, 1, cut.r, cut.c), lambda d, s: (0, d, 0, 0))
    return pl.pallas_call(
        functools.partial(weight_grad_kernel, cut),
        grid_spec=pltpu.PrefetchScalarGridSpec(
            num_scalar_prefetch=1,
            grid=(shards,),
            in_specs=[
                pl.BlockSpec((tokens, cut.rows), lambda d, s: (0, lax.rem(s[1] + shards - d, shards))),
                pl.BlockSpec(right.shape, lambda d, s: (0, 0)),
            ]
            + [ANY_SPEC] * len(after),
            out_specs=[piece] * 2 + [pl.BlockSpec((8, 128), lambda d, s: (0, 0))],
            scratch_shapes=[pltpu.VMEM((cut.rows, cut.columns), F32)],
        ),
        out_shape=[jax.ShapeDtypeStruct(shape, BF)] * 2 + [MARK],
        compiler_params=pltpu.CompilerParams(vmem_limit_bytes=56 * MIB),
        cost_estimate=cost(10),
    )(place, left, right, *after)


def gather_rows(cut, place, other, lefts, rows):
    size = cut.rows // 2
    half = lax.rem(place[0] + other, 2) * size
    for d in range(cut.shards):
        if len(lefts) > 1:
            part = lefts[d][:, pl.ds(pl.multiple_of(half, 128), size)]
        else:
            column = lax.rem(place[1] + cut.shards - d, cut.shards) * cut.rows + half
            part = lefts[0][:, pl.ds(pl.multiple_of(column, 128), size)]
        rows[:, d * size : (d + 1) * size] = part


def wide_kernel(cut, other, reverse, count, place, right, *refs):
    lefts, refs = refs[:count], refs[count:]
    rows, turned, whole = refs[-3:]
    refs = refs[:-1]
    refs[-3][...] = jnp.zeros_like(refs[-3])
    step = pl.program_id(0)

    @pl.when(step == 0)
    def _():
        gather_rows(cut, place, other, lefts, rows)
        turned[...] = rows[...].astype(F32).T.astype(BF)

    whole[...] = dot_mm(turned[...], right[...])
    half, size = cut.nr // 2, cut.rows // 2
    chip = lax.rem(lax.div(place[0], 2), half)

    def part(n, d):
        row = jnp.bitwise_xor(chip, n) * cut.r + d * size
        return whole[pl.ds(pl.multiple_of(row, 16), cut.r), :]

    for d in range(cut.shards):
        for n in range(half):
            if other:
                refs[-4][n, d] = rnd(part(n, d))
                continue
            got, (stay, go) = refs[0], refs[-5:-3]
            value = rnd(part(n, d) + got[n, d].astype(F32))
            if cut.nc == 1:
                leaves, m = (n >= half // 2, n % (half // 2)) if reverse else (n % 2 == 1, n // 2)
                (go if leaves else stay)[m, d] = value
            else:

                @pl.when(step < cut.nc // 2)
                def _():
                    stay[n, d] = value

                @pl.when(step >= cut.nc // 2)
                def _():
                    go[n, d] = value


def wide_grad(cut, place, left, right, other, got, reverse, after):
    lefts = left if isinstance(left, list) else [left]
    tokens, half, count = right.shape[0], cut.nr // 2, cut.nc // 2
    block = (half, cut.shards, cut.r, cut.c)
    here = lambda i, s: (i, 0, 0, 0)
    if other:
        specs, sizes = [pl.BlockSpec(block, here)], [cut.replicas // 2]
    elif cut.nc == 1:
        specs, sizes = [pl.BlockSpec((half // 2,) + block[1:], here)] * 2, [cut.replicas // 4] * 2
    else:
        specs = [
            pl.BlockSpec(block, lambda i, s: (jnp.minimum(i, count - 1), 0, 0, 0)),
            pl.BlockSpec(block, lambda i, s: (jnp.maximum(i - count, 0), 0, 0, 0)),
        ]
        sizes = [cut.replicas // 4] * 2
    return pl.pallas_call(
        functools.partial(wide_kernel, cut, other, reverse, len(lefts)),
        grid_spec=pltpu.PrefetchScalarGridSpec(
            num_scalar_prefetch=1,
            grid=(cut.nc,),
            in_specs=[
                pl.BlockSpec(
                    (tokens, cut.c), lambda i, s: (0, jnp.bitwise_xor(lax.div(s[0], 2 * half), i))
                ),
            ]
            + [pl.BlockSpec(a.shape, lambda i, s: (0, 0)) for a in lefts]
            + [pl.BlockSpec(block, here)] * len(got)
            + [ANY_SPEC] * len(after),
            out_specs=specs + [pl.BlockSpec((8, 128), lambda i, s: (0, 0))],
            scratch_shapes=[
                pltpu.VMEM((tokens, cut.shards * cut.rows // 2), BF),
                pltpu.VMEM((cut.shards * cut.rows // 2, tokens), BF),
                pltpu.VMEM((cut.shards * cut.rows // 2, cut.c), F32),
            ],
        ),
        out_shape=[jax.ShapeDtypeStruct((n, cut.shards, cut.r, cut.c), BF) for n in sizes] + [MARK],
        compiler_params=pltpu.CompilerParams(vmem_limit_bytes=56 * MIB),
        cost_estimate=cost(6),
    )(place, right, *lefts, *got, *after)


def half_spots(cut, me):
    half = cut.nr // 2
    for m in range(cut.replicas // 2):
        chip = jnp.bitwise_xor(lax.div(me, 2), m)
        row = pl.multiple_of(lax.rem(chip, half) * cut.r, 8 if cut.r % 16 else 16)
        column = pl.multiple_of(lax.div(chip, half) * cut.c, 128)
        yield m, (pl.ds(row, cut.r), pl.ds(column, cut.c))


def send_grad_kernel(cut, place, left, right, *refs):
    send, mark, whole = refs[-3:]
    mark[...] = jnp.zeros_like(mark)
    whole[...] = lax.dot_general(
        left[...], right[...], (((0,), (0,)), ((), ())), preferred_element_type=F32
    )
    for m, spot in half_spots(cut, place[0]):
        send[m, 0] = rnd(whole[spot])


def keep_grad_kernel(cut, reverse, place, left, right, got, *refs):
    stay, go, mark, whole = refs[-4:]
    mark[...] = jnp.zeros_like(mark)
    whole[...] = lax.dot_general(
        left[...], right[...], (((0,), (0,)), ((), ())), preferred_element_type=F32
    )
    count = cut.replicas // 4
    for m, spot in half_spots(cut, place[0]):
        leaves, n = (m >= count, m % count) if reverse else (m % 2 == 1, m // 2)
        (go if leaves else stay)[n, 0] = rnd(whole[spot] + got[m, 0].astype(F32))


def half_grad(kernel, cut, place, left, right, other, slots, results, after):
    tokens, shards = left.shape[0], cut.shards
    pick = lambda d, s: (
        0,
        lax.rem(s[1] + shards - d, shards) * 2 + lax.rem(s[0] + other, 2),
    )
    piece = lambda count: pl.BlockSpec((count, 1, cut.r, cut.c), lambda d, s: (0, d, 0, 0))
    return pl.pallas_call(
        kernel,
        grid_spec=pltpu.PrefetchScalarGridSpec(
            num_scalar_prefetch=1,
            grid=(shards,),
            in_specs=[
                pl.BlockSpec((tokens, cut.rows // 2), pick),
                pl.BlockSpec(right.shape, lambda d, s: (0, 0)),
            ]
            + [piece(a.shape[0]) for a in slots]
            + [ANY_SPEC] * len(after),
            out_specs=[piece(n) for n in results] + [pl.BlockSpec((8, 128), lambda d, s: (0, 0))],
            scratch_shapes=[pltpu.VMEM((cut.rows // 2, cut.columns), F32)],
        ),
        out_shape=[jax.ShapeDtypeStruct((n, shards, cut.r, cut.c), BF) for n in results] + [MARK],
        compiler_params=pltpu.CompilerParams(vmem_limit_bytes=56 * MIB),
        cost_estimate=cost(7.5),
    )(place, left, right, *slots, *after)


def send_grad(cut, place, left, right, after=()):
    if cut.rows <= 256:
        return wide_grad(cut, place, left, right, 1, (), False, after)
    kernel = functools.partial(send_grad_kernel, cut)
    return half_grad(kernel, cut, place, left, right, 1, (), (cut.replicas // 2,), after)


def keep_grad(cut, place, left, right, got, reverse, after=()):
    if cut.rows <= 256:
        return wide_grad(cut, place, left, right, 0, (got,), reverse, after)
    kernel = functools.partial(keep_grad_kernel, cut, reverse)
    return half_grad(kernel, cut, place, left, right, 0, (got,), (cut.replicas // 4,) * 2, after)


def qkv_grad_kernel(slim, replicas, shards, place, dq, dk, dv, small, *refs):
    keep, send, mark, whole = refs[-4:]
    blocks = refs[:shards]
    rows = blocks[0].shape[0]
    mark[...] = jnp.zeros_like(mark)
    local = dq.shape[1]
    for n, right in enumerate((dq, dk, dv)):
        total = jnp.zeros((whole.shape[0], local), F32)
        for d in range(shards):
            at = pl.ds(pl.multiple_of(lax.rem(place[1] + shards - d, shards) * rows, 16), rows)
            total += lax.dot_general(
                blocks[d][...], right[at, :], (((0,), (0,)), ((), ())), preferred_element_type=F32
            )
        whole[:, n * local : (n + 1) * local] = total
    first = lax.broadcasted_iota(jnp.int32, (16, 3 * local), 0) == 0
    for j in range(replicas):
        piece = jnp.bitwise_xor(place[0], j)
        out = (keep, send)[j & 1]
        out[j >> 1, 0, 0:slim] = rnd(whole[pl.ds(pl.multiple_of(piece * slim, 8), slim), :])
        out[j >> 1, 0, slim:] = rnd(jnp.where(first, small[0, pl.ds(piece, 1), :], 0.0))


def qkv_grad(place, hiddens, dq, dk, dv, small, slim, shards, after):
    replicas, (tokens, local) = small.shape[1], dq.shape
    rows, width = slim * replicas, 3 * local
    here = pl.BlockSpec((tokens, local), lambda f, s: (0, 0))
    piece = pl.BlockSpec((replicas // 2, 1, slim + 16, width), lambda f, s: (0, f, 0, 0))
    return pl.pallas_call(
        functools.partial(qkv_grad_kernel, slim, replicas, shards),
        grid_spec=pltpu.PrefetchScalarGridSpec(
            num_scalar_prefetch=1,
            grid=(shards,),
            in_specs=[here, here, here]
            + [pl.BlockSpec((1, replicas, width), lambda f, s: (f, 0, 0))]
            + [pl.BlockSpec((tokens // shards, rows), lambda f, s: (0, f))] * shards
            + [ANY_SPEC] * len(after),
            out_specs=[piece] * 2 + [pl.BlockSpec((8, 128), lambda f, s: (0, 0))],
            scratch_shapes=[pltpu.VMEM((rows, width), F32)],
        ),
        out_shape=[jax.ShapeDtypeStruct((replicas // 2, shards, slim + 16, width), BF)] * 2 + [MARK],
        compiler_params=pltpu.CompilerParams(vmem_limit_bytes=48 * MIB),
        cost_estimate=cost(6.5),
    )(place, dq, dk, dv, small, *hiddens, *after)


def widen_kernel(cuts, qkv_rows, place, own_a, other_a, own_b, other_b, w_out, w_up, w_down, w_qkv, small):
    cut_out, cut_up, cut_down = cuts
    width = own_a.shape[2]
    for j in range(cut_out.replicas):
        piece = jnp.bitwise_xor(place[0], j)
        left, right, m = (own_a, own_b, j >> 1) if j % 2 == 0 else (other_a, other_b, j >> 1)
        row = cut_out.r
        w_out[cut_out.spot(piece)] = left[m, 0:row].astype(F32)
        w_up[cut_up.spot(piece)] = left[m, row : row + cut_up.r].astype(F32)
        row += cut_up.r
        spot = pl.ds(pl.multiple_of(piece * 8, 8), 8)
        small[spot, :] = left[m, row : row + 8].astype(F32)
        above, below = row + 16, cut_down.r
        w_down[cut_down.spot(piece)] = right[m, 0:below].astype(F32)
        spot = pl.ds(pl.multiple_of(piece * qkv_rows, 8), qkv_rows)
        shards, local = cut_out.shards, width // cut_out.shards
        for k in range(3):
            for d in range(shards):
                column = k * width + lax.rem(place[1] + shards - d, shards) * local
                source, row = (right, below + (k - 1) * qkv_rows) if k else (left, above)
                part = source[m, row : row + qkv_rows, d * local : (d + 1) * local].astype(F32)
                w_qkv[spot, pl.ds(pl.multiple_of(column, 128), local)] = part


def widen(cuts, qkv_rows, place, own_a, other_a, own_b, other_b):
    width = own_a.shape[2]
    shapes = [(cut.rows, cut.columns) for cut in cuts]
    shapes += [(qkv_rows * cuts[0].replicas, 3 * width), (8 * cuts[0].replicas, width)]
    return pl.pallas_call(
        functools.partial(widen_kernel, cuts, qkv_rows),
        in_specs=[SMEM_SPEC] + [VMEM_SPEC] * 4,
        out_specs=[VMEM_SPEC] * 5,
        out_shape=[jax.ShapeDtypeStruct(shape, F32) for shape in shapes],
        compiler_params=pltpu.CompilerParams(vmem_limit_bytes=48 * MIB),
        cost_estimate=cost(7),
    )(place, own_a, other_a, own_b, other_b)


def hidden_grad_kernel(place, block, dq, dk, dv, weight, *refs):
    out, sums = refs[-2:]
    local = dq.shape[1]
    grad = dot_last(dq[...], weight[:, 0:local])
    grad += dot_last(dk[...], weight[:, local : 2 * local])
    grad += dot_last(dv[...], weight[:, 2 * local :])
    out[...] = rnd(grad)
    normal, _ = moments(block[...].astype(F32))
    sums[0:1, :] = jnp.sum(grad * normal, 0, keepdims=True)
    sums[1:2, :] = jnp.sum(grad, 0, keepdims=True)
    sums[2:8, :] = jnp.zeros((6, sums.shape[1]), F32)


def hidden_grad(place, block, dq, dk, dv, weight, distance, shards, after=()):
    rows, width = block.shape
    local = dq.shape[1]
    at = lambda i, s: (lax.rem(s[1] + shards - distance, shards), 0)
    here = lambda i, s: (0, 0)
    return pl.pallas_call(
        hidden_grad_kernel,
        grid_spec=pltpu.PrefetchScalarGridSpec(
            num_scalar_prefetch=1,
            grid=(1,),
            in_specs=[pl.BlockSpec((rows, width), here)]
            + [pl.BlockSpec((rows, local), at)] * 3
            + [pl.BlockSpec(weight.shape, here)]
            + [ANY_SPEC] * len(after),
            out_specs=[pl.BlockSpec((rows, width), here), pl.BlockSpec((8, width), here)],
        ),
        out_shape=[jax.ShapeDtypeStruct((rows, width), BF), jax.ShapeDtypeStruct((8, width), F32)],
        compiler_params=pltpu.CompilerParams(vmem_limit_bytes=40 * MIB),
        cost_estimate=cost(3),
    )(place, block, dq, dk, dv, weight, *after)


def last_kernel(tokens, travel, own, dx2, gain, out, mark):
    mark[...] = jnp.zeros_like(mark)
    normal, scale = moments(tokens[...].astype(F32))
    grad = travel[...].astype(F32) + own[...].astype(F32)
    out[...] = rnd(dx2[...] + norm_grad(grad, gain[...], normal, scale))


def last(tokens, travel, own, dx2, gain):
    return pl.pallas_call(
        last_kernel,
        in_specs=[VMEM_SPEC] * 5,
        out_specs=[VMEM_SPEC] * 2,
        out_shape=[jax.ShapeDtypeStruct(tokens.shape, BF), MARK],
        compiler_params=pltpu.CompilerParams(vmem_limit_bytes=40 * MIB),
        cost_estimate=cost(2.5),
    )(tokens, travel, own, dx2, gain)


def swap(value, bit, replicas):
    return lax.ppermute(value, "dp", [(i, i ^ bit) for i in range(replicas)])


def around(value, shards):
    blocks = {0: value}
    for d in range(1, shards // 2 + 1):
        blocks[d] = turn(blocks[d - 1], shards)
        if shards - d not in blocks:
            blocks[shards - d] = turn(blocks[(shards - d + 1) % shards], shards, shards - 1)
    return blocks


def turn(value, shards, step=1):
    return lax.ppermute(value, "fsdp", [(i, (i + step) % shards) for i in range(shards)])


def chip_bits(replicas, reverse):
    bits = [1 << n for n in range(1, replicas.bit_length() - 1)]
    return bits[::-1] if reverse else bits


def share_chips(piece, replicas, reverse=False, pause=lambda part: part):
    parts = {0: piece}
    for n, bit in enumerate(chip_bits(replicas, reverse)):
        more = {m | bit: swap(part, bit, replicas) for m, part in parts.items()}
        parts |= {m: part if n else pause(part) for m, part in more.items()}
    return [parts[2 * m] for m in range(replicas // 2)]


def share_both(upper, lower, replicas):
    first, second = {0: upper}, {0: lower}
    for one, two in zip(chip_bits(replicas, False), chip_bits(replicas, True)):
        more = {m | one: swap(part, one, replicas) for m, part in first.items()}
        even = {m | two: swap(part, two, replicas) for m, part in second.items()}
        if len(first) == 1 and replicas > 4:
            more = {m: gate(part, *even.values()) for m, part in more.items()}
            even = {m: gate(part, *more.values()) for m, part in even.items()}
        first |= more
        second |= even
    slots = [2 * m for m in range(replicas // 2)]
    return jnp.stack([first[m] for m in slots]), jnp.stack([second[m] for m in slots])


def share(piece, replicas, reverse=False, pause=lambda part: part):
    slots = []
    for part in share_chips(piece, replicas, reverse, pause):
        slots += [part, swap(part, 1, replicas)]
    return slots


def idle_kernel(*refs):
    pass


def gate(value, *after):
    return pl.pallas_call(
        idle_kernel,
        in_specs=[ANY_SPEC] * (1 + len(after)),
        out_specs=ANY_SPEC,
        out_shape=jax.ShapeDtypeStruct(value.shape, value.dtype),
        input_output_aliases={0: 0},
        cost_estimate=cost(0),
    )(value, *after)


def add_low(left, right):
    return rnd(left.astype(F32) + right.astype(F32))


def fold_kernel(left_stay, right_stay, left_go, right_go, *refs):
    stay, go, mark = refs[-3:]
    stay[...] = add_low(left_stay[...], right_stay[...])
    go[...] = add_low(left_go[...], right_go[...])
    mark[...] = jnp.zeros_like(mark)


def fold(left, right, reverse, after=()):
    n, shards, r, c = left.shape
    deep = shards if r * c < 2**16 else 1
    stay = lambda i, d: (i if reverse else 2 * i, d, 0, 0)
    go = lambda i, d: (i + n // 2 if reverse else 2 * i + 1, d, 0, 0)
    block = (1, deep, r, c)
    return pl.pallas_call(
        fold_kernel,
        grid=(n // 2, shards // deep),
        in_specs=[pl.BlockSpec(block, stay)] * 2 + [pl.BlockSpec(block, go)] * 2 + [ANY_SPEC] * len(after),
        out_specs=[pl.BlockSpec(block, lambda i, d: (i, d, 0, 0))] * 2
        + [pl.BlockSpec((8, 128), lambda i, d: (0, 0))],
        out_shape=[jax.ShapeDtypeStruct((n // 2, shards, r, c), BF)] * 2 + [MARK],
        compiler_params=pltpu.CompilerParams(vmem_limit_bytes=32 * MIB),
        cost_estimate=cost(3),
    )(left, right, left, right, *after)


def close_kernel(counts, *refs):
    total, first, mark = refs[-3:]
    mark[...] = jnp.zeros_like(mark)
    row = n = 0
    for count in counts:
        value = refs[n][0, 0].astype(F32)
        for m in range(1, count):
            value += refs[n + m][0, 0].astype(F32)
        value = rnd(value)
        n += count
        rows = pl.ds(row, value.shape[0])
        total[0, rows, :] = value

        @pl.when(pl.program_id(0) == min(1, pl.num_programs(0) - 1))
        def _():
            first[rows, :] = value

        row += value.shape[0]


def close(groups, after=()):
    _, shards, _, c = groups[0][0].shape
    height = sum(group[0].shape[2] for group in groups)
    flat = [a for group in groups for a in group]
    return pl.pallas_call(
        functools.partial(close_kernel, [len(group) for group in groups]),
        grid=(shards,),
        in_specs=[pl.BlockSpec((1, 1) + a.shape[2:], lambda d: (0, d, 0, 0)) for a in flat]
        + [ANY_SPEC] * len(after),
        out_specs=[
            pl.BlockSpec((1, height, c), lambda d: (d, 0, 0)),
            pl.BlockSpec((height, c), lambda d: (0, 0)),
            pl.BlockSpec((8, 128), lambda d: (0, 0)),
        ],
        out_shape=[
            jax.ShapeDtypeStruct((shards, height, c), BF),
            jax.ShapeDtypeStruct((height, c), BF),
            MARK,
        ],
        compiler_params=pltpu.CompilerParams(vmem_limit_bytes=32 * MIB),
        cost_estimate=cost(3),
    )(*flat, *after)


def close_parts_kernel(count, *refs):
    value = refs[0][...].astype(F32)
    for m in range(1, count):
        value += refs[m][...].astype(F32)
    refs[-2][...] = rnd(value)
    refs[-1][...] = jnp.zeros_like(refs[-1])


def close_parts(parts, after=()):
    return pl.pallas_call(
        functools.partial(close_parts_kernel, len(parts)),
        in_specs=[VMEM_SPEC] * len(parts) + [ANY_SPEC] * len(after),
        out_specs=[VMEM_SPEC] * 2,
        out_shape=[jax.ShapeDtypeStruct(parts[0].shape, BF), MARK],
        compiler_params=pltpu.CompilerParams(vmem_limit_bytes=32 * MIB),
        cost_estimate=cost(1),
    )(*parts, *after)


def join_kernel(travel, part, *refs):
    total, mark = refs[-2:]
    total[...] = add_low(travel[...], part[0])
    mark[...] = jnp.zeros_like(mark)


def join(travel, parts, d, after=()):
    r, c = travel.shape
    return pl.pallas_call(
        join_kernel,
        grid=(1,),
        in_specs=[
            pl.BlockSpec((r, c), lambda i: (0, 0)),
            pl.BlockSpec((1, r, c), lambda i: (d, 0, 0)),
        ]
        + [ANY_SPEC] * len(after),
        out_specs=[pl.BlockSpec((r, c), lambda i: (0, 0)), pl.BlockSpec((8, 128), lambda i: (0, 0))],
        out_shape=[jax.ShapeDtypeStruct((r, c), BF), MARK],
        compiler_params=pltpu.CompilerParams(vmem_limit_bytes=32 * MIB),
        cost_estimate=cost(1),
    )(travel, parts, *after)


def direct(parts, replicas):
    return [part if m == 0 else swap(part, 2 * m, replicas) for m, part in enumerate(parts)]


def spread_kernel(left, right, *refs):
    count = left.shape[0]
    for m in range(count):
        refs[-1 - count + m][...] = add_low(left[m], right[m])
    refs[-1][...] = jnp.zeros_like(refs[-1])


def spread(left, right, after=()):
    n, shards, r, c = left.shape
    block = pl.BlockSpec((n, 1, r, c), lambda d: (0, d, 0, 0))
    part = pl.BlockSpec((1, r, c), lambda d: (d, 0, 0))
    return pl.pallas_call(
        spread_kernel,
        grid=(shards,),
        in_specs=[block] * 2 + [ANY_SPEC] * len(after),
        out_specs=[part] * n + [pl.BlockSpec((8, 128), lambda d: (0, 0))],
        out_shape=[jax.ShapeDtypeStruct((shards, r, c), BF)] * n + [MARK],
        compiler_params=pltpu.CompilerParams(vmem_limit_bytes=32 * MIB),
        cost_estimate=cost(3),
    )(left, right, *after)


def gather_sum_kernel(count, place, *refs):
    value = refs[0][...].astype(F32)
    for m in range(1, count):
        value += refs[m][...].astype(F32)
    refs[-2][...] = rnd(value)
    refs[-1][...] = jnp.zeros_like(refs[-1])


def gather_sum(place, parts, after=()):
    shards, r, c = parts[0].shape
    return pl.pallas_call(
        functools.partial(gather_sum_kernel, len(parts)),
        grid_spec=pltpu.PrefetchScalarGridSpec(
            num_scalar_prefetch=1,
            grid=(shards,),
            in_specs=[pl.BlockSpec((1, r, c), lambda d, s: (lax.rem(s[1] + d, shards), 0, 0))] * len(parts)
            + [ANY_SPEC] * len(after),
            out_specs=[
                pl.BlockSpec((1, r, c), lambda d, s: (d, 0, 0)),
                pl.BlockSpec((8, 128), lambda d, s: (0, 0)),
            ],
        ),
        out_shape=[jax.ShapeDtypeStruct((shards, r, c), BF), MARK],
        compiler_params=pltpu.CompilerParams(vmem_limit_bytes=32 * MIB),
        cost_estimate=cost(2),
    )(place, *parts, *after)


class Scatter:
    def __init__(self, keep, send, replicas, reverse, first=0):
        self.replicas, self.reverse = replicas, reverse
        self.bits = chip_bits(replicas, reverse)
        bit = self.bits.pop(0) if first else 1
        self.pair = (keep, swap(send, bit, replicas))

    def step(self, mark):
        keep, go, mark = fold(*self.pair, self.reverse, (mark,))
        self.pair = (keep, swap(go, self.bits.pop(0), self.replicas))
        return mark


def flip_by(value, axis, me, replicas):
    shape = value.shape
    bits = replicas.bit_length() - 1
    value = value.reshape(shape[:axis] + (2,) * bits + shape[axis + 1 :])
    for n in range(bits):
        where = axis + bits - 1 - n
        value = jnp.where((me >> n) & 1 == 1, jnp.flip(value, where), value)
    return value.reshape(shape)


def window_low(lengths, group_len):
    prompt = group_len // 2
    order = jnp.arange(lengths.shape[0], dtype=jnp.int32)
    ends = jnp.sum(jnp.where(order[:, None] <= order[None, :], lengths[:, None], 0), 0)
    pos = jnp.arange(prompt, dtype=jnp.int32)
    starts = jnp.max(jnp.where(ends[:, None] <= pos[None, :], ends[:, None], 0), 0)
    return jnp.concatenate([jnp.zeros((prompt,), jnp.int32), prompt + starts])[None]


def body(
    tokens,
    cotangent,
    cont_lengths,
    ln1_gain,
    ln1_bias,
    w_qkv,
    q_bias,
    v_bias,
    w_out,
    out_bias,
    ln2_gain,
    ln2_bias,
    w_up,
    up_bias,
    w_down,
    down_bias,
):
    rows, width = tokens.shape
    shards, replicas = lax.axis_size("fsdp"), lax.axis_size("dp")
    z, me = lax.axis_index("fsdp"), lax.axis_index("dp")
    place = jnp.stack([me, z]).astype(jnp.int32)
    group_len = rows * shards
    head_dim = width // H
    local = width // shards
    hidden = w_up.shape[2]
    w_qkv, w_out, w_up, w_down = w_qkv[0], w_out[0], w_up[0], w_down[0]
    cut_out = Cut(w_out.shape[0], width, 1, replicas, shards)
    cut_up = Cut(w_up.shape[0], hidden, hidden // width, replicas, shards)
    cut_down = Cut(w_down.shape[0], width, 1, replicas, shards)
    cuts = (cut_out, cut_up, cut_down)

    vectors = (ln1_gain, ln1_bias, q_bias, v_bias, out_bias, ln2_gain, ln2_bias, down_bias, up_bias)
    packed = jnp.concatenate(vectors, 1)
    slim = w_qkv.shape[0] // replicas
    mine = lax.dynamic_slice_in_dim(w_qkv, me * slim, slim, 0)
    mine = mine.reshape(slim, 3, shards, local).transpose(2, 0, 1, 3).reshape(shards, slim, 3 * local)
    turned = [packed] + [turn(packed, shards, step) for step in range(shards - 1, 0, -1)]
    turned = jnp.concatenate(turned + turned, 0)
    packed_all = lax.dynamic_slice_in_dim(turned, lax.rem(shards - z, shards), shards)
    full = []
    offset = 0
    for vector in vectors:
        size = vector.shape[1]
        full.append(packed_all[:, offset : offset + size].reshape(1, shards * size).astype(F32))
        offset += size
    gain_one, bias_one, _, _, bias_out, gain_two, bias_two, bias_down, bias_up = full
    middle_vectors = jnp.concatenate([bias_out, gain_two, bias_two, bias_down] * 2, 0)
    start_at = z * local
    bias_q = lax.dynamic_slice_in_dim(full[2], start_at, local, 1)
    bias_v = lax.dynamic_slice_in_dim(full[3], start_at, local, 1)
    bias_qkv = jnp.concatenate([bias_q, jnp.zeros_like(bias_q), bias_v], 1)

    piece = jnp.concatenate(
        [cut.of(shard, me) for cut, shard in ((cut_out, w_out), (cut_up, w_up), (cut_down, w_down))], 0
    )
    piece = gate(piece, mine)
    slots = around(piece, shards)
    near = (slots[1], slots[shards - 1])
    blocks = around(gate(tokens, packed, *near), shards)
    mine = gate(lax.all_to_all(mine, "fsdp", 0, 0, tiled=True), *near)
    weight_qkv = flip_by(jnp.stack(share(mine, replicas)), 0, me, replicas)
    weight_qkv = weight_qkv.transpose(1, 0, 2, 3).reshape(width, 3 * local)

    hiddens = [None] * shards
    combined = jnp.zeros((group_len, 3 * local), BF)
    for d in [0] + sorted(range(1, shards), key=lambda d: min(d, shards - d)):
        if d == shards // 2:
            early = mark
        hiddens[d], combined, mark = project(
            place, blocks[d], gain_one, bias_one, weight_qkv, bias_qkv, combined, d, shards
        )

    edge = cut_out.r + cut_up.r
    slots = [gate(slots[d], early) for d in range(1, shards)]
    upper = jnp.stack([slot[:edge] for slot in slots])
    lower = jnp.stack([slot[edge:] for slot in slots])

    low = window_low(cont_lengths[0], group_len)
    mixed, lse = attend(combined, low, head_dim)
    attended = [
        lax.dynamic_slice_in_dim(mixed, lax.rem(z + d, shards) * rows, rows) for d in range(shards)
    ]
    attended = [turn(block, shards, d) if d else block for d, block in enumerate(attended)]
    pause = lambda part: gate(part, mark)
    lists = share(upper, replicas, False, pause) + share(lower, replicas, True, pause)
    lists += [w_out, w_up, w_down]
    output, hidden_two, middle, acted, slope = feed_forward(
        place, attended, tokens, middle_vectors, bias_up, cuts, lists
    )

    dm = cotangent
    du, dx2, da, do, grad_bias_up, sums = feed_backward(
        place, dm, slope, middle, middle_vectors, cuts, lists
    )
    grad_mixed = lax.all_to_all(do, "fsdp", 1, 0, tiled=True)
    terms = ((cut_down, acted, dm, False), (cut_up, hidden_two, du, True), (cut_out, attended, da, False))
    mark = grad_bias_up
    scatters = []
    if all(cut.rows % 256 == 0 for cut in cuts):
        gots = []
        for cut, left, right, _ in terms:
            send, mark = send_grad(cut, place, left, right, (mark,) if gots else ())
            gots.append(swap(send, 1, replicas))
        for (cut, left, right, reverse), got in zip(terms, gots):
            stay, go, mark = keep_grad(cut, place, left, right, got, reverse, (mark,))
            if cut is cut_out:
                halves = (stay, go)
                out = [halves[m % 2][m // 2 : m // 2 + 1] for m in range(replicas // 2)]
            else:
                scatters.append(Scatter(stay, go, replicas, reverse, True))
    else:
        turned = [attended[-d % shards] for d in range(shards)] * 2
        joined = lax.dynamic_slice_in_dim(
            jnp.concatenate(turned, 1), lax.rem(shards - z, shards) * local, width, 1
        )
        for cut, left, right, reverse in terms:
            left = joined if left is attended else left
            keep, send, mark = weight_grad(cut, place, left, right, (mark,))
            if cut is cut_out:
                *out, mark = spread(keep, swap(send, 1, replicas), (mark,))
                out = [part[None] for part in out]
            else:
                scatters.append(Scatter(keep, send, replicas, reverse))
        for scatter in scatters:
            mark = scatter.step(mark)
    down, up = scatters
    out = direct(out, replicas)

    dq, dk, dv, bias_sums = attend_grad(combined, low, mixed, lse, grad_mixed, head_dim, (mark,))
    parts = {}
    parts[1 % shards], first_sums = hidden_grad(place, blocks[1 % shards], dq, dk, dv, weight_qkv, 1, shards)
    travel = turn(parts[1 % shards], shards)
    mark = first_sums
    while down.bits:
        mark = down.step(mark)
        mark = up.step(mark)
    out, mark = close_parts(out, (mark,))
    others = list(range(2, shards))
    for d in [*others, 0]:
        parts[d], mark = hidden_grad(
            place, blocks[d], dq, dk, dv, weight_qkv, d, shards, (mark,)
        )
        first_sums += mark
        if d == 2:
            step, mark = join(travel, parts[d][None], 0, (mark,))
            travel = turn(step, shards)

    blank = jnp.zeros((width,), F32)
    grad_bias_q = lax.dynamic_update_slice(blank, bias_sums[:, 0].reshape(-1), (start_at,))
    grad_bias_v = lax.dynamic_update_slice(blank, bias_sums[:, 1].reshape(-1), (start_at,))
    small = (
        first_sums[0],
        first_sums[1],
        grad_bias_q,
        grad_bias_v,
        sums[3],
        sums[1],
        sums[2],
        sums[0],
        grad_bias_up,
    )
    small = jnp.concatenate([g.reshape(shards, -1) for g in small], 1)
    count = small.shape[1] // replicas
    small = small.reshape(shards, replicas, count)
    small = jnp.pad(small, ((0, 0), (0, 0), (0, 3 * local - count)))
    keep, send, mark = qkv_grad(place, hiddens, dq, dk, dv, small, slim, shards, (mark,))
    got = swap(send, 1, replicas)

    late = None
    if others[1:]:
        late, mark = join(travel, parts[others[1]][None], 0, (mark,))
    sums_all, first, mark = close(([out], up.pair, down.pair), (mark,))
    ring = turn(first, shards)
    *qkv, mark = spread(keep, got, (mark,))
    qkv = direct(qkv, replicas)
    come = None
    for d in range(2, shards + 1):
        total, mark = join(ring, sums_all, d % shards, (mark,))
        if d < shards:
            ring = turn(total, shards)
        if come is None:
            piece, mark = gather_sum(place, qkv, (mark,))
            come = [piece[0]] + [turn(piece[e], shards, e) for e in range(1, shards)]
    if late is not None:
        travel = turn(gate(late, mark), shards)
    for d in others[2:]:
        step, mark = join(travel, parts[d][None], 0, (mark,))
        travel = turn(step, shards)
    input_grad, last_mark = last(tokens, travel, parts[0], dx2, gain_one)
    rows_qkv = jnp.concatenate(
        [
            jnp.concatenate([block[:slim, k * local : (k + 1) * local] for block in come], 1)
            for k in range(3)
        ],
        0,
    )
    row_small = rnd(sum(block[slim, :count].astype(F32) for block in come))
    row_small = jnp.pad(row_small[None], ((0, 15), (0, width - count)))
    upper = jnp.concatenate([total[:edge], row_small, rows_qkv[:slim]], 0)
    lower = jnp.concatenate([total[edge:], rows_qkv[slim:]], 0)
    own_a, own_b = share_both(upper, lower, replicas)
    own_a, own_b = gate(own_a, last_mark), gate(own_b, last_mark)
    out_w_out, out_w_up, out_w_down, out_w_qkv, total = widen(
        cuts, slim, place, own_a, swap(own_a, 1, replicas), own_b, swap(own_b, 1, replicas)
    )
    total = total.reshape(replicas, 8, width)[:, 0, :count].reshape(1, -1)
    outs = []
    offset = 0
    for vector in vectors:
        outs.append(total[:, offset : offset + vector.shape[1]])
        offset += vector.shape[1]
    return (
        output,
        input_grad,
        outs[0],
        outs[1],
        out_w_qkv[None],
        outs[2],
        outs[3],
        out_w_out[None],
        outs[4],
        outs[5],
        outs[6],
        out_w_up[None],
        outs[8],
        out_w_down[None],
        outs[7],
    )


def solution(mesh):
    vec = P(None, "fsdp")
    mat = P(None, "fsdp", None)
    tok = P(("dp", "fsdp"), None)
    in_specs = (tok, tok, P("dp", None), vec, vec, mat, vec, vec, mat, vec, vec, vec, mat, vec, mat, vec)
    out_specs = (tok, tok, vec, vec, mat, vec, vec, mat, vec, vec, vec, mat, vec, mat, vec)
    return jax.shard_map(body, mesh=mesh, in_specs=in_specs, out_specs=out_specs, check_vma=False)
```

```python
import functools

import jax
import jax.numpy as jnp
from jax import lax
from jax.experimental import pallas as pl
from jax.experimental.pallas import tpu as pltpu
from jax.sharding import PartitionSpec as P

H = 16
EPSILON = 1e-05
NEG_LARGE = -1e30
F32 = jnp.float32
BF = jnp.bfloat16
MIB = 2**20
COST_UNIT = 10**8


def rnd(v):
    return v.astype(BF)


def cost(time):
    return pl.CostEstimate(flops=int(time * COST_UNIT), bytes_accessed=1, transcendentals=0)


def dot_last(left, right):
    return lax.dot_general(left, right, (((1,), (1,)), ((), ())), preferred_element_type=F32)


def dot_mm(left, right):
    return jnp.dot(left, right, preferred_element_type=F32)


def key_ranges(start, group_len):
    prompt = group_len // 2
    if start < prompt:
        return start, start
    return prompt, max(prompt, start - group_len // 8)


def allowed_mask(shape, key_start, query_start, low_row):
    key_pos = lax.broadcasted_iota(jnp.int32, shape, 0) + key_start
    query_pos = lax.broadcasted_iota(jnp.int32, shape, 1) + query_start
    return (key_pos <= query_pos) & (key_pos >= low_row)


def attend_kernel(group_len, head_dim, q_ref, k_ref, v_ref, low_ref, o_ref, lse_ref):
    size = min(512, group_len // 4)
    scale = jnp.asarray(head_dim**-0.5, BF)
    values_t = v_ref[...].astype(F32).T.astype(BF)
    for start in range(0, group_len, size):
        stop = start + size
        full, near = key_ranges(start, group_len)
        results = []
        for head in range(128 // head_dim):
            lanes = slice(head * head_dim, (head + 1) * head_dim)
            queries = q_ref[start:stop, lanes] * scale
            part = dot_last(k_ref[near:stop, lanes], queries)
            ok = allowed_mask(part.shape, near, start, low_ref[0:1, start:stop])
            part = jnp.where(ok, part, NEG_LARGE)
            top = jnp.max(part, 0, keepdims=True)
            if full:
                rest = dot_last(k_ref[0:full, lanes], queries)
                top = jnp.maximum(top, jnp.max(rest, 0, keepdims=True))
            part = jnp.exp(part - top)
            total = jnp.sum(part, 0, keepdims=True)
            mixed = dot_mm(values_t[lanes, near:stop], part.astype(BF))
            if full:
                rest = jnp.exp(rest - top)
                total += jnp.sum(rest, 0, keepdims=True)
                mixed += dot_mm(values_t[lanes, 0:full], rest.astype(BF))
            results.append(mixed * (1.0 / total))
            lse_ref[0, head : head + 1, start:stop] = top + jnp.log(total)
        o_ref[start:stop, :] = jnp.concatenate(results, 0).T.astype(BF)


def attend_grad_kernel(
    group_len, head_dim, q_ref, k_ref, v_ref, low_ref, o_ref, lse_ref, do_ref, *refs
):
    dq_ref, dk_ref, dv_ref, bias_ref, dk_sum, dv_sum = refs[-6:]
    bias = jnp.zeros((1, 128), F32)
    size = min(256, group_len // 8)
    scale = jnp.asarray(head_dim**-0.5, BF)
    keys_t = k_ref[...].astype(F32).T.astype(BF)
    dk_sum[...] = jnp.zeros_like(dk_sum)
    dv_sum[...] = jnp.zeros_like(dv_sum)
    for start in range(0, group_len, size):
        stop = start + size
        full, near = key_ranges(start, group_len)
        product_t = (do_ref[start:stop, :].astype(F32) * o_ref[start:stop, :].astype(F32)).T
        results = []
        for head in range(128 // head_dim):
            lanes = slice(head * head_dim, (head + 1) * head_dim)
            queries = q_ref[start:stop, lanes] * scale
            grads = do_ref[start:stop, lanes]
            delta = jnp.sum(product_t[lanes, :], 0, keepdims=True)
            lse = lse_ref[0, head : head + 1, start:stop]
            dq_t = jnp.zeros((head_dim, size), F32)
            for first, last, masked in ((near, stop, True), (0, full, False)):
                if first == last:
                    continue
                probs = jnp.exp(dot_last(k_ref[first:last, lanes], queries) - lse)
                if masked:
                    ok = allowed_mask(probs.shape, first, start, low_ref[0:1, start:stop])
                    probs = jnp.where(ok, probs, 0.0)
                grad_probs = dot_last(v_ref[first:last, lanes], grads)
                ds = (probs * (grad_probs - delta)).astype(BF)
                dv_sum[head, first:last, :] += dot_mm(probs.astype(BF), grads)
                dk_sum[head, first:last, :] += dot_mm(ds, queries)
                dq_t += dot_mm(keys_t[lanes, first:last], ds)
            results.append(dq_t * head_dim**-0.5)
        dq = jnp.concatenate(results, 0).T.astype(BF)
        dq_ref[start:stop, :] = dq
        bias += jnp.sum(dq.astype(F32), 0, keepdims=True)
    heads = range(128 // head_dim)
    dk_ref[...] = jnp.concatenate([dk_sum[head] for head in heads], 1).astype(BF)
    dv = jnp.concatenate([dv_sum[head] for head in heads], 1).astype(BF)
    dv_ref[...] = dv
    bias_ref[0, 0:1, :] = bias
    bias_ref[0, 1:2, :] = jnp.sum(dv.astype(F32), 0, keepdims=True)


def attend(combined, low, head_dim):
    group_len, width = combined.shape[0], combined.shape[1] // 3
    steps = width // 128
    heads = 128 // head_dim
    block = lambda offset: pl.BlockSpec((group_len, 128), lambda i: (0, offset + i))
    return pl.pallas_call(
        functools.partial(attend_kernel, group_len, head_dim),
        grid=(steps,),
        in_specs=[block(0), block(steps), block(2 * steps), pl.BlockSpec((1, group_len), lambda i: (0, 0))],
        out_specs=[block(0), pl.BlockSpec((1, heads, group_len), lambda i: (i, 0, 0))],
        out_shape=[
            jax.ShapeDtypeStruct((group_len, width), BF),
            jax.ShapeDtypeStruct((steps, heads, group_len), F32),
        ],
        compiler_params=pltpu.CompilerParams(vmem_limit_bytes=56 * MIB),
        cost_estimate=cost(18),
    )(combined, combined, combined, low)


def attend_grad(combined, low, mixed, lse, grad_mixed, head_dim, after=()):
    group_len, width = mixed.shape
    steps = width // 128
    heads = 128 // head_dim
    block = lambda offset: pl.BlockSpec((group_len, 128), lambda i: (0, offset + i))
    return pl.pallas_call(
        functools.partial(attend_grad_kernel, group_len, head_dim),
        grid=(steps,),
        in_specs=[
            block(0),
            block(steps),
            block(2 * steps),
            pl.BlockSpec((1, group_len), lambda i: (0, 0)),
            block(0),
            pl.BlockSpec((1, heads, group_len), lambda i: (i, 0, 0)),
            block(0),
        ]
        + [pl.BlockSpec(memory_space=pl.ANY)] * len(after),
        out_specs=[block(0)] * 3 + [pl.BlockSpec((1, 2, 128), lambda i: (i, 0, 0))],
        out_shape=[jax.ShapeDtypeStruct((group_len, width), BF)] * 3
        + [jax.ShapeDtypeStruct((steps, 2, 128), F32)],
        scratch_shapes=[pltpu.VMEM((heads, group_len, head_dim), F32)] * 2,
        compiler_params=pltpu.CompilerParams(vmem_limit_bytes=56 * MIB),
        cost_estimate=cost(28),
    )(combined, combined, combined, low, mixed, lse, grad_mixed, *after)


class Cut:
    def __init__(self, rows, columns, column_parts, replicas, shards):
        self.rows, self.columns, self.shards, self.replicas = rows, columns, shards, replicas
        self.nc, self.nr = column_parts, replicas // column_parts
        self.r, self.c = rows // self.nr, columns // self.nc

    def place(self, piece):
        half = self.nr // 2
        row = (lax.rem(piece, 2) * half + lax.rem(lax.div(piece, 2), half)) * self.r
        column = lax.div(piece, self.nr) * self.c
        return pl.multiple_of(row, 8 if self.r % 16 else 16), pl.multiple_of(column, 128)

    def spot(self, piece, base=0):
        row, column = self.place(piece)
        return pl.ds(base + row, self.r), pl.ds(column, self.c)

    def of(self, shard, piece):
        return lax.dynamic_slice(shard, self.place(piece), (self.r, self.c))

    @property
    def copies(self):
        return 1 + (self.shards - 1) * self.replicas


def fetch(cut, me, z, slots, first_row, shard, whole, sems):
    base = pl.multiple_of(z * cut.rows, 16)
    copies = [pltpu.make_async_copy(shard, whole.at[pl.ds(base, cut.rows), :], sems.at[0])]
    for d in range(1, cut.shards):
        base = pl.multiple_of(lax.rem(z + cut.shards - d, cut.shards) * cut.rows, 16)
        for j in range(cut.replicas):
            copies.append(
                pltpu.make_async_copy(
                    slots[j].at[d - 1, pl.ds(first_row, cut.r), :],
                    whole.at[cut.spot(jnp.bitwise_xor(me, j), base)],
                    sems.at[len(copies)],
                )
            )
    return copies


def loads_of(cuts, place, lists, wholes, sems):
    count = cuts[0].replicas
    both, down, shards = lists[:count], lists[count : 2 * count], lists[2 * count :]
    sources = ((both, 0), (both, cuts[0].r), (down, 0))
    return [
        fetch(cut, place[0], place[1], slots, row, shard, whole, sem)
        for cut, (slots, row), shard, whole, sem in zip(cuts, sources, shards, wholes, sems)
    ]


def start(copies):
    for copy in copies:
        copy.start()


def finish(copies):
    for copy in copies:
        copy.wait()


MARK = jax.ShapeDtypeStruct((8, 128), F32)
SMEM_SPEC = pl.BlockSpec(memory_space=pltpu.SMEM)
ANY_SPEC = pl.BlockSpec(memory_space=pl.ANY)
VMEM_SPEC = pl.BlockSpec(memory_space=pltpu.VMEM)


def moments(stream):
    mean = jnp.mean(stream, -1, keepdims=True)
    centered = stream - mean
    scale = lax.rsqrt(jnp.mean(centered * centered, -1, keepdims=True) + EPSILON)
    return centered * scale, scale


def norm_grad(grad_hidden, gain, normal, scale):
    t = grad_hidden * gain
    return scale * (
        t - jnp.mean(t, -1, keepdims=True) - normal * jnp.mean(t * normal, -1, keepdims=True)
    )


def project_kernel(place, block, gain, bias, weight, bias_qkv, c_in, h_out, c_out, mark):
    mark[...] = jnp.zeros_like(mark)
    normal, _ = moments(block[...].astype(F32))
    hidden = rnd(normal * gain[...] + bias[...])
    h_out[...] = hidden
    c_out[...] = rnd(dot_mm(hidden, weight[...]) + bias_qkv[...])


def project(place, block, gain, bias, weight, bias_qkv, c_all, distance, shards):
    rows, width = block.shape
    whole = lambda a: pl.BlockSpec(a.shape, lambda i, s: (0,) * a.ndim)
    at = lambda i, s: (lax.rem(s[1] + shards - distance, shards), 0)
    return pl.pallas_call(
        project_kernel,
        grid_spec=pltpu.PrefetchScalarGridSpec(
            num_scalar_prefetch=1,
            grid=(1,),
            in_specs=[whole(a) for a in (block, gain, bias, weight, bias_qkv)] + [ANY_SPEC],
            out_specs=[
                pl.BlockSpec((rows, width), lambda i, s: (0, 0)),
                pl.BlockSpec((rows, c_all.shape[1]), at),
                pl.BlockSpec((8, 128), lambda i, s: (0, 0)),
            ],
        ),
        out_shape=[jax.ShapeDtypeStruct(a.shape, BF) for a in (block, c_all)] + [MARK],
        input_output_aliases={6: 1},
        compiler_params=pltpu.CompilerParams(vmem_limit_bytes=40 * MIB),
        cost_estimate=cost(2.5),
    )(place, block, gain, bias, weight, bias_qkv, c_all)


GELU_A = 0.7978845608028654
GELU_B = 0.044715


def gelu_both(u):
    square = u * u
    s = 0.5 * jnp.tanh(u * (GELU_A + GELU_A * GELU_B * square)) + 0.5
    value = u * s
    return value, s + value * (1.0 - s) * (2.0 * GELU_A + 6.0 * GELU_A * GELU_B * square)


def feed_kernel(cuts, step, place, tokens, dm, vectors, bias_up, *refs):
    shards, count = cuts[0].shards, 2 * cuts[0].replicas + 3
    mixed, lists, refs = refs[:shards], refs[shards : shards + count], refs[shards + count :]
    out, hidden, acted, du, dx2, da, do, grad_up, sums, w_out, w_up, w_down, slope, *sems = refs
    loads = loads_of(cuts, place, lists, (w_out, w_up, w_down), sems)
    for copies in loads:
        start(copies)
    finish(loads[0])
    stream = tokens[...].astype(F32) + vectors[0:1, :]
    local = mixed[0].shape[1]
    for d in range(shards):
        at = pl.multiple_of(lax.rem(place[1] + shards - d, shards) * local, 16)
        stream += dot_mm(mixed[d][...], w_out[pl.ds(at, local), :])
    normal, scale = moments(stream)
    hidden[...] = rnd(normal * vectors[1:2, :] + vectors[2:3, :])
    total = vectors[3:4, :] + stream
    finish(loads[1])
    for block in range(0, w_up.shape[1], step):
        columns = slice(block, block + step)
        value, grad = gelu_both(dot_mm(hidden[...], w_up[:, columns]) + bias_up[:, columns])
        value = rnd(value)
        acted[:, columns] = value
        slope[:, columns] = rnd(grad)
        if block == 0:
            finish(loads[2])
        total += dot_mm(value, w_down[columns, :])
    out[...] = rnd(total)
    dh2 = jnp.zeros(stream.shape, F32)
    for block in range(0, w_up.shape[1], step):
        columns = slice(block, block + step)
        part = rnd(dot_last(dm[...], w_down[columns, :]) * slope[:, columns].astype(F32))
        du[:, columns] = part
        grad_up[:, columns] = jnp.sum(part.astype(F32), 0, keepdims=True)
        dh2 += dot_last(part, w_up[:, columns])
    incoming = dm[...].astype(F32)
    stream = incoming + norm_grad(dh2, vectors[1:2, :], normal, scale)
    dx2[...] = stream
    low = rnd(stream)
    da[...] = low
    do[...] = rnd(dot_last(low, w_out[...]))
    sums[0:1, :] = jnp.sum(incoming, 0, keepdims=True)
    sums[1:2, :] = jnp.sum(dh2 * normal, 0, keepdims=True)
    sums[2:3, :] = jnp.sum(dh2, 0, keepdims=True)
    sums[3:4, :] = jnp.sum(low.astype(F32), 0, keepdims=True)
    sums[4:8, :] = jnp.zeros((4, sums.shape[1]), F32)


def feed(place, mixed, tokens, dm, vectors, bias_up, cuts, lists):
    rows, width = tokens.shape
    hidden = bias_up.shape[1]
    shapes = [((rows, width), BF), ((rows, width), BF), ((rows, hidden), BF), ((rows, hidden), BF)]
    shapes += [((rows, width), F32), ((rows, width), BF), ((rows, width), BF)]
    shapes += [((1, hidden), F32), ((8, width), F32)]
    return pl.pallas_call(
        functools.partial(feed_kernel, cuts, min(1024, hidden)),
        in_specs=[SMEM_SPEC] + [VMEM_SPEC] * (4 + len(mixed)) + [ANY_SPEC] * len(lists),
        out_specs=[VMEM_SPEC] * len(shapes),
        out_shape=[jax.ShapeDtypeStruct(*shape) for shape in shapes],
        scratch_shapes=[
            pltpu.VMEM((width, width), BF),
            pltpu.VMEM((width, hidden), BF),
            pltpu.VMEM((hidden, width), BF),
            pltpu.VMEM((rows, hidden), BF),
        ]
        + [pltpu.SemaphoreType.DMA((cut.copies,)) for cut in cuts],
        compiler_params=pltpu.CompilerParams(vmem_limit_bytes=60 * MIB),
        cost_estimate=cost(40),
    )(place, tokens, dm, vectors, bias_up, *mixed, *lists)


def weight_grad_kernel(cut, place, left, right, *refs):
    keep, send, mark, whole = refs[-4:]
    mark[...] = jnp.zeros_like(mark)
    whole[...] = lax.dot_general(
        left[...], right[...], (((0,), (0,)), ((), ())), preferred_element_type=F32
    )
    for j in range(cut.replicas):
        value = whole[cut.spot(jnp.bitwise_xor(place[0], j))]
        (keep, send)[j & 1][j >> 1, 0] = rnd(value)


def weight_grad(cut, place, left, right, after=()):
    tokens, shards = left.shape[0], cut.shards
    shape = (cut.replicas // 2, shards, cut.r, cut.c)
    piece = pl.BlockSpec((cut.replicas // 2, 1, cut.r, cut.c), lambda d, s: (0, d, 0, 0))
    return pl.pallas_call(
        functools.partial(weight_grad_kernel, cut),
        grid_spec=pltpu.PrefetchScalarGridSpec(
            num_scalar_prefetch=1,
            grid=(shards,),
            in_specs=[
                pl.BlockSpec((tokens, cut.rows), lambda d, s: (0, lax.rem(s[1] + shards - d, shards))),
                pl.BlockSpec(right.shape, lambda d, s: (0, 0)),
            ]
            + [ANY_SPEC] * len(after),
            out_specs=[piece] * 2 + [pl.BlockSpec((8, 128), lambda d, s: (0, 0))],
            scratch_shapes=[pltpu.VMEM((cut.rows, cut.columns), F32)],
        ),
        out_shape=[jax.ShapeDtypeStruct(shape, BF)] * 2 + [MARK],
        compiler_params=pltpu.CompilerParams(vmem_limit_bytes=56 * MIB),
        cost_estimate=cost(10),
    )(place, left, right, *after)


def gather_rows(cut, place, other, lefts, rows):
    size = cut.rows // 2
    half = lax.rem(place[0] + other, 2) * size
    for d in range(cut.shards):
        if len(lefts) > 1:
            part = lefts[d][:, pl.ds(pl.multiple_of(half, 128), size)]
        else:
            column = lax.rem(place[1] + cut.shards - d, cut.shards) * cut.rows + half
            part = lefts[0][:, pl.ds(pl.multiple_of(column, 128), size)]
        rows[:, d * size : (d + 1) * size] = part


def wide_kernel(cut, other, reverse, count, place, right, *refs):
    lefts, refs = refs[:count], refs[count:]
    rows, turned, whole = refs[-3:]
    refs = refs[:-1]
    refs[-3][...] = jnp.zeros_like(refs[-3])
    step = pl.program_id(0)

    @pl.when(step == 0)
    def _():
        gather_rows(cut, place, other, lefts, rows)
        turned[...] = rows[...].astype(F32).T.astype(BF)

    whole[...] = dot_mm(turned[...], right[...])
    half, size = cut.nr // 2, cut.rows // 2
    chip = lax.rem(lax.div(place[0], 2), half)

    def part(n, d):
        row = jnp.bitwise_xor(chip, n) * cut.r + d * size
        return whole[pl.ds(pl.multiple_of(row, 16), cut.r), :]

    for d in range(cut.shards):
        for n in range(half):
            if other:
                refs[-4][n, d] = rnd(part(n, d))
                continue
            got, (stay, go) = refs[0], refs[-5:-3]
            value = rnd(part(n, d) + got[n, d].astype(F32))
            if cut.nc == 1:
                leaves, m = (n >= half // 2, n % (half // 2)) if reverse else (n % 2 == 1, n // 2)
                (go if leaves else stay)[m, d] = value
            else:

                @pl.when(step < cut.nc // 2)
                def _():
                    stay[n, d] = value

                @pl.when(step >= cut.nc // 2)
                def _():
                    go[n, d] = value


def wide_grad(cut, place, left, right, other, got, reverse, after):
    lefts = left if isinstance(left, list) else [left]
    tokens, half, count = right.shape[0], cut.nr // 2, cut.nc // 2
    block = (half, cut.shards, cut.r, cut.c)
    here = lambda i, s: (i, 0, 0, 0)
    if other:
        specs, sizes = [pl.BlockSpec(block, here)], [cut.replicas // 2]
    elif cut.nc == 1:
        specs, sizes = [pl.BlockSpec((half // 2,) + block[1:], here)] * 2, [cut.replicas // 4] * 2
    else:
        specs = [
            pl.BlockSpec(block, lambda i, s: (jnp.minimum(i, count - 1), 0, 0, 0)),
            pl.BlockSpec(block, lambda i, s: (jnp.maximum(i - count, 0), 0, 0, 0)),
        ]
        sizes = [cut.replicas // 4] * 2
    return pl.pallas_call(
        functools.partial(wide_kernel, cut, other, reverse, len(lefts)),
        grid_spec=pltpu.PrefetchScalarGridSpec(
            num_scalar_prefetch=1,
            grid=(cut.nc,),
            in_specs=[
                pl.BlockSpec(
                    (tokens, cut.c), lambda i, s: (0, jnp.bitwise_xor(lax.div(s[0], 2 * half), i))
                ),
            ]
            + [pl.BlockSpec(a.shape, lambda i, s: (0, 0)) for a in lefts]
            + [pl.BlockSpec(block, here)] * len(got)
            + [ANY_SPEC] * len(after),
            out_specs=specs + [pl.BlockSpec((8, 128), lambda i, s: (0, 0))],
            scratch_shapes=[
                pltpu.VMEM((tokens, cut.shards * cut.rows // 2), BF),
                pltpu.VMEM((cut.shards * cut.rows // 2, tokens), BF),
                pltpu.VMEM((cut.shards * cut.rows // 2, cut.c), F32),
            ],
        ),
        out_shape=[jax.ShapeDtypeStruct((n, cut.shards, cut.r, cut.c), BF) for n in sizes] + [MARK],
        compiler_params=pltpu.CompilerParams(vmem_limit_bytes=56 * MIB),
        cost_estimate=cost(6),
    )(place, right, *lefts, *got, *after)


def half_spots(cut, me):
    half = cut.nr // 2
    for m in range(cut.replicas // 2):
        chip = jnp.bitwise_xor(lax.div(me, 2), m)
        row = pl.multiple_of(lax.rem(chip, half) * cut.r, 8 if cut.r % 16 else 16)
        column = pl.multiple_of(lax.div(chip, half) * cut.c, 128)
        yield m, (pl.ds(row, cut.r), pl.ds(column, cut.c))


def send_grad_kernel(cut, place, left, right, *refs):
    send, mark, whole = refs[-3:]
    mark[...] = jnp.zeros_like(mark)
    whole[...] = lax.dot_general(
        left[...], right[...], (((0,), (0,)), ((), ())), preferred_element_type=F32
    )
    for m, spot in half_spots(cut, place[0]):
        send[m, 0] = rnd(whole[spot])


def keep_grad_kernel(cut, reverse, place, left, right, got, *refs):
    stay, go, mark, whole = refs[-4:]
    mark[...] = jnp.zeros_like(mark)
    whole[...] = lax.dot_general(
        left[...], right[...], (((0,), (0,)), ((), ())), preferred_element_type=F32
    )
    count = cut.replicas // 4
    for m, spot in half_spots(cut, place[0]):
        leaves, n = (m >= count, m % count) if reverse else (m % 2 == 1, m // 2)
        (go if leaves else stay)[n, 0] = rnd(whole[spot] + got[m, 0].astype(F32))


def half_grad(kernel, cut, place, left, right, other, slots, results, after):
    tokens, shards = left.shape[0], cut.shards
    pick = lambda d, s: (
        0,
        lax.rem(s[1] + shards - d, shards) * 2 + lax.rem(s[0] + other, 2),
    )
    piece = lambda count: pl.BlockSpec((count, 1, cut.r, cut.c), lambda d, s: (0, d, 0, 0))
    return pl.pallas_call(
        kernel,
        grid_spec=pltpu.PrefetchScalarGridSpec(
            num_scalar_prefetch=1,
            grid=(shards,),
            in_specs=[
                pl.BlockSpec((tokens, cut.rows // 2), pick),
                pl.BlockSpec(right.shape, lambda d, s: (0, 0)),
            ]
            + [piece(a.shape[0]) for a in slots]
            + [ANY_SPEC] * len(after),
            out_specs=[piece(n) for n in results] + [pl.BlockSpec((8, 128), lambda d, s: (0, 0))],
            scratch_shapes=[pltpu.VMEM((cut.rows // 2, cut.columns), F32)],
        ),
        out_shape=[jax.ShapeDtypeStruct((n, shards, cut.r, cut.c), BF) for n in results] + [MARK],
        compiler_params=pltpu.CompilerParams(vmem_limit_bytes=56 * MIB),
        cost_estimate=cost(7.5),
    )(place, left, right, *slots, *after)


def send_grad(cut, place, left, right, after=()):
    if cut.rows <= 256:
        return wide_grad(cut, place, left, right, 1, (), False, after)
    kernel = functools.partial(send_grad_kernel, cut)
    return half_grad(kernel, cut, place, left, right, 1, (), (cut.replicas // 2,), after)


def keep_grad(cut, place, left, right, got, reverse, after=()):
    if cut.rows <= 256:
        return wide_grad(cut, place, left, right, 0, (got,), reverse, after)
    kernel = functools.partial(keep_grad_kernel, cut, reverse)
    return half_grad(kernel, cut, place, left, right, 0, (got,), (cut.replicas // 4,) * 2, after)


def qkv_grad_kernel(slim, replicas, shards, place, dq, dk, dv, small, *refs):
    keep, send, mark, whole = refs[-4:]
    blocks = refs[:shards]
    rows = blocks[0].shape[0]
    mark[...] = jnp.zeros_like(mark)
    local = dq.shape[1]
    for n, right in enumerate((dq, dk, dv)):
        total = jnp.zeros((whole.shape[0], local), F32)
        for d in range(shards):
            at = pl.ds(pl.multiple_of(lax.rem(place[1] + shards - d, shards) * rows, 16), rows)
            total += lax.dot_general(
                blocks[d][...], right[at, :], (((0,), (0,)), ((), ())), preferred_element_type=F32
            )
        whole[:, n * local : (n + 1) * local] = total
    first = lax.broadcasted_iota(jnp.int32, (16, 3 * local), 0) == 0
    for j in range(replicas):
        piece = jnp.bitwise_xor(place[0], j)
        out = (keep, send)[j & 1]
        out[j >> 1, 0, 0:slim] = rnd(whole[pl.ds(pl.multiple_of(piece * slim, 8), slim), :])
        out[j >> 1, 0, slim:] = rnd(jnp.where(first, small[0, pl.ds(piece, 1), :], 0.0))


def qkv_grad(place, hiddens, dq, dk, dv, small, slim, shards, after):
    replicas, (tokens, local) = small.shape[1], dq.shape
    rows, width = slim * replicas, 3 * local
    here = pl.BlockSpec((tokens, local), lambda f, s: (0, 0))
    piece = pl.BlockSpec((replicas // 2, 1, slim + 16, width), lambda f, s: (0, f, 0, 0))
    return pl.pallas_call(
        functools.partial(qkv_grad_kernel, slim, replicas, shards),
        grid_spec=pltpu.PrefetchScalarGridSpec(
            num_scalar_prefetch=1,
            grid=(shards,),
            in_specs=[here, here, here]
            + [pl.BlockSpec((1, replicas, width), lambda f, s: (f, 0, 0))]
            + [pl.BlockSpec((tokens // shards, rows), lambda f, s: (0, f))] * shards
            + [ANY_SPEC] * len(after),
            out_specs=[piece] * 2 + [pl.BlockSpec((8, 128), lambda f, s: (0, 0))],
            scratch_shapes=[pltpu.VMEM((rows, width), F32)],
        ),
        out_shape=[jax.ShapeDtypeStruct((replicas // 2, shards, slim + 16, width), BF)] * 2 + [MARK],
        compiler_params=pltpu.CompilerParams(vmem_limit_bytes=48 * MIB),
        cost_estimate=cost(6.5),
    )(place, dq, dk, dv, small, *hiddens, *after)


def widen_kernel(cuts, qkv_rows, place, own_a, other_a, own_b, other_b, w_out, w_up, w_down, w_qkv, small):
    cut_out, cut_up, cut_down = cuts
    width = own_a.shape[2]
    for j in range(cut_out.replicas):
        piece = jnp.bitwise_xor(place[0], j)
        left, right, m = (own_a, own_b, j >> 1) if j % 2 == 0 else (other_a, other_b, j >> 1)
        row = cut_out.r
        w_out[cut_out.spot(piece)] = left[m, 0:row].astype(F32)
        w_up[cut_up.spot(piece)] = left[m, row : row + cut_up.r].astype(F32)
        row += cut_up.r
        spot = pl.ds(pl.multiple_of(piece * 8, 8), 8)
        small[spot, :] = left[m, row : row + 8].astype(F32)
        above, below = row + 16, cut_down.r
        w_down[cut_down.spot(piece)] = right[m, 0:below].astype(F32)
        spot = pl.ds(pl.multiple_of(piece * qkv_rows, 8), qkv_rows)
        shards, local = cut_out.shards, width // cut_out.shards
        for k in range(3):
            for d in range(shards):
                column = k * width + lax.rem(place[1] + shards - d, shards) * local
                source, row = (right, below + (k - 1) * qkv_rows) if k else (left, above)
                part = source[m, row : row + qkv_rows, d * local : (d + 1) * local].astype(F32)
                w_qkv[spot, pl.ds(pl.multiple_of(column, 128), local)] = part


def widen(cuts, qkv_rows, place, own_a, other_a, own_b, other_b):
    width = own_a.shape[2]
    shapes = [(cut.rows, cut.columns) for cut in cuts]
    shapes += [(qkv_rows * cuts[0].replicas, 3 * width), (8 * cuts[0].replicas, width)]
    return pl.pallas_call(
        functools.partial(widen_kernel, cuts, qkv_rows),
        in_specs=[SMEM_SPEC] + [VMEM_SPEC] * 4,
        out_specs=[VMEM_SPEC] * 5,
        out_shape=[jax.ShapeDtypeStruct(shape, F32) for shape in shapes],
        compiler_params=pltpu.CompilerParams(vmem_limit_bytes=48 * MIB),
        cost_estimate=cost(7),
    )(place, own_a, other_a, own_b, other_b)


def hidden_grad_kernel(place, block, dq, dk, dv, weight, *refs):
    out, sums = refs[-2:]
    local = dq.shape[1]
    grad = dot_last(dq[...], weight[:, 0:local])
    grad += dot_last(dk[...], weight[:, local : 2 * local])
    grad += dot_last(dv[...], weight[:, 2 * local :])
    out[...] = rnd(grad)
    normal, _ = moments(block[...].astype(F32))
    sums[0:1, :] = jnp.sum(grad * normal, 0, keepdims=True)
    sums[1:2, :] = jnp.sum(grad, 0, keepdims=True)
    sums[2:8, :] = jnp.zeros((6, sums.shape[1]), F32)


def hidden_grad(place, block, dq, dk, dv, weight, distance, shards, after=()):
    rows, width = block.shape
    local = dq.shape[1]
    at = lambda i, s: (lax.rem(s[1] + shards - distance, shards), 0)
    here = lambda i, s: (0, 0)
    return pl.pallas_call(
        hidden_grad_kernel,
        grid_spec=pltpu.PrefetchScalarGridSpec(
            num_scalar_prefetch=1,
            grid=(1,),
            in_specs=[pl.BlockSpec((rows, width), here)]
            + [pl.BlockSpec((rows, local), at)] * 3
            + [pl.BlockSpec(weight.shape, here)]
            + [ANY_SPEC] * len(after),
            out_specs=[pl.BlockSpec((rows, width), here), pl.BlockSpec((8, width), here)],
        ),
        out_shape=[jax.ShapeDtypeStruct((rows, width), BF), jax.ShapeDtypeStruct((8, width), F32)],
        compiler_params=pltpu.CompilerParams(vmem_limit_bytes=40 * MIB),
        cost_estimate=cost(3),
    )(place, block, dq, dk, dv, weight, *after)


def last_kernel(tokens, travel, own, dx2, gain, out, mark):
    mark[...] = jnp.zeros_like(mark)
    normal, scale = moments(tokens[...].astype(F32))
    grad = travel[...].astype(F32) + own[...].astype(F32)
    out[...] = rnd(dx2[...] + norm_grad(grad, gain[...], normal, scale))


def last(tokens, travel, own, dx2, gain):
    return pl.pallas_call(
        last_kernel,
        in_specs=[VMEM_SPEC] * 5,
        out_specs=[VMEM_SPEC] * 2,
        out_shape=[jax.ShapeDtypeStruct(tokens.shape, BF), MARK],
        compiler_params=pltpu.CompilerParams(vmem_limit_bytes=40 * MIB),
        cost_estimate=cost(2.5),
    )(tokens, travel, own, dx2, gain)


def swap(value, bit, replicas):
    return lax.ppermute(value, "dp", [(i, i ^ bit) for i in range(replicas)])


def around(value, shards):
    blocks = {0: value}
    for d in range(1, shards // 2 + 1):
        blocks[d] = turn(blocks[d - 1], shards)
        if shards - d not in blocks:
            blocks[shards - d] = turn(blocks[(shards - d + 1) % shards], shards, shards - 1)
    return blocks


def turn(value, shards, step=1):
    return lax.ppermute(value, "fsdp", [(i, (i + step) % shards) for i in range(shards)])


def chip_bits(replicas, reverse):
    bits = [1 << n for n in range(1, replicas.bit_length() - 1)]
    return bits[::-1] if reverse else bits


def share_chips(piece, replicas, reverse=False, pause=lambda part: part):
    parts = {0: piece}
    for n, bit in enumerate(chip_bits(replicas, reverse)):
        more = {m | bit: swap(part, bit, replicas) for m, part in parts.items()}
        parts |= {m: part if n else pause(part) for m, part in more.items()}
    return [parts[2 * m] for m in range(replicas // 2)]


def share_both(upper, lower, replicas):
    first, second = {0: upper}, {0: lower}
    for one, two in zip(chip_bits(replicas, False), chip_bits(replicas, True)):
        more = {m | one: swap(part, one, replicas) for m, part in first.items()}
        even = {m | two: swap(part, two, replicas) for m, part in second.items()}
        if len(first) == 1 and replicas > 4:
            more = {m: gate(part, *even.values()) for m, part in more.items()}
            even = {m: gate(part, *more.values()) for m, part in even.items()}
        first |= more
        second |= even
    slots = [2 * m for m in range(replicas // 2)]
    return jnp.stack([first[m] for m in slots]), jnp.stack([second[m] for m in slots])


def share(piece, replicas, reverse=False, pause=lambda part: part):
    slots = []
    for part in share_chips(piece, replicas, reverse, pause):
        slots += [part, swap(part, 1, replicas)]
    return slots


def idle_kernel(*refs):
    pass


def gate(value, *after):
    return pl.pallas_call(
        idle_kernel,
        in_specs=[ANY_SPEC] * (1 + len(after)),
        out_specs=ANY_SPEC,
        out_shape=jax.ShapeDtypeStruct(value.shape, value.dtype),
        input_output_aliases={0: 0},
        cost_estimate=cost(0),
    )(value, *after)


def add_low(left, right):
    return rnd(left.astype(F32) + right.astype(F32))


def fold_kernel(left_stay, right_stay, left_go, right_go, *refs):
    stay, go, mark = refs[-3:]
    stay[...] = add_low(left_stay[...], right_stay[...])
    go[...] = add_low(left_go[...], right_go[...])
    mark[...] = jnp.zeros_like(mark)


def fold(left, right, reverse, after=()):
    n, shards, r, c = left.shape
    deep = shards if r * c < 2**16 else 1
    stay = lambda i, d: (i if reverse else 2 * i, d, 0, 0)
    go = lambda i, d: (i + n // 2 if reverse else 2 * i + 1, d, 0, 0)
    block = (1, deep, r, c)
    return pl.pallas_call(
        fold_kernel,
        grid=(n // 2, shards // deep),
        in_specs=[pl.BlockSpec(block, stay)] * 2 + [pl.BlockSpec(block, go)] * 2 + [ANY_SPEC] * len(after),
        out_specs=[pl.BlockSpec(block, lambda i, d: (i, d, 0, 0))] * 2
        + [pl.BlockSpec((8, 128), lambda i, d: (0, 0))],
        out_shape=[jax.ShapeDtypeStruct((n // 2, shards, r, c), BF)] * 2 + [MARK],
        compiler_params=pltpu.CompilerParams(vmem_limit_bytes=32 * MIB),
        cost_estimate=cost(3),
    )(left, right, left, right, *after)


def close_kernel(counts, *refs):
    total, first, mark = refs[-3:]
    mark[...] = jnp.zeros_like(mark)
    row = n = 0
    for count in counts:
        value = refs[n][0, 0].astype(F32)
        for m in range(1, count):
            value += refs[n + m][0, 0].astype(F32)
        value = rnd(value)
        n += count
        rows = pl.ds(row, value.shape[0])
        total[0, rows, :] = value

        @pl.when(pl.program_id(0) == min(1, pl.num_programs(0) - 1))
        def _():
            first[rows, :] = value

        row += value.shape[0]


def close(groups, after=()):
    _, shards, _, c = groups[0][0].shape
    height = sum(group[0].shape[2] for group in groups)
    flat = [a for group in groups for a in group]
    return pl.pallas_call(
        functools.partial(close_kernel, [len(group) for group in groups]),
        grid=(shards,),
        in_specs=[pl.BlockSpec((1, 1) + a.shape[2:], lambda d: (0, d, 0, 0)) for a in flat]
        + [ANY_SPEC] * len(after),
        out_specs=[
            pl.BlockSpec((1, height, c), lambda d: (d, 0, 0)),
            pl.BlockSpec((height, c), lambda d: (0, 0)),
            pl.BlockSpec((8, 128), lambda d: (0, 0)),
        ],
        out_shape=[
            jax.ShapeDtypeStruct((shards, height, c), BF),
            jax.ShapeDtypeStruct((height, c), BF),
            MARK,
        ],
        compiler_params=pltpu.CompilerParams(vmem_limit_bytes=32 * MIB),
        cost_estimate=cost(3),
    )(*flat, *after)


def close_parts_kernel(count, *refs):
    value = refs[0][...].astype(F32)
    for m in range(1, count):
        value += refs[m][...].astype(F32)
    refs[-2][...] = rnd(value)
    refs[-1][...] = jnp.zeros_like(refs[-1])


def close_parts(parts, after=()):
    return pl.pallas_call(
        functools.partial(close_parts_kernel, len(parts)),
        in_specs=[VMEM_SPEC] * len(parts) + [ANY_SPEC] * len(after),
        out_specs=[VMEM_SPEC] * 2,
        out_shape=[jax.ShapeDtypeStruct(parts[0].shape, BF), MARK],
        compiler_params=pltpu.CompilerParams(vmem_limit_bytes=32 * MIB),
        cost_estimate=cost(1),
    )(*parts, *after)


def join_kernel(travel, part, *refs):
    total, mark = refs[-2:]
    total[...] = add_low(travel[...], part[0])
    mark[...] = jnp.zeros_like(mark)


def join(travel, parts, d, after=()):
    r, c = travel.shape
    return pl.pallas_call(
        join_kernel,
        grid=(1,),
        in_specs=[
            pl.BlockSpec((r, c), lambda i: (0, 0)),
            pl.BlockSpec((1, r, c), lambda i: (d, 0, 0)),
        ]
        + [ANY_SPEC] * len(after),
        out_specs=[pl.BlockSpec((r, c), lambda i: (0, 0)), pl.BlockSpec((8, 128), lambda i: (0, 0))],
        out_shape=[jax.ShapeDtypeStruct((r, c), BF), MARK],
        compiler_params=pltpu.CompilerParams(vmem_limit_bytes=32 * MIB),
        cost_estimate=cost(1),
    )(travel, parts, *after)


def direct(parts, replicas):
    return [part if m == 0 else swap(part, 2 * m, replicas) for m, part in enumerate(parts)]


def spread_kernel(left, right, *refs):
    count = left.shape[0]
    for m in range(count):
        refs[-1 - count + m][...] = add_low(left[m], right[m])
    refs[-1][...] = jnp.zeros_like(refs[-1])


def spread(left, right, after=()):
    n, shards, r, c = left.shape
    block = pl.BlockSpec((n, 1, r, c), lambda d: (0, d, 0, 0))
    part = pl.BlockSpec((1, r, c), lambda d: (d, 0, 0))
    return pl.pallas_call(
        spread_kernel,
        grid=(shards,),
        in_specs=[block] * 2 + [ANY_SPEC] * len(after),
        out_specs=[part] * n + [pl.BlockSpec((8, 128), lambda d: (0, 0))],
        out_shape=[jax.ShapeDtypeStruct((shards, r, c), BF)] * n + [MARK],
        compiler_params=pltpu.CompilerParams(vmem_limit_bytes=32 * MIB),
        cost_estimate=cost(3),
    )(left, right, *after)


def gather_sum_kernel(count, place, *refs):
    value = refs[0][...].astype(F32)
    for m in range(1, count):
        value += refs[m][...].astype(F32)
    refs[-2][...] = rnd(value)
    refs[-1][...] = jnp.zeros_like(refs[-1])


def gather_sum(place, parts, after=()):
    shards, r, c = parts[0].shape
    return pl.pallas_call(
        functools.partial(gather_sum_kernel, len(parts)),
        grid_spec=pltpu.PrefetchScalarGridSpec(
            num_scalar_prefetch=1,
            grid=(shards,),
            in_specs=[pl.BlockSpec((1, r, c), lambda d, s: (lax.rem(s[1] + d, shards), 0, 0))] * len(parts)
            + [ANY_SPEC] * len(after),
            out_specs=[
                pl.BlockSpec((1, r, c), lambda d, s: (d, 0, 0)),
                pl.BlockSpec((8, 128), lambda d, s: (0, 0)),
            ],
        ),
        out_shape=[jax.ShapeDtypeStruct((shards, r, c), BF), MARK],
        compiler_params=pltpu.CompilerParams(vmem_limit_bytes=32 * MIB),
        cost_estimate=cost(2),
    )(place, *parts, *after)


class Scatter:
    def __init__(self, keep, send, replicas, reverse, first=0):
        self.replicas, self.reverse = replicas, reverse
        self.bits = chip_bits(replicas, reverse)
        bit = self.bits.pop(0) if first else 1
        self.pair = (keep, swap(send, bit, replicas))

    def step(self, mark):
        keep, go, mark = fold(*self.pair, self.reverse, (mark,))
        self.pair = (keep, swap(go, self.bits.pop(0), self.replicas))
        return mark


def flip_by(value, axis, me, replicas):
    shape = value.shape
    bits = replicas.bit_length() - 1
    value = value.reshape(shape[:axis] + (2,) * bits + shape[axis + 1 :])
    for n in range(bits):
        where = axis + bits - 1 - n
        value = jnp.where((me >> n) & 1 == 1, jnp.flip(value, where), value)
    return value.reshape(shape)


def window_low(lengths, group_len):
    prompt = group_len // 2
    order = jnp.arange(lengths.shape[0], dtype=jnp.int32)
    ends = jnp.sum(jnp.where(order[:, None] <= order[None, :], lengths[:, None], 0), 0)
    pos = jnp.arange(prompt, dtype=jnp.int32)
    starts = jnp.max(jnp.where(ends[:, None] <= pos[None, :], ends[:, None], 0), 0)
    return jnp.concatenate([jnp.zeros((prompt,), jnp.int32), prompt + starts])[None]


def body(
    tokens,
    cotangent,
    cont_lengths,
    ln1_gain,
    ln1_bias,
    w_qkv,
    q_bias,
    v_bias,
    w_out,
    out_bias,
    ln2_gain,
    ln2_bias,
    w_up,
    up_bias,
    w_down,
    down_bias,
):
    rows, width = tokens.shape
    shards, replicas = lax.axis_size("fsdp"), lax.axis_size("dp")
    z, me = lax.axis_index("fsdp"), lax.axis_index("dp")
    place = jnp.stack([me, z]).astype(jnp.int32)
    group_len = rows * shards
    head_dim = width // H
    local = width // shards
    hidden = w_up.shape[2]
    w_qkv, w_out, w_up, w_down = w_qkv[0], w_out[0], w_up[0], w_down[0]
    cut_out = Cut(w_out.shape[0], width, 1, replicas, shards)
    cut_up = Cut(w_up.shape[0], hidden, hidden // width, replicas, shards)
    cut_down = Cut(w_down.shape[0], width, 1, replicas, shards)
    cuts = (cut_out, cut_up, cut_down)

    vectors = (ln1_gain, ln1_bias, q_bias, v_bias, out_bias, ln2_gain, ln2_bias, down_bias, up_bias)
    packed = jnp.concatenate(vectors, 1)
    slim = w_qkv.shape[0] // replicas
    mine = lax.dynamic_slice_in_dim(w_qkv, me * slim, slim, 0)
    mine = mine.reshape(slim, 3, shards, local).transpose(2, 0, 1, 3).reshape(shards, slim, 3 * local)
    turned = [packed] + [turn(packed, shards, step) for step in range(shards - 1, 0, -1)]
    turned = jnp.concatenate(turned + turned, 0)
    packed_all = lax.dynamic_slice_in_dim(turned, lax.rem(shards - z, shards), shards)
    full = []
    offset = 0
    for vector in vectors:
        size = vector.shape[1]
        full.append(packed_all[:, offset : offset + size].reshape(1, shards * size).astype(F32))
        offset += size
    gain_one, bias_one, _, _, bias_out, gain_two, bias_two, bias_down, bias_up = full
    middle_vectors = jnp.concatenate([bias_out, gain_two, bias_two, bias_down] * 2, 0)
    start_at = z * local
    bias_q = lax.dynamic_slice_in_dim(full[2], start_at, local, 1)
    bias_v = lax.dynamic_slice_in_dim(full[3], start_at, local, 1)
    bias_qkv = jnp.concatenate([bias_q, jnp.zeros_like(bias_q), bias_v], 1)

    piece = jnp.concatenate(
        [cut.of(shard, me) for cut, shard in ((cut_out, w_out), (cut_up, w_up), (cut_down, w_down))], 0
    )
    piece = gate(piece, mine)
    slots = around(piece, shards)
    near = (slots[1], slots[shards - 1])
    blocks = around(gate(tokens, packed, *near), shards)
    mine = gate(lax.all_to_all(mine, "fsdp", 0, 0, tiled=True), *near)
    weight_qkv = flip_by(jnp.stack(share(mine, replicas)), 0, me, replicas)
    weight_qkv = weight_qkv.transpose(1, 0, 2, 3).reshape(width, 3 * local)

    hiddens = [None] * shards
    combined = jnp.zeros((group_len, 3 * local), BF)
    for d in [0] + sorted(range(1, shards), key=lambda d: min(d, shards - d)):
        if d == shards // 2:
            early = mark
        hiddens[d], combined, mark = project(
            place, blocks[d], gain_one, bias_one, weight_qkv, bias_qkv, combined, d, shards
        )

    edge = cut_out.r + cut_up.r
    slots = [gate(slots[d], early) for d in range(1, shards)]
    upper = jnp.stack([slot[:edge] for slot in slots])
    lower = jnp.stack([slot[edge:] for slot in slots])

    low = window_low(cont_lengths[0], group_len)
    mixed, lse = attend(combined, low, head_dim)
    attended = [
        lax.dynamic_slice_in_dim(mixed, lax.rem(z + d, shards) * rows, rows) for d in range(shards)
    ]
    attended = [turn(block, shards, d) if d else block for d, block in enumerate(attended)]
    pause = lambda part: gate(part, lse)
    lists = share(upper, replicas, False, pause) + share(lower, replicas, True, pause)
    lists += [w_out, w_up, w_down]
    dm = cotangent
    output, hidden_two, acted, du, dx2, da, do, grad_bias_up, sums = feed(
        place, attended, tokens, dm, middle_vectors, bias_up, cuts, lists
    )

    grad_mixed = lax.all_to_all(do, "fsdp", 1, 0, tiled=True)
    terms = ((cut_down, acted, dm, False), (cut_up, hidden_two, du, True), (cut_out, attended, da, False))
    mark = grad_bias_up
    scatters = []
    if all(cut.rows % 256 == 0 for cut in cuts):
        gots = []
        for cut, left, right, _ in terms:
            send, mark = send_grad(cut, place, left, right, (mark,) if gots else ())
            gots.append(swap(send, 1, replicas))
        for (cut, left, right, reverse), got in zip(terms, gots):
            stay, go, mark = keep_grad(cut, place, left, right, got, reverse, (mark,))
            if cut is cut_out:
                halves = (stay, go)
                out = [halves[m % 2][m // 2 : m // 2 + 1] for m in range(replicas // 2)]
            else:
                scatters.append(Scatter(stay, go, replicas, reverse, True))
    else:
        turned = [attended[-d % shards] for d in range(shards)] * 2
        joined = lax.dynamic_slice_in_dim(
            jnp.concatenate(turned, 1), lax.rem(shards - z, shards) * local, width, 1
        )
        for cut, left, right, reverse in terms:
            left = joined if left is attended else left
            keep, send, mark = weight_grad(cut, place, left, right, (mark,))
            if cut is cut_out:
                *out, mark = spread(keep, swap(send, 1, replicas), (mark,))
                out = [part[None] for part in out]
            else:
                scatters.append(Scatter(keep, send, replicas, reverse))
        for scatter in scatters:
            mark = scatter.step(mark)
    down, up = scatters
    out = direct(out, replicas)

    dq, dk, dv, bias_sums = attend_grad(combined, low, mixed, lse, grad_mixed, head_dim, (mark,))
    parts = {}
    parts[1 % shards], first_sums = hidden_grad(place, blocks[1 % shards], dq, dk, dv, weight_qkv, 1, shards)
    travel = turn(parts[1 % shards], shards)
    mark = first_sums
    while down.bits:
        mark = down.step(mark)
        mark = up.step(mark)
    out, mark = close_parts(out, (mark,))
    others = list(range(2, shards))
    for d in [*others, 0]:
        parts[d], mark = hidden_grad(
            place, blocks[d], dq, dk, dv, weight_qkv, d, shards, (mark,)
        )
        first_sums += mark
        if d == 2:
            step, mark = join(travel, parts[d][None], 0, (mark,))
            travel = turn(step, shards)

    blank = jnp.zeros((width,), F32)
    grad_bias_q = lax.dynamic_update_slice(blank, bias_sums[:, 0].reshape(-1), (start_at,))
    grad_bias_v = lax.dynamic_update_slice(blank, bias_sums[:, 1].reshape(-1), (start_at,))
    small = (
        first_sums[0],
        first_sums[1],
        grad_bias_q,
        grad_bias_v,
        sums[3],
        sums[1],
        sums[2],
        sums[0],
        grad_bias_up,
    )
    small = jnp.concatenate([g.reshape(shards, -1) for g in small], 1)
    count = small.shape[1] // replicas
    small = small.reshape(shards, replicas, count)
    small = jnp.pad(small, ((0, 0), (0, 0), (0, 3 * local - count)))
    keep, send, mark = qkv_grad(place, hiddens, dq, dk, dv, small, slim, shards, (mark,))
    got = swap(send, 1, replicas)

    late = None
    if others[1:]:
        late, mark = join(travel, parts[others[1]][None], 0, (mark,))
    sums_all, first, mark = close(([out], up.pair, down.pair), (mark,))
    ring = turn(first, shards)
    *qkv, mark = spread(keep, got, (mark,))
    qkv = direct(qkv, replicas)
    come = None
    for d in range(2, shards + 1):
        total, mark = join(ring, sums_all, d % shards, (mark,))
        if d < shards:
            ring = turn(total, shards)
        if come is None:
            piece, mark = gather_sum(place, qkv, (mark,))
            come = [piece[0]] + [turn(piece[e], shards, e) for e in range(1, shards)]
    if late is not None:
        travel = turn(gate(late, mark), shards)
    for d in others[2:]:
        step, mark = join(travel, parts[d][None], 0, (mark,))
        travel = turn(step, shards)
    input_grad, last_mark = last(tokens, travel, parts[0], dx2, gain_one)
    rows_qkv = jnp.concatenate(
        [
            jnp.concatenate([block[:slim, k * local : (k + 1) * local] for block in come], 1)
            for k in range(3)
        ],
        0,
    )
    row_small = rnd(sum(block[slim, :count].astype(F32) for block in come))
    row_small = jnp.pad(row_small[None], ((0, 15), (0, width - count)))
    upper = jnp.concatenate([total[:edge], row_small, rows_qkv[:slim]], 0)
    lower = jnp.concatenate([total[edge:], rows_qkv[slim:]], 0)
    own_a, own_b = share_both(upper, lower, replicas)
    own_a, own_b = gate(own_a, last_mark), gate(own_b, last_mark)
    out_w_out, out_w_up, out_w_down, out_w_qkv, total = widen(
        cuts, slim, place, own_a, swap(own_a, 1, replicas), own_b, swap(own_b, 1, replicas)
    )
    total = total.reshape(replicas, 8, width)[:, 0, :count].reshape(1, -1)
    outs = []
    offset = 0
    for vector in vectors:
        outs.append(total[:, offset : offset + vector.shape[1]])
        offset += vector.shape[1]
    return (
        output,
        input_grad,
        outs[0],
        outs[1],
        out_w_qkv[None],
        outs[2],
        outs[3],
        out_w_out[None],
        outs[4],
        outs[5],
        outs[6],
        out_w_up[None],
        outs[8],
        out_w_down[None],
        outs[7],
    )


def solution(mesh):
    vec = P(None, "fsdp")
    mat = P(None, "fsdp", None)
    tok = P(("dp", "fsdp"), None)
    in_specs = (tok, tok, P("dp", None), vec, vec, mat, vec, vec, mat, vec, vec, vec, mat, vec, mat, vec)
    out_specs = (tok, tok, vec, vec, mat, vec, vec, mat, vec, vec, vec, mat, vec, mat, vec)
    return jax.shard_map(body, mesh=mesh, in_specs=in_specs, out_specs=out_specs, check_vma=False)
```

```python
import functools

import jax
import jax.numpy as jnp
from jax import lax
from jax.experimental import pallas as pl
from jax.experimental.pallas import tpu as pltpu
from jax.sharding import PartitionSpec as P

H = 16
EPSILON = 1e-05
NEG_LARGE = -1e30
F32 = jnp.float32
BF = jnp.bfloat16
MIB = 2**20
COST_UNIT = 6 * 10**7


def rnd(v):
    return v.astype(BF)


def cost(time):
    return pl.CostEstimate(flops=int(time * COST_UNIT), bytes_accessed=1, transcendentals=0)


def dot_last(left, right):
    return lax.dot_general(left, right, (((1,), (1,)), ((), ())), preferred_element_type=F32)


def dot_mm(left, right):
    return jnp.dot(left, right, preferred_element_type=F32)


def key_ranges(start, group_len):
    prompt = group_len // 2
    if start < prompt:
        return start, start
    return prompt, max(prompt, start - group_len // 8)


def allowed_mask(shape, key_start, query_start, low_row):
    key_pos = lax.broadcasted_iota(jnp.int32, shape, 0) + key_start
    query_pos = lax.broadcasted_iota(jnp.int32, shape, 1) + query_start
    return (key_pos <= query_pos) & (key_pos >= low_row)


def attend_kernel(group_len, head_dim, q_ref, k_ref, v_ref, low_ref, o_ref, lse_ref):
    size = min(512, group_len // 4)
    scale = jnp.asarray(head_dim**-0.5, BF)
    values_t = v_ref[...].astype(F32).T.astype(BF)
    for start in range(0, group_len, size):
        stop = start + size
        full, near = key_ranges(start, group_len)
        results = []
        for head in range(128 // head_dim):
            lanes = slice(head * head_dim, (head + 1) * head_dim)
            queries = q_ref[start:stop, lanes] * scale
            part = dot_last(k_ref[near:stop, lanes], queries)
            ok = allowed_mask(part.shape, near, start, low_ref[0:1, start:stop])
            part = jnp.where(ok, part, NEG_LARGE)
            top = jnp.max(part, 0, keepdims=True)
            if full:
                rest = dot_last(k_ref[0:full, lanes], queries)
                top = jnp.maximum(top, jnp.max(rest, 0, keepdims=True))
            part = jnp.exp(part - top)
            total = jnp.sum(part, 0, keepdims=True)
            mixed = dot_mm(values_t[lanes, near:stop], part.astype(BF))
            if full:
                rest = jnp.exp(rest - top)
                total += jnp.sum(rest, 0, keepdims=True)
                mixed += dot_mm(values_t[lanes, 0:full], rest.astype(BF))
            results.append(mixed * (1.0 / total))
            lse_ref[0, head : head + 1, start:stop] = top + jnp.log(total)
        o_ref[start:stop, :] = jnp.concatenate(results, 0).T.astype(BF)


def attend_grad_kernel(
    group_len, head_dim, q_ref, k_ref, v_ref, low_ref, o_ref, lse_ref, do_ref, *refs
):
    dq_ref, dk_ref, dv_ref, bias_ref, dk_sum, dv_sum = refs[-6:]
    bias = jnp.zeros((1, 128), F32)
    size = min(256, group_len // 8)
    scale = jnp.asarray(head_dim**-0.5, BF)
    keys_t = k_ref[...].astype(F32).T.astype(BF)
    dk_sum[...] = jnp.zeros_like(dk_sum)
    dv_sum[...] = jnp.zeros_like(dv_sum)
    for start in range(0, group_len, size):
        stop = start + size
        full, near = key_ranges(start, group_len)
        product_t = (do_ref[start:stop, :].astype(F32) * o_ref[start:stop, :].astype(F32)).T
        results = []
        for head in range(128 // head_dim):
            lanes = slice(head * head_dim, (head + 1) * head_dim)
            queries = q_ref[start:stop, lanes] * scale
            grads = do_ref[start:stop, lanes]
            delta = jnp.sum(product_t[lanes, :], 0, keepdims=True)
            lse = lse_ref[0, head : head + 1, start:stop]
            dq_t = jnp.zeros((head_dim, size), F32)
            for first, last, masked in ((near, stop, True), (0, full, False)):
                if first == last:
                    continue
                probs = jnp.exp(dot_last(k_ref[first:last, lanes], queries) - lse)
                if masked:
                    ok = allowed_mask(probs.shape, first, start, low_ref[0:1, start:stop])
                    probs = jnp.where(ok, probs, 0.0)
                grad_probs = dot_last(v_ref[first:last, lanes], grads)
                ds = (probs * (grad_probs - delta)).astype(BF)
                dv_sum[head, first:last, :] += dot_mm(probs.astype(BF), grads)
                dk_sum[head, first:last, :] += dot_mm(ds, queries)
                dq_t += dot_mm(keys_t[lanes, first:last], ds)
            results.append(dq_t * head_dim**-0.5)
        dq = jnp.concatenate(results, 0).T.astype(BF)
        dq_ref[start:stop, :] = dq
        bias += jnp.sum(dq.astype(F32), 0, keepdims=True)
    heads = range(128 // head_dim)
    dk_ref[...] = jnp.concatenate([dk_sum[head] for head in heads], 1).astype(BF)
    dv = jnp.concatenate([dv_sum[head] for head in heads], 1).astype(BF)
    dv_ref[...] = dv
    bias_ref[0, 0:1, :] = bias
    bias_ref[0, 1:2, :] = jnp.sum(dv.astype(F32), 0, keepdims=True)


def attend(combined, low, head_dim):
    group_len, width = combined.shape[0], combined.shape[1] // 3
    steps = width // 128
    heads = 128 // head_dim
    block = lambda offset: pl.BlockSpec((group_len, 128), lambda i: (0, offset + i))
    return pl.pallas_call(
        functools.partial(attend_kernel, group_len, head_dim),
        grid=(steps,),
        in_specs=[block(0), block(steps), block(2 * steps), pl.BlockSpec((1, group_len), lambda i: (0, 0))],
        out_specs=[block(0), pl.BlockSpec((1, heads, group_len), lambda i: (i, 0, 0))],
        out_shape=[
            jax.ShapeDtypeStruct((group_len, width), BF),
            jax.ShapeDtypeStruct((steps, heads, group_len), F32),
        ],
        compiler_params=pltpu.CompilerParams(vmem_limit_bytes=56 * MIB),
        cost_estimate=cost(18),
    )(combined, combined, combined, low)


def attend_grad(combined, low, mixed, lse, grad_mixed, head_dim, after=()):
    group_len, width = mixed.shape
    steps = width // 128
    heads = 128 // head_dim
    block = lambda offset: pl.BlockSpec((group_len, 128), lambda i: (0, offset + i))
    return pl.pallas_call(
        functools.partial(attend_grad_kernel, group_len, head_dim),
        grid=(steps,),
        in_specs=[
            block(0),
            block(steps),
            block(2 * steps),
            pl.BlockSpec((1, group_len), lambda i: (0, 0)),
            block(0),
            pl.BlockSpec((1, heads, group_len), lambda i: (i, 0, 0)),
            block(0),
        ]
        + [pl.BlockSpec(memory_space=pl.ANY)] * len(after),
        out_specs=[block(0)] * 3 + [pl.BlockSpec((1, 2, 128), lambda i: (i, 0, 0))],
        out_shape=[jax.ShapeDtypeStruct((group_len, width), BF)] * 3
        + [jax.ShapeDtypeStruct((steps, 2, 128), F32)],
        scratch_shapes=[pltpu.VMEM((heads, group_len, head_dim), F32)] * 2,
        compiler_params=pltpu.CompilerParams(vmem_limit_bytes=56 * MIB),
        cost_estimate=cost(28),
    )(combined, combined, combined, low, mixed, lse, grad_mixed, *after)


class Cut:
    def __init__(self, rows, columns, column_parts, replicas, shards):
        self.rows, self.columns, self.shards, self.replicas = rows, columns, shards, replicas
        self.nc, self.nr = column_parts, replicas // column_parts
        self.r, self.c = rows // self.nr, columns // self.nc

    def place(self, piece):
        half = self.nr // 2
        row = (lax.rem(piece, 2) * half + lax.rem(lax.div(piece, 2), half)) * self.r
        column = lax.div(piece, self.nr) * self.c
        return pl.multiple_of(row, 8 if self.r % 16 else 16), pl.multiple_of(column, 128)

    def spot(self, piece, base=0):
        row, column = self.place(piece)
        return pl.ds(base + row, self.r), pl.ds(column, self.c)

    def of(self, shard, piece):
        return lax.dynamic_slice(shard, self.place(piece), (self.r, self.c))

    @property
    def copies(self):
        return 1 + (self.shards - 1) * self.replicas


def fetch(cut, me, z, slots, first_row, shard, whole, sems):
    base = pl.multiple_of(z * cut.rows, 16)
    copies = [pltpu.make_async_copy(shard, whole.at[pl.ds(base, cut.rows), :], sems.at[0])]
    for d in range(1, cut.shards):
        base = pl.multiple_of(lax.rem(z + cut.shards - d, cut.shards) * cut.rows, 16)
        for j in range(cut.replicas):
            copies.append(
                pltpu.make_async_copy(
                    slots[j].at[d - 1, pl.ds(first_row, cut.r), :],
                    whole.at[cut.spot(jnp.bitwise_xor(me, j), base)],
                    sems.at[len(copies)],
                )
            )
    return copies


def loads_of(cuts, place, lists, wholes, sems):
    count = cuts[0].replicas
    both, down, shards = lists[:count], lists[count : 2 * count], lists[2 * count :]
    sources = ((both, 0), (both, cuts[0].r), (down, 0))
    return [
        fetch(cut, place[0], place[1], slots, row, shard, whole, sem)
        for cut, (slots, row), shard, whole, sem in zip(cuts, sources, shards, wholes, sems)
    ]


def start(copies):
    for copy in copies:
        copy.start()


def finish(copies):
    for copy in copies:
        copy.wait()


MARK = jax.ShapeDtypeStruct((8, 128), F32)
SMEM_SPEC = pl.BlockSpec(memory_space=pltpu.SMEM)
ANY_SPEC = pl.BlockSpec(memory_space=pl.ANY)
VMEM_SPEC = pl.BlockSpec(memory_space=pltpu.VMEM)


def moments(stream):
    mean = jnp.mean(stream, -1, keepdims=True)
    centered = stream - mean
    scale = lax.rsqrt(jnp.mean(centered * centered, -1, keepdims=True) + EPSILON)
    return centered * scale, scale


def norm_grad(grad_hidden, gain, normal, scale):
    t = grad_hidden * gain
    return scale * (
        t - jnp.mean(t, -1, keepdims=True) - normal * jnp.mean(t * normal, -1, keepdims=True)
    )


def project_kernel(place, block, gain, bias, weight, bias_qkv, c_in, h_out, c_out, mark):
    mark[...] = jnp.zeros_like(mark)
    normal, _ = moments(block[...].astype(F32))
    hidden = rnd(normal * gain[...] + bias[...])
    h_out[...] = hidden
    c_out[...] = rnd(dot_mm(hidden, weight[...]) + bias_qkv[...])


def project(place, block, gain, bias, weight, bias_qkv, c_all, distance, shards):
    rows, width = block.shape
    whole = lambda a: pl.BlockSpec(a.shape, lambda i, s: (0,) * a.ndim)
    at = lambda i, s: (lax.rem(s[1] + shards - distance, shards), 0)
    return pl.pallas_call(
        project_kernel,
        grid_spec=pltpu.PrefetchScalarGridSpec(
            num_scalar_prefetch=1,
            grid=(1,),
            in_specs=[whole(a) for a in (block, gain, bias, weight, bias_qkv)] + [ANY_SPEC],
            out_specs=[
                pl.BlockSpec((rows, width), lambda i, s: (0, 0)),
                pl.BlockSpec((rows, c_all.shape[1]), at),
                pl.BlockSpec((8, 128), lambda i, s: (0, 0)),
            ],
        ),
        out_shape=[jax.ShapeDtypeStruct(a.shape, BF) for a in (block, c_all)] + [MARK],
        input_output_aliases={6: 1},
        compiler_params=pltpu.CompilerParams(vmem_limit_bytes=40 * MIB),
        cost_estimate=cost(2.5),
    )(place, block, gain, bias, weight, bias_qkv, c_all)


GELU_A = 0.7978845608028654
GELU_B = 0.044715


def gelu_both(u):
    square = u * u
    s = 0.5 * jnp.tanh(u * (GELU_A + GELU_A * GELU_B * square)) + 0.5
    value = u * s
    return value, s + value * (1.0 - s) * (2.0 * GELU_A + 6.0 * GELU_A * GELU_B * square)


def feed_kernel(cuts, step, place, tokens, dm, vectors, bias_up, *refs):
    shards, count = cuts[0].shards, 2 * cuts[0].replicas + 3
    mixed, lists, refs = refs[:shards], refs[shards : shards + count], refs[shards + count :]
    out, hidden, acted, du, dx2, da, do, grad_up, sums, w_out, w_up, w_down, slope, *sems = refs
    loads = loads_of(cuts, place, lists, (w_out, w_up, w_down), sems)
    for copies in loads:
        start(copies)
    finish(loads[0])
    stream = tokens[...].astype(F32) + vectors[0:1, :]
    local = mixed[0].shape[1]
    for d in range(shards):
        at = pl.multiple_of(lax.rem(place[1] + shards - d, shards) * local, 16)
        stream += dot_mm(mixed[d][...], w_out[pl.ds(at, local), :])
    normal, scale = moments(stream)
    hidden[...] = rnd(normal * vectors[1:2, :] + vectors[2:3, :])
    total = vectors[3:4, :] + stream
    finish(loads[1])
    for block in range(0, w_up.shape[1], step):
        columns = slice(block, block + step)
        value, grad = gelu_both(dot_mm(hidden[...], w_up[:, columns]) + bias_up[:, columns])
        value = rnd(value)
        acted[:, columns] = value
        slope[:, columns] = rnd(grad)
        if block == 0:
            finish(loads[2])
        total += dot_mm(value, w_down[columns, :])
    out[...] = rnd(total)
    dh2 = jnp.zeros(stream.shape, F32)
    for block in range(0, w_up.shape[1], step):
        columns = slice(block, block + step)
        part = rnd(dot_last(dm[...], w_down[columns, :]) * slope[:, columns].astype(F32))
        du[:, columns] = part
        grad_up[:, columns] = jnp.sum(part.astype(F32), 0, keepdims=True)
        dh2 += dot_last(part, w_up[:, columns])
    incoming = dm[...].astype(F32)
    stream = incoming + norm_grad(dh2, vectors[1:2, :], normal, scale)
    dx2[...] = stream
    low = rnd(stream)
    da[...] = low
    do[...] = rnd(dot_last(low, w_out[...]))
    sums[0:1, :] = jnp.sum(incoming, 0, keepdims=True)
    sums[1:2, :] = jnp.sum(dh2 * normal, 0, keepdims=True)
    sums[2:3, :] = jnp.sum(dh2, 0, keepdims=True)
    sums[3:4, :] = jnp.sum(low.astype(F32), 0, keepdims=True)
    sums[4:8, :] = jnp.zeros((4, sums.shape[1]), F32)


def feed(place, mixed, tokens, dm, vectors, bias_up, cuts, lists):
    rows, width = tokens.shape
    hidden = bias_up.shape[1]
    shapes = [((rows, width), BF), ((rows, width), BF), ((rows, hidden), BF), ((rows, hidden), BF)]
    shapes += [((rows, width), F32), ((rows, width), BF), ((rows, width), BF)]
    shapes += [((1, hidden), F32), ((8, width), F32)]
    return pl.pallas_call(
        functools.partial(feed_kernel, cuts, min(1024, hidden)),
        in_specs=[SMEM_SPEC] + [VMEM_SPEC] * (4 + len(mixed)) + [ANY_SPEC] * len(lists),
        out_specs=[VMEM_SPEC] * len(shapes),
        out_shape=[jax.ShapeDtypeStruct(*shape) for shape in shapes],
        scratch_shapes=[
            pltpu.VMEM((width, width), BF),
            pltpu.VMEM((width, hidden), BF),
            pltpu.VMEM((hidden, width), BF),
            pltpu.VMEM((rows, hidden), BF),
        ]
        + [pltpu.SemaphoreType.DMA((cut.copies,)) for cut in cuts],
        compiler_params=pltpu.CompilerParams(vmem_limit_bytes=60 * MIB),
        cost_estimate=cost(40),
    )(place, tokens, dm, vectors, bias_up, *mixed, *lists)


def weight_grad_kernel(cut, place, left, right, *refs):
    keep, send, mark, whole = refs[-4:]
    mark[...] = jnp.zeros_like(mark)
    whole[...] = lax.dot_general(
        left[...], right[...], (((0,), (0,)), ((), ())), preferred_element_type=F32
    )
    for j in range(cut.replicas):
        value = whole[cut.spot(jnp.bitwise_xor(place[0], j))]
        (keep, send)[j & 1][j >> 1, 0] = rnd(value)


def weight_grad(cut, place, left, right, after=()):
    tokens, shards = left.shape[0], cut.shards
    shape = (cut.replicas // 2, shards, cut.r, cut.c)
    piece = pl.BlockSpec((cut.replicas // 2, 1, cut.r, cut.c), lambda d, s: (0, d, 0, 0))
    return pl.pallas_call(
        functools.partial(weight_grad_kernel, cut),
        grid_spec=pltpu.PrefetchScalarGridSpec(
            num_scalar_prefetch=1,
            grid=(shards,),
            in_specs=[
                pl.BlockSpec((tokens, cut.rows), lambda d, s: (0, lax.rem(s[1] + shards - d, shards))),
                pl.BlockSpec(right.shape, lambda d, s: (0, 0)),
            ]
            + [ANY_SPEC] * len(after),
            out_specs=[piece] * 2 + [pl.BlockSpec((8, 128), lambda d, s: (0, 0))],
            scratch_shapes=[pltpu.VMEM((cut.rows, cut.columns), F32)],
        ),
        out_shape=[jax.ShapeDtypeStruct(shape, BF)] * 2 + [MARK],
        compiler_params=pltpu.CompilerParams(vmem_limit_bytes=56 * MIB),
        cost_estimate=cost(10),
    )(place, left, right, *after)


def gather_rows(cut, place, other, lefts, rows):
    size = cut.rows // 2
    half = lax.rem(place[0] + other, 2) * size
    for d in range(cut.shards):
        if len(lefts) > 1:
            part = lefts[d][:, pl.ds(pl.multiple_of(half, 128), size)]
        else:
            column = lax.rem(place[1] + cut.shards - d, cut.shards) * cut.rows + half
            part = lefts[0][:, pl.ds(pl.multiple_of(column, 128), size)]
        rows[:, d * size : (d + 1) * size] = part


def wide_kernel(cut, other, reverse, count, place, right, *refs):
    lefts, refs = refs[:count], refs[count:]
    rows, turned, whole = refs[-3:]
    refs = refs[:-1]
    refs[-3][...] = jnp.zeros_like(refs[-3])
    step = pl.program_id(0)

    @pl.when(step == 0)
    def _():
        gather_rows(cut, place, other, lefts, rows)
        turned[...] = rows[...].astype(F32).T.astype(BF)

    whole[...] = dot_mm(turned[...], right[...])
    half, size = cut.nr // 2, cut.rows // 2
    chip = lax.rem(lax.div(place[0], 2), half)

    def part(n, d):
        row = jnp.bitwise_xor(chip, n) * cut.r + d * size
        return whole[pl.ds(pl.multiple_of(row, 16), cut.r), :]

    for d in range(cut.shards):
        for n in range(half):
            if other:
                refs[-4][n, d] = rnd(part(n, d))
                continue
            got, (stay, go) = refs[0], refs[-5:-3]
            value = rnd(part(n, d) + got[n, d].astype(F32))
            if cut.nc == 1:
                leaves, m = (n >= half // 2, n % (half // 2)) if reverse else (n % 2 == 1, n // 2)
                (go if leaves else stay)[m, d] = value
            else:

                @pl.when(step < cut.nc // 2)
                def _():
                    stay[n, d] = value

                @pl.when(step >= cut.nc // 2)
                def _():
                    go[n, d] = value


def wide_grad(cut, place, left, right, other, got, reverse, after):
    lefts = left if isinstance(left, list) else [left]
    tokens, half, count = right.shape[0], cut.nr // 2, cut.nc // 2
    block = (half, cut.shards, cut.r, cut.c)
    here = lambda i, s: (i, 0, 0, 0)
    if other:
        specs, sizes = [pl.BlockSpec(block, here)], [cut.replicas // 2]
    elif cut.nc == 1:
        specs, sizes = [pl.BlockSpec((half // 2,) + block[1:], here)] * 2, [cut.replicas // 4] * 2
    else:
        specs = [
            pl.BlockSpec(block, lambda i, s: (jnp.minimum(i, count - 1), 0, 0, 0)),
            pl.BlockSpec(block, lambda i, s: (jnp.maximum(i - count, 0), 0, 0, 0)),
        ]
        sizes = [cut.replicas // 4] * 2
    return pl.pallas_call(
        functools.partial(wide_kernel, cut, other, reverse, len(lefts)),
        grid_spec=pltpu.PrefetchScalarGridSpec(
            num_scalar_prefetch=1,
            grid=(cut.nc,),
            in_specs=[
                pl.BlockSpec(
                    (tokens, cut.c), lambda i, s: (0, jnp.bitwise_xor(lax.div(s[0], 2 * half), i))
                ),
            ]
            + [pl.BlockSpec(a.shape, lambda i, s: (0, 0)) for a in lefts]
            + [pl.BlockSpec(block, here)] * len(got)
            + [ANY_SPEC] * len(after),
            out_specs=specs + [pl.BlockSpec((8, 128), lambda i, s: (0, 0))],
            scratch_shapes=[
                pltpu.VMEM((tokens, cut.shards * cut.rows // 2), BF),
                pltpu.VMEM((cut.shards * cut.rows // 2, tokens), BF),
                pltpu.VMEM((cut.shards * cut.rows // 2, cut.c), F32),
            ],
        ),
        out_shape=[jax.ShapeDtypeStruct((n, cut.shards, cut.r, cut.c), BF) for n in sizes] + [MARK],
        compiler_params=pltpu.CompilerParams(vmem_limit_bytes=56 * MIB),
        cost_estimate=cost(6),
    )(place, right, *lefts, *got, *after)


def half_spots(cut, me):
    half = cut.nr // 2
    for m in range(cut.replicas // 2):
        chip = jnp.bitwise_xor(lax.div(me, 2), m)
        row = pl.multiple_of(lax.rem(chip, half) * cut.r, 8 if cut.r % 16 else 16)
        column = pl.multiple_of(lax.div(chip, half) * cut.c, 128)
        yield m, (pl.ds(row, cut.r), pl.ds(column, cut.c))


def send_grad_kernel(cut, place, left, right, *refs):
    send, mark, whole = refs[-3:]
    mark[...] = jnp.zeros_like(mark)
    whole[...] = lax.dot_general(
        left[...], right[...], (((0,), (0,)), ((), ())), preferred_element_type=F32
    )
    for m, spot in half_spots(cut, place[0]):
        send[m, 0] = rnd(whole[spot])


def keep_grad_kernel(cut, reverse, place, left, right, got, *refs):
    stay, go, mark, whole = refs[-4:]
    mark[...] = jnp.zeros_like(mark)
    whole[...] = lax.dot_general(
        left[...], right[...], (((0,), (0,)), ((), ())), preferred_element_type=F32
    )
    count = cut.replicas // 4
    for m, spot in half_spots(cut, place[0]):
        leaves, n = (m >= count, m % count) if reverse else (m % 2 == 1, m // 2)
        (go if leaves else stay)[n, 0] = rnd(whole[spot] + got[m, 0].astype(F32))


def half_grad(kernel, cut, place, left, right, other, slots, results, after):
    tokens, shards = left.shape[0], cut.shards
    pick = lambda d, s: (
        0,
        lax.rem(s[1] + shards - d, shards) * 2 + lax.rem(s[0] + other, 2),
    )
    piece = lambda count: pl.BlockSpec((count, 1, cut.r, cut.c), lambda d, s: (0, d, 0, 0))
    return pl.pallas_call(
        kernel,
        grid_spec=pltpu.PrefetchScalarGridSpec(
            num_scalar_prefetch=1,
            grid=(shards,),
            in_specs=[
                pl.BlockSpec((tokens, cut.rows // 2), pick),
                pl.BlockSpec(right.shape, lambda d, s: (0, 0)),
            ]
            + [piece(a.shape[0]) for a in slots]
            + [ANY_SPEC] * len(after),
            out_specs=[piece(n) for n in results] + [pl.BlockSpec((8, 128), lambda d, s: (0, 0))],
            scratch_shapes=[pltpu.VMEM((cut.rows // 2, cut.columns), F32)],
        ),
        out_shape=[jax.ShapeDtypeStruct((n, shards, cut.r, cut.c), BF) for n in results] + [MARK],
        compiler_params=pltpu.CompilerParams(vmem_limit_bytes=56 * MIB),
        cost_estimate=cost(7.5),
    )(place, left, right, *slots, *after)


def send_grad(cut, place, left, right, after=()):
    if cut.rows <= 256:
        return wide_grad(cut, place, left, right, 1, (), False, after)
    kernel = functools.partial(send_grad_kernel, cut)
    return half_grad(kernel, cut, place, left, right, 1, (), (cut.replicas // 2,), after)


def keep_grad(cut, place, left, right, got, reverse, after=()):
    if cut.rows <= 256:
        return wide_grad(cut, place, left, right, 0, (got,), reverse, after)
    kernel = functools.partial(keep_grad_kernel, cut, reverse)
    return half_grad(kernel, cut, place, left, right, 0, (got,), (cut.replicas // 4,) * 2, after)


def qkv_grad_kernel(slim, replicas, shards, place, dq, dk, dv, small, *refs):
    keep, send, mark, whole = refs[-4:]
    blocks = refs[:shards]
    rows = blocks[0].shape[0]
    mark[...] = jnp.zeros_like(mark)
    local = dq.shape[1]
    for n, right in enumerate((dq, dk, dv)):
        total = jnp.zeros((whole.shape[0], local), F32)
        for d in range(shards):
            at = pl.ds(pl.multiple_of(lax.rem(place[1] + shards - d, shards) * rows, 16), rows)
            total += lax.dot_general(
                blocks[d][...], right[at, :], (((0,), (0,)), ((), ())), preferred_element_type=F32
            )
        whole[:, n * local : (n + 1) * local] = total
    first = lax.broadcasted_iota(jnp.int32, (16, 3 * local), 0) == 0
    for j in range(replicas):
        piece = jnp.bitwise_xor(place[0], j)
        out = (keep, send)[j & 1]
        out[j >> 1, 0, 0:slim] = rnd(whole[pl.ds(pl.multiple_of(piece * slim, 8), slim), :])
        out[j >> 1, 0, slim:] = rnd(jnp.where(first, small[0, pl.ds(piece, 1), :], 0.0))


def qkv_grad(place, hiddens, dq, dk, dv, small, slim, shards, after):
    replicas, (tokens, local) = small.shape[1], dq.shape
    rows, width = slim * replicas, 3 * local
    here = pl.BlockSpec((tokens, local), lambda f, s: (0, 0))
    piece = pl.BlockSpec((replicas // 2, 1, slim + 16, width), lambda f, s: (0, f, 0, 0))
    return pl.pallas_call(
        functools.partial(qkv_grad_kernel, slim, replicas, shards),
        grid_spec=pltpu.PrefetchScalarGridSpec(
            num_scalar_prefetch=1,
            grid=(shards,),
            in_specs=[here, here, here]
            + [pl.BlockSpec((1, replicas, width), lambda f, s: (f, 0, 0))]
            + [pl.BlockSpec((tokens // shards, rows), lambda f, s: (0, f))] * shards
            + [ANY_SPEC] * len(after),
            out_specs=[piece] * 2 + [pl.BlockSpec((8, 128), lambda f, s: (0, 0))],
            scratch_shapes=[pltpu.VMEM((rows, width), F32)],
        ),
        out_shape=[jax.ShapeDtypeStruct((replicas // 2, shards, slim + 16, width), BF)] * 2 + [MARK],
        compiler_params=pltpu.CompilerParams(vmem_limit_bytes=48 * MIB),
        cost_estimate=cost(6.5),
    )(place, dq, dk, dv, small, *hiddens, *after)


def widen_kernel(cuts, qkv_rows, place, own_a, other_a, own_b, other_b, w_out, w_up, w_down, w_qkv, small):
    cut_out, cut_up, cut_down = cuts
    width = own_a.shape[2]
    for j in range(cut_out.replicas):
        piece = jnp.bitwise_xor(place[0], j)
        left, right, m = (own_a, own_b, j >> 1) if j % 2 == 0 else (other_a, other_b, j >> 1)
        row = cut_out.r
        w_out[cut_out.spot(piece)] = left[m, 0:row].astype(F32)
        w_up[cut_up.spot(piece)] = left[m, row : row + cut_up.r].astype(F32)
        row += cut_up.r
        spot = pl.ds(pl.multiple_of(piece * 8, 8), 8)
        small[spot, :] = left[m, row : row + 8].astype(F32)
        above, below = row + 16, cut_down.r
        w_down[cut_down.spot(piece)] = right[m, 0:below].astype(F32)
        spot = pl.ds(pl.multiple_of(piece * qkv_rows, 8), qkv_rows)
        shards, local = cut_out.shards, width // cut_out.shards
        for k in range(3):
            for d in range(shards):
                column = k * width + lax.rem(place[1] + shards - d, shards) * local
                source, row = (right, below + (k - 1) * qkv_rows) if k else (left, above)
                part = source[m, row : row + qkv_rows, d * local : (d + 1) * local].astype(F32)
                w_qkv[spot, pl.ds(pl.multiple_of(column, 128), local)] = part


def widen(cuts, qkv_rows, place, own_a, other_a, own_b, other_b):
    width = own_a.shape[2]
    shapes = [(cut.rows, cut.columns) for cut in cuts]
    shapes += [(qkv_rows * cuts[0].replicas, 3 * width), (8 * cuts[0].replicas, width)]
    return pl.pallas_call(
        functools.partial(widen_kernel, cuts, qkv_rows),
        in_specs=[SMEM_SPEC] + [VMEM_SPEC] * 4,
        out_specs=[VMEM_SPEC] * 5,
        out_shape=[jax.ShapeDtypeStruct(shape, F32) for shape in shapes],
        compiler_params=pltpu.CompilerParams(vmem_limit_bytes=48 * MIB),
        cost_estimate=cost(7),
    )(place, own_a, other_a, own_b, other_b)


def hidden_grad_kernel(place, block, dq, dk, dv, weight, *refs):
    out, sums = refs[-2:]
    local = dq.shape[1]
    grad = dot_last(dq[...], weight[:, 0:local])
    grad += dot_last(dk[...], weight[:, local : 2 * local])
    grad += dot_last(dv[...], weight[:, 2 * local :])
    out[...] = rnd(grad)
    normal, _ = moments(block[...].astype(F32))
    sums[0:1, :] = jnp.sum(grad * normal, 0, keepdims=True)
    sums[1:2, :] = jnp.sum(grad, 0, keepdims=True)
    sums[2:8, :] = jnp.zeros((6, sums.shape[1]), F32)


def hidden_grad(place, block, dq, dk, dv, weight, distance, shards, after=()):
    rows, width = block.shape
    local = dq.shape[1]
    at = lambda i, s: (lax.rem(s[1] + shards - distance, shards), 0)
    here = lambda i, s: (0, 0)
    return pl.pallas_call(
        hidden_grad_kernel,
        grid_spec=pltpu.PrefetchScalarGridSpec(
            num_scalar_prefetch=1,
            grid=(1,),
            in_specs=[pl.BlockSpec((rows, width), here)]
            + [pl.BlockSpec((rows, local), at)] * 3
            + [pl.BlockSpec(weight.shape, here)]
            + [ANY_SPEC] * len(after),
            out_specs=[pl.BlockSpec((rows, width), here), pl.BlockSpec((8, width), here)],
        ),
        out_shape=[jax.ShapeDtypeStruct((rows, width), BF), jax.ShapeDtypeStruct((8, width), F32)],
        compiler_params=pltpu.CompilerParams(vmem_limit_bytes=40 * MIB),
        cost_estimate=cost(3),
    )(place, block, dq, dk, dv, weight, *after)


def last_kernel(tokens, travel, own, dx2, gain, out, mark):
    mark[...] = jnp.zeros_like(mark)
    normal, scale = moments(tokens[...].astype(F32))
    grad = travel[...].astype(F32) + own[...].astype(F32)
    out[...] = rnd(dx2[...] + norm_grad(grad, gain[...], normal, scale))


def last(tokens, travel, own, dx2, gain):
    return pl.pallas_call(
        last_kernel,
        in_specs=[VMEM_SPEC] * 5,
        out_specs=[VMEM_SPEC] * 2,
        out_shape=[jax.ShapeDtypeStruct(tokens.shape, BF), MARK],
        compiler_params=pltpu.CompilerParams(vmem_limit_bytes=40 * MIB),
        cost_estimate=cost(2.5),
    )(tokens, travel, own, dx2, gain)


def swap(value, bit, replicas):
    return lax.ppermute(value, "dp", [(i, i ^ bit) for i in range(replicas)])


def around(value, shards):
    blocks = {0: value}
    for d in range(1, shards // 2 + 1):
        blocks[d] = turn(blocks[d - 1], shards)
        if shards - d not in blocks:
            blocks[shards - d] = turn(blocks[(shards - d + 1) % shards], shards, shards - 1)
    return blocks


def turn(value, shards, step=1):
    return lax.ppermute(value, "fsdp", [(i, (i + step) % shards) for i in range(shards)])


def chip_bits(replicas, reverse):
    bits = [1 << n for n in range(1, replicas.bit_length() - 1)]
    return bits[::-1] if reverse else bits


def share_chips(piece, replicas, reverse=False, pause=lambda part: part):
    parts = {0: piece}
    for n, bit in enumerate(chip_bits(replicas, reverse)):
        more = {m | bit: swap(part, bit, replicas) for m, part in parts.items()}
        parts |= {m: part if n else pause(part) for m, part in more.items()}
    return [parts[2 * m] for m in range(replicas // 2)]


def share_both(upper, lower, replicas):
    first, second = {0: upper}, {0: lower}
    for one, two in zip(chip_bits(replicas, False), chip_bits(replicas, True)):
        more = {m | one: swap(part, one, replicas) for m, part in first.items()}
        even = {m | two: swap(part, two, replicas) for m, part in second.items()}
        if len(first) == 1 and replicas > 4:
            more = {m: gate(part, *even.values()) for m, part in more.items()}
            even = {m: gate(part, *more.values()) for m, part in even.items()}
        first |= more
        second |= even
    slots = [2 * m for m in range(replicas // 2)]
    return jnp.stack([first[m] for m in slots]), jnp.stack([second[m] for m in slots])


def share(piece, replicas, reverse=False, pause=lambda part: part):
    slots = []
    for part in share_chips(piece, replicas, reverse, pause):
        slots += [part, swap(part, 1, replicas)]
    return slots


def idle_kernel(*refs):
    pass


def gate(value, *after):
    return pl.pallas_call(
        idle_kernel,
        in_specs=[ANY_SPEC] * (1 + len(after)),
        out_specs=ANY_SPEC,
        out_shape=jax.ShapeDtypeStruct(value.shape, value.dtype),
        input_output_aliases={0: 0},
        cost_estimate=cost(0),
    )(value, *after)


def add_low(left, right):
    return rnd(left.astype(F32) + right.astype(F32))


def fold_kernel(left_stay, right_stay, left_go, right_go, *refs):
    stay, go, mark = refs[-3:]
    stay[...] = add_low(left_stay[...], right_stay[...])
    go[...] = add_low(left_go[...], right_go[...])
    mark[...] = jnp.zeros_like(mark)


def fold(left, right, reverse, after=()):
    n, shards, r, c = left.shape
    deep = shards if r * c < 2**16 else 1
    stay = lambda i, d: (i if reverse else 2 * i, d, 0, 0)
    go = lambda i, d: (i + n // 2 if reverse else 2 * i + 1, d, 0, 0)
    block = (1, deep, r, c)
    return pl.pallas_call(
        fold_kernel,
        grid=(n // 2, shards // deep),
        in_specs=[pl.BlockSpec(block, stay)] * 2 + [pl.BlockSpec(block, go)] * 2 + [ANY_SPEC] * len(after),
        out_specs=[pl.BlockSpec(block, lambda i, d: (i, d, 0, 0))] * 2
        + [pl.BlockSpec((8, 128), lambda i, d: (0, 0))],
        out_shape=[jax.ShapeDtypeStruct((n // 2, shards, r, c), BF)] * 2 + [MARK],
        compiler_params=pltpu.CompilerParams(vmem_limit_bytes=32 * MIB),
        cost_estimate=cost(3),
    )(left, right, left, right, *after)


def close_kernel(counts, *refs):
    total, first, mark = refs[-3:]
    mark[...] = jnp.zeros_like(mark)
    row = n = 0
    for count in counts:
        value = refs[n][0, 0].astype(F32)
        for m in range(1, count):
            value += refs[n + m][0, 0].astype(F32)
        value = rnd(value)
        n += count
        rows = pl.ds(row, value.shape[0])
        total[0, rows, :] = value

        @pl.when(pl.program_id(0) == min(1, pl.num_programs(0) - 1))
        def _():
            first[rows, :] = value

        row += value.shape[0]


def close(groups, after=()):
    _, shards, _, c = groups[0][0].shape
    height = sum(group[0].shape[2] for group in groups)
    flat = [a for group in groups for a in group]
    return pl.pallas_call(
        functools.partial(close_kernel, [len(group) for group in groups]),
        grid=(shards,),
        in_specs=[pl.BlockSpec((1, 1) + a.shape[2:], lambda d: (0, d, 0, 0)) for a in flat]
        + [ANY_SPEC] * len(after),
        out_specs=[
            pl.BlockSpec((1, height, c), lambda d: (d, 0, 0)),
            pl.BlockSpec((height, c), lambda d: (0, 0)),
            pl.BlockSpec((8, 128), lambda d: (0, 0)),
        ],
        out_shape=[
            jax.ShapeDtypeStruct((shards, height, c), BF),
            jax.ShapeDtypeStruct((height, c), BF),
            MARK,
        ],
        compiler_params=pltpu.CompilerParams(vmem_limit_bytes=32 * MIB),
        cost_estimate=cost(3),
    )(*flat, *after)


def close_parts_kernel(count, *refs):
    value = refs[0][...].astype(F32)
    for m in range(1, count):
        value += refs[m][...].astype(F32)
    refs[-2][...] = rnd(value)
    refs[-1][...] = jnp.zeros_like(refs[-1])


def close_parts(parts, after=()):
    return pl.pallas_call(
        functools.partial(close_parts_kernel, len(parts)),
        in_specs=[VMEM_SPEC] * len(parts) + [ANY_SPEC] * len(after),
        out_specs=[VMEM_SPEC] * 2,
        out_shape=[jax.ShapeDtypeStruct(parts[0].shape, BF), MARK],
        compiler_params=pltpu.CompilerParams(vmem_limit_bytes=32 * MIB),
        cost_estimate=cost(1),
    )(*parts, *after)


def join_kernel(travel, part, *refs):
    total, mark = refs[-2:]
    total[...] = add_low(travel[...], part[0])
    mark[...] = jnp.zeros_like(mark)


def join(travel, parts, d, after=()):
    r, c = travel.shape
    return pl.pallas_call(
        join_kernel,
        grid=(1,),
        in_specs=[
            pl.BlockSpec((r, c), lambda i: (0, 0)),
            pl.BlockSpec((1, r, c), lambda i: (d, 0, 0)),
        ]
        + [ANY_SPEC] * len(after),
        out_specs=[pl.BlockSpec((r, c), lambda i: (0, 0)), pl.BlockSpec((8, 128), lambda i: (0, 0))],
        out_shape=[jax.ShapeDtypeStruct((r, c), BF), MARK],
        compiler_params=pltpu.CompilerParams(vmem_limit_bytes=32 * MIB),
        cost_estimate=cost(1),
    )(travel, parts, *after)


def direct(parts, replicas):
    return [part if m == 0 else swap(part, 2 * m, replicas) for m, part in enumerate(parts)]


def spread_kernel(left, right, *refs):
    count = left.shape[0]
    for m in range(count):
        refs[-1 - count + m][...] = add_low(left[m], right[m])
    refs[-1][...] = jnp.zeros_like(refs[-1])


def spread(left, right, after=()):
    n, shards, r, c = left.shape
    block = pl.BlockSpec((n, 1, r, c), lambda d: (0, d, 0, 0))
    part = pl.BlockSpec((1, r, c), lambda d: (d, 0, 0))
    return pl.pallas_call(
        spread_kernel,
        grid=(shards,),
        in_specs=[block] * 2 + [ANY_SPEC] * len(after),
        out_specs=[part] * n + [pl.BlockSpec((8, 128), lambda d: (0, 0))],
        out_shape=[jax.ShapeDtypeStruct((shards, r, c), BF)] * n + [MARK],
        compiler_params=pltpu.CompilerParams(vmem_limit_bytes=32 * MIB),
        cost_estimate=cost(3),
    )(left, right, *after)


def gather_sum_kernel(count, place, *refs):
    value = refs[0][...].astype(F32)
    for m in range(1, count):
        value += refs[m][...].astype(F32)
    refs[-2][...] = rnd(value)
    refs[-1][...] = jnp.zeros_like(refs[-1])


def gather_sum(place, parts, after=()):
    shards, r, c = parts[0].shape
    return pl.pallas_call(
        functools.partial(gather_sum_kernel, len(parts)),
        grid_spec=pltpu.PrefetchScalarGridSpec(
            num_scalar_prefetch=1,
            grid=(shards,),
            in_specs=[pl.BlockSpec((1, r, c), lambda d, s: (lax.rem(s[1] + d, shards), 0, 0))] * len(parts)
            + [ANY_SPEC] * len(after),
            out_specs=[
                pl.BlockSpec((1, r, c), lambda d, s: (d, 0, 0)),
                pl.BlockSpec((8, 128), lambda d, s: (0, 0)),
            ],
        ),
        out_shape=[jax.ShapeDtypeStruct((shards, r, c), BF), MARK],
        compiler_params=pltpu.CompilerParams(vmem_limit_bytes=32 * MIB),
        cost_estimate=cost(2),
    )(place, *parts, *after)


class Scatter:
    def __init__(self, keep, send, replicas, reverse, first=0):
        self.replicas, self.reverse = replicas, reverse
        self.bits = chip_bits(replicas, reverse)
        bit = self.bits.pop(0) if first else 1
        self.pair = (keep, swap(send, bit, replicas))

    def step(self, mark):
        keep, go, mark = fold(*self.pair, self.reverse, (mark,))
        self.pair = (keep, swap(go, self.bits.pop(0), self.replicas))
        return mark


def flip_by(value, axis, me, replicas):
    shape = value.shape
    bits = replicas.bit_length() - 1
    value = value.reshape(shape[:axis] + (2,) * bits + shape[axis + 1 :])
    for n in range(bits):
        where = axis + bits - 1 - n
        value = jnp.where((me >> n) & 1 == 1, jnp.flip(value, where), value)
    return value.reshape(shape)


def window_low(lengths, group_len):
    prompt = group_len // 2
    order = jnp.arange(lengths.shape[0], dtype=jnp.int32)
    ends = jnp.sum(jnp.where(order[:, None] <= order[None, :], lengths[:, None], 0), 0)
    pos = jnp.arange(prompt, dtype=jnp.int32)
    starts = jnp.max(jnp.where(ends[:, None] <= pos[None, :], ends[:, None], 0), 0)
    return jnp.concatenate([jnp.zeros((prompt,), jnp.int32), prompt + starts])[None]


def body(
    tokens,
    cotangent,
    cont_lengths,
    ln1_gain,
    ln1_bias,
    w_qkv,
    q_bias,
    v_bias,
    w_out,
    out_bias,
    ln2_gain,
    ln2_bias,
    w_up,
    up_bias,
    w_down,
    down_bias,
):
    rows, width = tokens.shape
    shards, replicas = lax.axis_size("fsdp"), lax.axis_size("dp")
    z, me = lax.axis_index("fsdp"), lax.axis_index("dp")
    place = jnp.stack([me, z]).astype(jnp.int32)
    group_len = rows * shards
    head_dim = width // H
    local = width // shards
    hidden = w_up.shape[2]
    w_qkv, w_out, w_up, w_down = w_qkv[0], w_out[0], w_up[0], w_down[0]
    cut_out = Cut(w_out.shape[0], width, 1, replicas, shards)
    cut_up = Cut(w_up.shape[0], hidden, hidden // width, replicas, shards)
    cut_down = Cut(w_down.shape[0], width, 1, replicas, shards)
    cuts = (cut_out, cut_up, cut_down)

    vectors = (ln1_gain, ln1_bias, q_bias, v_bias, out_bias, ln2_gain, ln2_bias, down_bias, up_bias)
    packed = jnp.concatenate(vectors, 1)
    slim = w_qkv.shape[0] // replicas
    mine = lax.dynamic_slice_in_dim(w_qkv, me * slim, slim, 0)
    mine = mine.reshape(slim, 3, shards, local).transpose(2, 0, 1, 3).reshape(shards, slim, 3 * local)
    turned = [packed] + [turn(packed, shards, step) for step in range(shards - 1, 0, -1)]
    turned = jnp.concatenate(turned + turned, 0)
    packed_all = lax.dynamic_slice_in_dim(turned, lax.rem(shards - z, shards), shards)
    full = []
    offset = 0
    for vector in vectors:
        size = vector.shape[1]
        full.append(packed_all[:, offset : offset + size].reshape(1, shards * size).astype(F32))
        offset += size
    gain_one, bias_one, _, _, bias_out, gain_two, bias_two, bias_down, bias_up = full
    middle_vectors = jnp.concatenate([bias_out, gain_two, bias_two, bias_down] * 2, 0)
    start_at = z * local
    bias_q = lax.dynamic_slice_in_dim(full[2], start_at, local, 1)
    bias_v = lax.dynamic_slice_in_dim(full[3], start_at, local, 1)
    bias_qkv = jnp.concatenate([bias_q, jnp.zeros_like(bias_q), bias_v], 1)

    piece = jnp.concatenate(
        [cut.of(shard, me) for cut, shard in ((cut_out, w_out), (cut_up, w_up), (cut_down, w_down))], 0
    )
    piece = gate(piece, mine)
    slots = around(piece, shards)
    near = (slots[1], slots[shards - 1])
    blocks = around(gate(tokens, packed, *near), shards)
    mine = gate(lax.all_to_all(mine, "fsdp", 0, 0, tiled=True), *near)
    weight_qkv = flip_by(jnp.stack(share(mine, replicas)), 0, me, replicas)
    weight_qkv = weight_qkv.transpose(1, 0, 2, 3).reshape(width, 3 * local)

    hiddens = [None] * shards
    combined = jnp.zeros((group_len, 3 * local), BF)
    for d in [0] + sorted(range(1, shards), key=lambda d: min(d, shards - d)):
        if d == shards // 2:
            early = mark
        hiddens[d], combined, mark = project(
            place, blocks[d], gain_one, bias_one, weight_qkv, bias_qkv, combined, d, shards
        )

    edge = cut_out.r + cut_up.r
    slots = [gate(slots[d], early) for d in range(1, shards)]
    upper = jnp.stack([slot[:edge] for slot in slots])
    lower = jnp.stack([slot[edge:] for slot in slots])

    low = window_low(cont_lengths[0], group_len)
    mixed, lse = attend(combined, low, head_dim)
    attended = [
        lax.dynamic_slice_in_dim(mixed, lax.rem(z + d, shards) * rows, rows) for d in range(shards)
    ]
    attended = [turn(block, shards, d) if d else block for d, block in enumerate(attended)]
    pause = lambda part: gate(part, lse)
    lists = share(upper, replicas, False, pause) + share(lower, replicas, True, pause)
    lists += [w_out, w_up, w_down]
    dm = cotangent
    output, hidden_two, acted, du, dx2, da, do, grad_bias_up, sums = feed(
        place, attended, tokens, dm, middle_vectors, bias_up, cuts, lists
    )

    grad_mixed = lax.all_to_all(do, "fsdp", 1, 0, tiled=True)
    terms = ((cut_down, acted, dm, False), (cut_up, hidden_two, du, True), (cut_out, attended, da, False))
    mark = grad_bias_up
    scatters = []
    if all(cut.rows % 256 == 0 for cut in cuts):
        gots = []
        for cut, left, right, _ in terms:
            send, mark = send_grad(cut, place, left, right, (mark,) if gots else ())
            gots.append(swap(send, 1, replicas))
        for (cut, left, right, reverse), got in zip(terms, gots):
            stay, go, mark = keep_grad(cut, place, left, right, got, reverse, (mark,))
            if cut is cut_out:
                halves = (stay, go)
                out = [halves[m % 2][m // 2 : m // 2 + 1] for m in range(replicas // 2)]
            else:
                scatters.append(Scatter(stay, go, replicas, reverse, True))
    else:
        turned = [attended[-d % shards] for d in range(shards)] * 2
        joined = lax.dynamic_slice_in_dim(
            jnp.concatenate(turned, 1), lax.rem(shards - z, shards) * local, width, 1
        )
        for cut, left, right, reverse in terms:
            left = joined if left is attended else left
            keep, send, mark = weight_grad(cut, place, left, right, (mark,))
            if cut is cut_out:
                *out, mark = spread(keep, swap(send, 1, replicas), (mark,))
                out = [part[None] for part in out]
            else:
                scatters.append(Scatter(keep, send, replicas, reverse))
        for scatter in scatters:
            mark = scatter.step(mark)
    down, up = scatters
    out = direct(out, replicas)

    dq, dk, dv, bias_sums = attend_grad(combined, low, mixed, lse, grad_mixed, head_dim, (mark,))
    parts = {}
    parts[1 % shards], first_sums = hidden_grad(place, blocks[1 % shards], dq, dk, dv, weight_qkv, 1, shards)
    travel = turn(parts[1 % shards], shards)
    mark = first_sums
    while down.bits:
        mark = down.step(mark)
        mark = up.step(mark)
    out, mark = close_parts(out, (mark,))
    others = list(range(2, shards))
    for d in [*others, 0]:
        parts[d], mark = hidden_grad(
            place, blocks[d], dq, dk, dv, weight_qkv, d, shards, (mark,)
        )
        first_sums += mark
        if d == 2:
            step, mark = join(travel, parts[d][None], 0, (mark,))
            travel = turn(step, shards)

    blank = jnp.zeros((width,), F32)
    grad_bias_q = lax.dynamic_update_slice(blank, bias_sums[:, 0].reshape(-1), (start_at,))
    grad_bias_v = lax.dynamic_update_slice(blank, bias_sums[:, 1].reshape(-1), (start_at,))
    small = (
        first_sums[0],
        first_sums[1],
        grad_bias_q,
        grad_bias_v,
        sums[3],
        sums[1],
        sums[2],
        sums[0],
        grad_bias_up,
    )
    small = jnp.concatenate([g.reshape(shards, -1) for g in small], 1)
    count = small.shape[1] // replicas
    small = small.reshape(shards, replicas, count)
    small = jnp.pad(small, ((0, 0), (0, 0), (0, 3 * local - count)))
    keep, send, mark = qkv_grad(place, hiddens, dq, dk, dv, small, slim, shards, (mark,))
    got = swap(send, 1, replicas)

    late = None
    if others[1:]:
        late, mark = join(travel, parts[others[1]][None], 0, (mark,))
    sums_all, first, mark = close(([out], up.pair, down.pair), (mark,))
    ring = turn(first, shards)
    *qkv, mark = spread(keep, got, (mark,))
    qkv = direct(qkv, replicas)
    come = None
    for d in range(2, shards + 1):
        total, mark = join(ring, sums_all, d % shards, (mark,))
        if d < shards:
            ring = turn(total, shards)
        if come is None:
            piece, mark = gather_sum(place, qkv, (mark,))
            come = [piece[0]] + [turn(piece[e], shards, e) for e in range(1, shards)]
    if late is not None:
        travel = turn(gate(late, mark), shards)
    for d in others[2:]:
        step, mark = join(travel, parts[d][None], 0, (mark,))
        travel = turn(step, shards)
    input_grad, last_mark = last(tokens, travel, parts[0], dx2, gain_one)
    rows_qkv = jnp.concatenate(
        [
            jnp.concatenate([block[:slim, k * local : (k + 1) * local] for block in come], 1)
            for k in range(3)
        ],
        0,
    )
    row_small = rnd(sum(block[slim, :count].astype(F32) for block in come))
    row_small = jnp.pad(row_small[None], ((0, 15), (0, width - count)))
    upper = jnp.concatenate([total[:edge], row_small, rows_qkv[:slim]], 0)
    lower = jnp.concatenate([total[edge:], rows_qkv[slim:]], 0)
    own_a, own_b = share_both(upper, lower, replicas)
    own_a, own_b = gate(own_a, last_mark), gate(own_b, last_mark)
    out_w_out, out_w_up, out_w_down, out_w_qkv, total = widen(
        cuts, slim, place, own_a, swap(own_a, 1, replicas), own_b, swap(own_b, 1, replicas)
    )
    total = total.reshape(replicas, 8, width)[:, 0, :count].reshape(1, -1)
    outs = []
    offset = 0
    for vector in vectors:
        outs.append(total[:, offset : offset + vector.shape[1]])
        offset += vector.shape[1]
    return (
        output,
        input_grad,
        outs[0],
        outs[1],
        out_w_qkv[None],
        outs[2],
        outs[3],
        out_w_out[None],
        outs[4],
        outs[5],
        outs[6],
        out_w_up[None],
        outs[8],
        out_w_down[None],
        outs[7],
    )


def solution(mesh):
    vec = P(None, "fsdp")
    mat = P(None, "fsdp", None)
    tok = P(("dp", "fsdp"), None)
    in_specs = (tok, tok, P("dp", None), vec, vec, mat, vec, vec, mat, vec, vec, vec, mat, vec, mat, vec)
    out_specs = (tok, tok, vec, vec, mat, vec, vec, mat, vec, vec, vec, mat, vec, mat, vec)
    return jax.shard_map(body, mesh=mesh, in_specs=in_specs, out_specs=out_specs, check_vma=False)
```
